128 devices in a mesh: aux: 8 (over x, core), orb: 16 (over y, z).
Axes of the slice: x: 4, y: 4, z: 4, core: 2. Of those that a mesh axis runs over, the one named last changes fastest.
Arguments:
- three_center: bfloat16 [1280, 16, 3, 4096], P(('aux', 'orb')), may hold values from -1.25 to 1.25
- atom_size: int32 [16], replicated, may hold values from 32 to 64
- tensor_pattern: int32 [80, 16, 3], P('aux', 'orb'), may hold values 0 or 1
- green_occ: bfloat16 [16, 3, 4096], P('orb'), may hold values from -0.5 to 0.5
- green_virt: bfloat16 [16, 3, 4096], P('orb'), may hold values from -0.5 to 0.5
- green_pattern: int32 [16, 3], P('orb'), may hold values 0 or 1
Outputs:
- chi: float32 [1280, 1280], P(('aux', 'orb'))
The draws below stay inside these ranges and needn't reach their ends.
Inputs may be any that keep to these rules, and one draw needn't show every extreme that they name: `atom_size`: functions in use per block.
All inputs are finite; a program needn't handle non-finite values. No bound on the sum of `tensor_pattern` or of `green_pattern` on one device may be relied on, other than what follows from the above.
Results may differ from the reference program's by a relative error of at most 0.0041.
Values may be sent and summed in bfloat16 or wider, within the bound.
No kernel may reach another device: no remote copies, remote signals or barrier semaphores. Data moves between devices by JAX's collectives and lax.ppermute only.
A program may use at most 128 MiB of HBM per device.

```python
import jax
import jax.numpy as jnp
from jax import lax

BS = 64
R = 1
W = 3
ABS = 16
AUX_DEV = 160
NAUX = 1280
NOB = 16
NAB = 80
N_AUX = 8


def set_ends(drawn, key, low, largest):
    dims = drawn.shape
    spot = [jax.random.randint(jax.random.fold_in(key, axis), (), 0, dims[axis]) for axis in range(len(dims))]
    drawn = drawn.at[tuple(spot)].set(low)
    longest = dims.index(max(dims))
    spot[longest] = (spot[longest] + 1) % dims[longest]
    return drawn.at[tuple(spot)].set(largest)


def strengthened(entries, key, source, target, shards_of, factor):
    owner, partner = [(jnp.arange(entries.shape[position]) // (entries.shape[position] // shards_of)).reshape([-1 if axis == position else 1 for axis in range(entries.ndim)]) for position in (source, target)]
    chosen = jax.random.permutation(key, shards_of)[partner]
    strong = (owner == chosen) | (owner == (partner + shards_of // 2) % shards_of)
    return jnp.where(strong, factor * entries, entries)


def block_levels(key, shape, split, least, largest):
    level, own = 1.0, jax.random.fold_in(key, 6)
    for axis_at, parts in split:
        steps = jnp.exp(jax.random.uniform(jax.random.fold_in(own, axis_at), (parts,), jnp.float32, least / len(split), largest / len(split)))
        level = level * jnp.repeat(steps, shape[axis_at] // parts).reshape([-1 if axis == axis_at else 1 for axis in range(len(shape))])
    return level


def gaussian(key, extent, width, most, pieces=(), kind=jnp.bfloat16):
    values = jax.random.normal(key, extent, jnp.float32) * width
    if len(pieces) > 0:
        values = block_levels(key, extent, pieces, -0.22, 0.18) * values
    return jnp.clip(values, min=-most, max=most).astype(kind)


def bell_draw_with(stream_key, shape, spread, limit, split, heavy, kind=jnp.bfloat16):
    drawn = spread * jax.random.normal(stream_key, shape, jnp.float32)
    if split:
        drawn = drawn * block_levels(stream_key, shape, split, -0.22, 0.18)
    return jnp.clip(strengthened(drawn, jax.random.fold_in(stream_key, 3), *heavy), -limit, limit).astype(kind)


def setup_inputs(seed: int = 0) -> dict:
    splits = jax.random.split(jax.random.key(seed), 7)
    three_center = bell_draw_with(splits[0], (NAUX, NOB, W, BS * BS), ((NOB * BS * BS) ** -0.25), 1.25, ((0, 128),), (1, 0, 16, 2.0))
    atom_size = set_ends(jax.random.randint(splits[1], (NOB,), BS // 2, BS + 1), jax.random.fold_in(splits[1], 1), BS // 2, BS).astype(jnp.int32)
    tensor_pattern = set_ends((jax.random.randint(splits[2], (NAB, NOB, W), 0, 4) < 3).astype(jnp.int32), jax.random.fold_in(splits[2], 1), 0, 1)
    green_occ = gaussian(splits[3], (NOB, W, BS * BS), (2 * BS) ** -0.5, 0.5, ((0, 16),))
    green_virt = gaussian(splits[4], (NOB, W, BS * BS), (2 * BS) ** -0.5, 0.5, ((0, 16),))
    green_pattern = set_ends((jax.random.randint(splits[5], (NOB, W), 0, 4) < 3).astype(jnp.int32), jax.random.fold_in(splits[5], 1), 0, 1)
    return dict(three_center=three_center, atom_size=atom_size, tensor_pattern=tensor_pattern, green_occ=green_occ, green_virt=green_virt, green_pattern=green_pattern)


def block_masks(atom_size, first_block, local_blocks):
    total_blocks = atom_size.shape[0]
    owned = first_block + jnp.arange(local_blocks, dtype=jnp.int32)
    offsets = jnp.arange(W, dtype=jnp.int32)
    partner = owned[:, None] + offsets[None, :] - R
    inside = (partner >= 0) & (partner < total_blocks)
    catalog = jnp.arange(total_blocks, dtype=jnp.int32)
    size_partner = jnp.sum(jnp.where(partner[:, :, None] == catalog, atom_size, 0), axis=2)
    size_owned = jnp.sum(jnp.where(owned[:, None] == catalog, atom_size, 0), axis=1)
    funcs = jnp.arange(BS, dtype=jnp.int32)
    rows_ok = (funcs[None, None, :] < size_partner[:, :, None]) & inside[:, :, None]
    cols_ok = funcs[None, :] < size_owned[:, None]
    pair_ok = rows_ok[:, :, :, None] & cols_ok[:, None, None, :]
    return inside, pair_ok.reshape(local_blocks, W, BS * BS)


def first_products(padded_occ, tensor):
    rows = tensor.shape[0]
    local_blocks = tensor.shape[1]
    results = []
    for target in range(W):
        total = jnp.zeros((rows, local_blocks, BS, BS), jnp.float32)
        for source in range(W):
            if abs(target - source) <= R:
                green = padded_occ[source:source + local_blocks, target - source + R].reshape(local_blocks, BS, BS)
                block = tensor[:, :, source].reshape(rows, local_blocks, BS, BS)
                total = total + jnp.einsum("nlm,pnmv->pnlv", green.astype(jnp.float32), block.astype(jnp.float32))
        results.append(total.reshape(rows, local_blocks, BS * BS))
    return jnp.stack(results, axis=2).astype(jnp.bfloat16)


def second_products(padded_tensor, virt):
    rows = padded_tensor.shape[0]
    local_blocks = virt.shape[0]
    results = []
    for target in range(W):
        total = jnp.zeros((rows, local_blocks, BS, BS), jnp.float32)
        for source in range(W):
            if abs(target - source) <= R:
                block = padded_tensor[:, source:source + local_blocks, target - source + R].reshape(rows, local_blocks, BS, BS)
                green = virt[:, source].reshape(local_blocks, BS, BS)
                total = total + jnp.einsum("pnls,nsv->pnlv", block.astype(jnp.float32), green.astype(jnp.float32))
        results.append(total.reshape(rows, local_blocks, BS * BS))
    return jnp.stack(results, axis=2).astype(jnp.bfloat16)


def reference(three_center, atom_size, tensor_pattern, green_occ, green_virt, green_pattern):
    inside, pair_ok = block_masks(atom_size, jnp.int32(0), NOB)
    pattern_rows = jnp.repeat(tensor_pattern, ABS, axis=0)
    keep = (pattern_rows[..., None] > 0) & pair_ok[None]
    tensor = jnp.where(keep, three_center, jnp.zeros((), three_center.dtype))
    diagonal = jnp.arange(W, dtype=jnp.int32) == R
    green_keep = ((green_pattern > 0) | diagonal[None, :]) & inside
    green_mask = green_keep[..., None] & pair_ok
    occ = jnp.where(green_mask, green_occ, jnp.zeros((), green_occ.dtype))
    virt = jnp.where(green_mask, green_virt, jnp.zeros((), green_virt.dtype))
    padded_occ = jnp.pad(occ, ((R, R), (0, 0), (0, 0)))
    groups = tensor.reshape(N_AUX, AUX_DEV, NOB, W, BS * BS)

    def second_group(group):
        return second_products(jnp.pad(group, ((0, 0), (R, R), (0, 0), (0, 0))), virt)

    second = lax.map(second_group, groups).reshape(NAUX, NOB * W * BS * BS)

    def chi_group(group):
        first = first_products(padded_occ, group).reshape(AUX_DEV, NOB * W * BS * BS)
        return lax.dot_general(first, second, (((1,), (1,)), ((), ())), preferred_element_type=jnp.float32)

    return lax.map(chi_group, groups).reshape(NAUX, NAUX)
```

```python
import functools

import jax
import jax.numpy as jnp
import numpy as np
from jax import lax
from jax.experimental import pallas as pl
from jax.experimental.pallas import tpu as pltpu
from jax.sharding import PartitionSpec as P

BS = 64
R = 1
W = 3
ABS = 16
NOB = 16
NPD = 10
NG = 10
BF = jnp.bfloat16
F32 = jnp.float32
VLIM = 56 * 1024 * 1024

STEPS = [(k // 2, k % 2) for k in range(8)]


def pairs_of(k):
    dx, dc = STEPS[k]
    return [(i, ((i // 2 + dx) % 4) * 2 + ((i % 2) ^ dc)) for i in range(8)]


def dest_of(a, k):
    dx, dc = STEPS[k]
    return lax.rem(a // 2 + dx, 4) * 2 + (lax.rem(a, 2) if dc == 0 else 1 - lax.rem(a, 2))


def src_of(a, k):
    dx, dc = STEPS[k]
    return lax.rem(a // 2 + 4 - dx, 4) * 2 + (lax.rem(a, 2) if dc == 0 else 1 - lax.rem(a, 2))


def swap16():
    r = np.arange(256)
    m = np.zeros((256, 256), np.float32)
    m[r, (r % 16) * 16 + r // 16] = 1.0
    return jnp.asarray(m, BF)


def vspec():
    return pl.BlockSpec(memory_space=pltpu.VMEM)


def sspec():
    return pl.BlockSpec(memory_space=pltpu.SMEM)


def spread_kernel(pos, perm, x_ref, ta_ref, *rest):
    tb, s = rest[:8], rest[8]
    a = pos[0]
    for d in range(W):
        x = x_ref[0, d]
        for o in range(16):
            ta_ref[o, d] = x[:, 256 * o : 256 * o + 256]
        halves = [
            jnp.concatenate([x[:, 128 * (16 * h + c) : 128 * (16 * h + c) + 128] for c in range(16)], axis=0)
            for h in range(2)
        ]
        y = jnp.dot(perm[...], jnp.concatenate(halves, axis=1), preferred_element_type=F32).astype(BF)
        for n in range(NOB):
            for h in range(2):
                s[n, d, 16 * h : 16 * h + 16] = y[16 * n : 16 * n + 16, 128 * h : 128 * h + 128]
    for k in range(8):
        t = dest_of(a, k)
        for i in range(2):
            tb[k][i, :, 0] = s[2 * t + i]


def spread(pos, perm, x):
    return pl.pallas_call(
        spread_kernel,
        grid=(NPD,),
        in_specs=[
            sspec(),
            pl.BlockSpec((256, 256), lambda i: (0, 0)),
            pl.BlockSpec((1, W, NOB, 4096), lambda i: (i, 0, 0, 0)),
        ],
        out_specs=[pl.BlockSpec((16, W, NOB, 256), lambda i: (0, i, 0, 0))]
        + [pl.BlockSpec((2, W, 1, 32, 128), lambda i: (0, 0, i, 0, 0))] * 8,
        out_shape=[jax.ShapeDtypeStruct((16, NPD * W, NOB, 256), BF)]
        + [jax.ShapeDtypeStruct((2, W, NPD, 32, 128), BF)] * 8,
        scratch_shapes=[pltpu.VMEM((NOB, W, 32, 128), BF)],
        compiler_params=pltpu.CompilerParams(vmem_limit_bytes=VLIM),
        cost_estimate=pl.CostEstimate(flops=10**9, bytes_accessed=12 * 10**6, transcendentals=0),
        name="spread",
    )(pos, perm, x)


def greens_kernel(pos, g_ref, k4_ref, w_ref):
    a = pos[0]
    lane = lax.broadcasted_iota(jnp.int32, (64, 128), 1)
    zero = jnp.zeros((64, 128), BF)

    def one(n, carry):
        for d in range(W):
            v = g_ref[n, 64 * d : 64 * d + 64, 0:64]
            vv = jnp.concatenate([v, v], axis=1)
            lo = jnp.where(lane < 64, vv, zero)
            hi = jnp.where(lane < 64, zero, vv)
            for r in range(4):
                for t in range(2):
                    part = zero if r // 2 != t else (lo if r % 2 == 0 else hi)
                    k4_ref[n, d, 64 * r : 64 * r + 64, 128 * t : 128 * t + 128] = part
        return carry

    lax.fori_loop(0, NOB, one, 0)
    z = jnp.zeros((32, 64), BF)
    for i in range(2):
        for g in range(2):
            for e in range(W):
                cols = []
                for d in range(W):
                    f = e - d + 1
                    if f < 0 or f >= W:
                        cols.append(z)
                        continue
                    m = 2 * a + i + d - 1
                    ok = (m >= 0) & (m < NOB)
                    mc = jnp.clip(m, 0, NOB - 1)
                    row = (f * 2 + g) * 32
                    v = g_ref[mc, row : row + 32, :][:, 64:128]
                    cols.append(jnp.where(ok, v, z))
                row = (g * W + e) * 32
                w_ref[i, row : row + 32, :] = jnp.concatenate(cols, axis=1)


def greens(pos, g):
    return pl.pallas_call(
        greens_kernel,
        in_specs=[sspec(), vspec()],
        out_specs=[vspec(), vspec()],
        out_shape=[
            jax.ShapeDtypeStruct((NOB, W, 256, 256), BF),
            jax.ShapeDtypeStruct((2, 192, 192), BF),
        ],
        compiler_params=pltpu.CompilerParams(vmem_limit_bytes=VLIM),
        cost_estimate=pl.CostEstimate(flops=10**6, bytes_accessed=8 * 10**6, transcendentals=0),
        name="greens",
    )(pos, g)


def second_kernel(pos, pat, perm, ta_ref, k4_ref, *rest):
    outs, s = rest[:8], rest[8]
    a = pos[0]
    s[0] = jnp.zeros(s.shape[1:], BF)
    s[NOB + 1] = jnp.zeros(s.shape[1:], BF)

    def regroup(g, carry):
        for d in range(W):
            x = ta_ref[pl.ds(16 * g, 16), d].reshape(256, 256)
            y = jnp.dot(perm[...], x, preferred_element_type=F32)
            for n in range(NOB):
                keep = pat[((a * NOB + n) * NG + g) * W + d] > 0
                part = y[16 * n : 16 * n + 16]
                s[n + 1, d, pl.ds(pl.multiple_of(16 * g, 16), 16)] = jnp.where(
                    keep, part, jnp.zeros_like(part)
                ).astype(BF)
        return carry

    lax.fori_loop(0, NG, regroup, 0)
    for k in range(8):
        t = dest_of(a, k)

        def one(i, carry, k=k, t=t):
            n = 2 * t + i
            for e in range(W):
                acc = None
                for d in range(W):
                    f = e - d + 1
                    if 0 <= f < W:
                        p = jnp.dot(s[n + d, f], k4_ref[n, d], preferred_element_type=F32)
                        acc = p if acc is None else acc + p
                outs[k][i * W + e] = acc.astype(BF)
            return carry

        lax.fori_loop(0, 2, one, 0)


def second_products(pos, pat, perm, ta, k4):
    return pl.pallas_call(
        second_kernel,
        in_specs=[sspec(), sspec(), vspec(), vspec(), vspec()],
        out_specs=[vspec()] * 8,
        out_shape=[jax.ShapeDtypeStruct((2 * W, 160, 256), BF)] * 8,
        scratch_shapes=[pltpu.VMEM((NOB + 2, W, 160, 256), BF)],
        compiler_params=pltpu.CompilerParams(vmem_limit_bytes=VLIM),
        cost_estimate=pl.CostEstimate(flops=4 * 10**9, bytes_accessed=15 * 10**6, transcendentals=0),
        name="second",
    )(pos, pat, perm, ta, k4)


def first_kernel(pos, pat, perm, w_ref, *rest):
    tb, out, s = rest[:8], rest[8], rest[9]
    a, o = pos[0], pos[1]
    lane = lax.broadcasted_iota(jnp.int32, (96, NPD * 128), 1)
    low = lax.rem(lane, 128) < 64
    for k in range(8):
        src = src_of(a, k)
        base = lax.rem(src, 2) * 40 + (src // 2) * 10

        def one(i, carry, k=k, src=src, base=base):
            n = 2 * a + i
            columns = []
            for p in range(NPD):
                rows = []
                for d in range(W):
                    keep = pat[((src * NOB + n) * NG + lax.div(o * NPD + p, ABS)) * W + d] > 0
                    x = tb[k][i, d, p]
                    x = jnp.where(keep, x, jnp.zeros_like(x))
                    rows.append(x)
                    rows.append(jnp.concatenate([x[:, 64:], x[:, :64]], axis=1))
                columns.append(jnp.concatenate(rows, axis=0))
            y = jnp.dot(w_ref[i], jnp.concatenate(columns, axis=1), preferred_element_type=F32)
            y = jnp.where(low, y[:96], y[96:]).astype(BF)
            for p in range(NPD):
                s[i, base + p] = y[:, 128 * p : 128 * p + 128]
            return carry

        lax.fori_loop(0, 2, one, 0)

    def regroup(j, carry):
        i = j // 5
        g = lax.rem(j, 5)
        tiles = s[i, pl.ds(16 * g, 16)]
        for e in range(W):
            x = jnp.concatenate(
                [tiles[:, 32 * e + 16 * h : 32 * e + 16 * h + 16].reshape(256, 128) for h in range(2)], axis=1
            )
            y = jnp.dot(perm[...], x, preferred_element_type=F32).astype(BF)
            for h in range(2):
                for q in range(16):
                    qq = 16 * h + q
                    out[qq // 2, i * W + e, pl.ds(pl.multiple_of(16 * g, 16), 16),
                        128 * (qq % 2) : 128 * (qq % 2) + 128] = y[16 * q : 16 * q + 16, 128 * h : 128 * h + 128]
        return carry

    lax.fori_loop(0, 10, regroup, 0)


def first_products(pos, pat, perm, w, tb):
    return pl.pallas_call(
        first_kernel,
        in_specs=[sspec(), sspec(), vspec(), vspec()] + [vspec()] * 8,
        out_specs=vspec(),
        out_shape=jax.ShapeDtypeStruct((16, 2 * W, 80, 256), BF),
        scratch_shapes=[pltpu.VMEM((2, 80, 96, 128), BF)],
        compiler_params=pltpu.CompilerParams(vmem_limit_bytes=VLIM),
        cost_estimate=pl.CostEstimate(flops=3 * 10**9, bytes_accessed=8 * 10**6, transcendentals=0),
        name="first",
    )(pos, pat, perm, w, *tb)


def chi_kernel(pos, first_ref, *rest):
    us, theirs, mine, rhs = rest[:8], rest[8], rest[9], rest[10]
    a = pos[0]
    core0 = lax.rem(a, 2) == 0
    for k in range(8):
        row = pl.multiple_of(src_of(a, k) * 160, 16)
        for kk in range(6):
            rhs[pl.ds(row, 160), 256 * kk : 256 * kk + 256] = us[k][kk]

    def tile(t, carry):
        lhs = jnp.concatenate([first_ref[:, kk].reshape(1280, 256) for kk in range(6)], axis=1)
        r = lax.dot_general(
            lhs,
            rhs[pl.ds(pl.multiple_of(256 * t, 256), 256)],
            (((1,), (1,)), ((), ())),
            preferred_element_type=F32,
        )
        cols = pl.ds(pl.multiple_of(256 * t, 256), 256)
        for b in range(16):
            lo, hi = r[80 * b : 80 * b + 40], r[80 * b + 40 : 80 * b + 80]
            mine[b, :, cols] = jnp.where(core0, lo, hi)
            theirs[b, :, cols] = jnp.where(core0, hi, lo)
        return carry

    lax.fori_loop(0, 5, tile, 0)


def chi_share(pos, first, us):
    return pl.pallas_call(
        chi_kernel,
        in_specs=[sspec(), vspec()] + [vspec()] * 8,
        out_specs=[vspec()] * 2,
        out_shape=[jax.ShapeDtypeStruct((16, 40, 1280), F32)] * 2,
        scratch_shapes=[pltpu.VMEM((1280, 1536), BF)],
        compiler_params=pltpu.CompilerParams(vmem_limit_bytes=VLIM),
        cost_estimate=pl.CostEstimate(flops=5 * 10**9, bytes_accessed=15 * 10**6, transcendentals=0),
        name="chi",
    )(pos, first, *us)


def own_masks(atom_size, n):
    partner = n + jnp.arange(W, dtype=jnp.int32) - R
    inside = (partner >= 0) & (partner < NOB)
    catalog = jnp.arange(NOB, dtype=jnp.int32)
    size_partner = jnp.sum(jnp.where(partner[:, None] == catalog, atom_size, 0), axis=1)
    size_owned = jnp.sum(jnp.where(n == catalog, atom_size, 0))
    funcs = jnp.arange(BS, dtype=jnp.int32)
    rows_ok = (funcs[None, :] < size_partner[:, None]) & inside[:, None]
    return inside, rows_ok[:, :, None] & (funcs < size_owned)[None, None, :]


def deinterleave():
    rows = np.zeros((2, 32, 64), np.float32)
    cols = np.zeros((2, 64, 64), np.float32)
    for g in range(2):
        for q in range(32):
            rows[g, q, 2 * q + g] = 1.0
        for j in range(2):
            for c in range(32):
                cols[g, 2 * c + (g ^ j), 32 * j + c] = 1.0
    return jnp.asarray(rows, BF), jnp.asarray(cols, BF)


def body(three_center, atom_size, tensor_pattern, green_occ, green_virt, green_pattern):
    a, o = lax.axis_index("aux"), lax.axis_index("orb")
    pos = jnp.stack([a, o]).astype(jnp.int32)
    perm = swap16()
    ta, *tb = spread(pos, perm, three_center.transpose(0, 2, 1, 3))
    ta = lax.all_to_all(ta, "orb", split_axis=0, concat_axis=0, tiled=True)
    tb = [tb[0]] + [lax.ppermute(tb[k], "aux", pairs_of(k)) for k in range(1, 8)]

    pat = jnp.pad(tensor_pattern.reshape(NG * W), (0, 2)).reshape(1, 32)
    pat = lax.all_gather(pat, ("aux", "orb"), axis=0, tiled=True)
    pat = pat[:, : NG * W].reshape(-1)
    inside, pair_ok = own_masks(atom_size, o)
    keep = ((green_pattern[0] > 0) | (jnp.arange(W) == R)) & inside
    mask = keep[:, None, None] & pair_ok
    occ = jnp.where(mask, green_occ.reshape(W, BS, BS), jnp.zeros((), BF))
    virt = jnp.where(mask, green_virt.reshape(W, BS, BS), jnp.zeros((), BF))
    rows, cols = deinterleave()
    occ = jnp.einsum("gql,flm->fgqm", rows, occ, preferred_element_type=F32).astype(BF)
    occ = jnp.einsum("fgqm,gmk->fgqk", occ, cols, preferred_element_type=F32).astype(BF)
    packed = jnp.concatenate([virt.reshape(192, 64), occ.reshape(192, 64)], axis=1)
    packed = lax.all_gather(packed[None], "orb", axis=0, tiled=True)
    k4, w = greens(pos, packed)

    us = second_products(pos, pat, perm, ta.reshape(160, W, NOB, 256), k4)
    first = first_products(pos, pat, perm, w, tb)
    first = lax.all_to_all(first, "orb", split_axis=0, concat_axis=0, tiled=True)
    us = [us[0]] + [lax.ppermute(us[k], "aux", pairs_of(k)) for k in range(1, 8)]

    theirs, mine = chi_share(pos, first, us)
    part = (mine + lax.ppermute(theirs, "aux", pairs_of(1))).astype(BF)
    part = lax.all_to_all(part, "orb", split_axis=0, concat_axis=0, tiled=True)
    part = jnp.sum(part.astype(F32), axis=0).reshape(4, NPD, 1280)
    x = a // 2
    total = lax.dynamic_index_in_dim(part, x, 0, keepdims=False)
    for dx in range(1, 4):
        piece = lax.dynamic_index_in_dim(part, lax.rem(x + dx, 4), 0, keepdims=False)
        total = total + lax.ppermute(piece, "aux", pairs_of(2 * dx))
    return total


def solution(mesh):
    return jax.shard_map(
        body,
        mesh=mesh,
        in_specs=(
            P(("aux", "orb"), None, None, None),
            P(),
            P("aux", "orb", None),
            P("orb", None, None),
            P("orb", None, None),
            P("orb", None),
        ),
        out_specs=P(("aux", "orb"), None),
        check_vma=False,
    )
```

```python
import functools

import jax
import jax.numpy as jnp
import numpy as np
from jax import lax
from jax.experimental import pallas as pl
from jax.experimental.pallas import tpu as pltpu
from jax.sharding import PartitionSpec as P

BS = 64
R = 1
W = 3
ABS = 16
NOB = 16
NPD = 10
NG = 10
BF = jnp.bfloat16
F32 = jnp.float32
VLIM = 56 * 1024 * 1024

STEPS = [(k // 2, k % 2) for k in range(8)]


def pairs_of(k):
    dx, dc = STEPS[k]
    return [(i, ((i // 2 + dx) % 4) * 2 + ((i % 2) ^ dc)) for i in range(8)]


def dest_of(a, k):
    dx, dc = STEPS[k]
    return lax.rem(a // 2 + dx, 4) * 2 + (lax.rem(a, 2) if dc == 0 else 1 - lax.rem(a, 2))


def pat_row(o, k, n):
    return k * NOB + lax.rem(o // 4 + 4 - n // 4, 4) * 4 + lax.rem(lax.rem(o, 4) + 4 - lax.rem(n, 4), 4)


def src_of(a, k):
    dx, dc = STEPS[k]
    return lax.rem(a // 2 + 4 - dx, 4) * 2 + (lax.rem(a, 2) if dc == 0 else 1 - lax.rem(a, 2))


def swap16():
    r = np.arange(256)
    m = np.zeros((256, 256), np.float32)
    m[r, (r % 16) * 16 + r // 16] = 1.0
    return jnp.asarray(m, BF)


def vspec():
    return pl.BlockSpec(memory_space=pltpu.VMEM)


def sspec():
    return pl.BlockSpec(memory_space=pltpu.SMEM)


def rows_kernel(x_ref, ta_ref):
    for d in range(W):
        for o in range(16):
            ta_ref[o, d] = x_ref[0, d, :, 256 * o : 256 * o + 256]


def row_slabs(x):
    return pl.pallas_call(
        rows_kernel,
        grid=(NPD,),
        in_specs=[pl.BlockSpec((1, W, NOB, 4096), lambda i: (i, 0, 0, 0))],
        out_specs=pl.BlockSpec((16, W, NOB, 256), lambda i: (0, i, 0, 0)),
        out_shape=jax.ShapeDtypeStruct((16, NPD * W, NOB, 256), BF),
        compiler_params=pltpu.CompilerParams(vmem_limit_bytes=VLIM),
        cost_estimate=pl.CostEstimate(flops=0, bytes_accessed=8 * 10**6, transcendentals=0),
        name="row_slabs",
    )(x)


def pairs_kernel(pos, perm, x_ref, *rest):
    tb, s = rest[:8], rest[8]
    a = pos[0]
    for d in range(W):
        x = x_ref[0, d]
        halves = [
            jnp.concatenate([x[:, 128 * (16 * h + c) : 128 * (16 * h + c) + 128] for c in range(16)], axis=0)
            for h in range(2)
        ]
        y = jnp.dot(perm[...], jnp.concatenate(halves, axis=1), preferred_element_type=F32).astype(BF)
        for n in range(NOB):
            for h in range(2):
                s[n, d, 16 * h : 16 * h + 16] = y[16 * n : 16 * n + 16, 128 * h : 128 * h + 128]
    for k in range(8):
        t = dest_of(a, k)
        for i in range(2):
            tb[k][i, :, 0] = s[2 * t + i]


def block_pairs(pos, perm, x):
    return pl.pallas_call(
        pairs_kernel,
        grid=(NPD,),
        in_specs=[
            sspec(),
            pl.BlockSpec((256, 256), lambda i: (0, 0)),
            pl.BlockSpec((1, W, NOB, 4096), lambda i: (i, 0, 0, 0)),
        ],
        out_specs=[pl.BlockSpec((2, W, 1, 32, 128), lambda i: (0, 0, i, 0, 0))] * 8,
        out_shape=[jax.ShapeDtypeStruct((2, W, NPD, 32, 128), BF)] * 8,
        scratch_shapes=[pltpu.VMEM((NOB, W, 32, 128), BF)],
        compiler_params=pltpu.CompilerParams(vmem_limit_bytes=VLIM),
        cost_estimate=pl.CostEstimate(flops=10**9, bytes_accessed=8 * 10**6, transcendentals=0),
        name="block_pairs",
    )(pos, perm, x)


def prep_kernel(pos, size, gpat, occ_ref, virt_ref, rows_ref, cols_ref, tpat_ref, out):
    n = pos[1]
    row = lax.broadcasted_iota(jnp.int32, (BS, BS), 0)
    col = lax.broadcasted_iota(jnp.int32, (BS, BS), 1)
    zero = jnp.zeros((BS, BS), BF)
    for d in range(W):
        m = n + d - R
        ok = (m >= 0) & (m < NOB)
        if d != R:
            ok = ok & (gpat[d] > 0)
        rows_in = jnp.where(ok, size[jnp.clip(m, 0, NOB - 1)], 0)
        mask = (row < rows_in) & (col < size[n])
        virt = jnp.where(mask, virt_ref[d], zero)
        occ = jnp.where(mask, occ_ref[d], zero)
        parts = []
        for g in range(2):
            t = jnp.dot(rows_ref[g], occ, preferred_element_type=F32).astype(BF)
            parts.append(jnp.dot(t, cols_ref[g], preferred_element_type=F32).astype(BF))
        out[64 * d : 64 * d + 64] = jnp.concatenate([virt, jnp.concatenate(parts, axis=0)], axis=1)
    out[192:208] = jnp.broadcast_to(tpat_ref[...].astype(F32), (16, 128)).astype(BF)


def prep(pos, size, gpat, occ, virt, rows, cols, tpat):
    return pl.pallas_call(
        prep_kernel,
        in_specs=[sspec()] * 3 + [vspec()] * 5,
        out_specs=vspec(),
        out_shape=jax.ShapeDtypeStruct((208, 128), BF),
        cost_estimate=pl.CostEstimate(flops=10**6, bytes_accessed=10**5, transcendentals=0),
        name="prep",
    )(pos, size, gpat, occ, virt, rows, cols, tpat)


def greens_kernel(pos, *rest):
    g4, k4_ref, w_ref, g_ref = rest[:4], rest[4], rest[5], rest[6]
    a, o = pos[0], pos[1]
    lane = lax.broadcasted_iota(jnp.int32, (64, 128), 1)
    zero = jnp.zeros((64, 128), BF)
    for dy in range(4):
        for dz in range(4):
            n = lax.rem(o // 4 + 4 - dy, 4) * 4 + lax.rem(lax.rem(o, 4) + 4 - dz, 4)
            g_ref[n] = g4[dy][dz, 0:192]

    def one(n, carry):
        for d in range(W):
            v = g_ref[n, 64 * d : 64 * d + 64, 0:64]
            vv = jnp.concatenate([v, v], axis=1)
            lo = jnp.where(lane < 64, vv, zero)
            hi = jnp.where(lane < 64, zero, vv)
            for r in range(4):
                for t in range(2):
                    part = zero if r // 2 != t else (lo if r % 2 == 0 else hi)
                    k4_ref[n, d, 64 * r : 64 * r + 64, 128 * t : 128 * t + 128] = part
        return carry

    lax.fori_loop(0, NOB, one, 0)
    z = jnp.zeros((32, 64), BF)
    for i in range(2):
        for g in range(2):
            for e in range(W):
                cols = []
                for d in range(W):
                    f = e - d + 1
                    if f < 0 or f >= W:
                        cols.append(z)
                        continue
                    m = 2 * a + i + d - 1
                    ok = (m >= 0) & (m < NOB)
                    mc = jnp.clip(m, 0, NOB - 1)
                    row = (f * 2 + g) * 32
                    v = g_ref[mc, row : row + 32, :][:, 64:128]
                    cols.append(jnp.where(ok, v, z))
                row = (g * W + e) * 32
                w_ref[i, row : row + 32, :] = jnp.concatenate(cols, axis=1)


def greens(pos, g4):
    return pl.pallas_call(
        greens_kernel,
        in_specs=[sspec()] + [vspec()] * 4,
        out_specs=[vspec(), vspec()],
        scratch_shapes=[pltpu.VMEM((NOB, 192, 128), BF)],
        out_shape=[
            jax.ShapeDtypeStruct((NOB, W, 256, 256), BF),
            jax.ShapeDtypeStruct((2, 192, 192), BF),
        ],
        compiler_params=pltpu.CompilerParams(vmem_limit_bytes=VLIM),
        cost_estimate=pl.CostEstimate(flops=10**6, bytes_accessed=8 * 10**6, transcendentals=0),
        name="greens",
    )(pos, *g4)


def second_kernel(pos, pat, perm, ta_ref, k4_ref, *rest):
    outs, s = rest[:8], rest[8]
    a, o = pos[0], pos[1]
    s[0] = jnp.zeros(s.shape[1:], BF)
    s[NOB + 1] = jnp.zeros(s.shape[1:], BF)

    def regroup(g, carry):
        for d in range(W):
            x = ta_ref[pl.ds(16 * g, 16), d].reshape(256, 256)
            y = jnp.dot(perm[...], x, preferred_element_type=F32)
            for n in range(NOB):
                keep = pat[pat_row(o, 0, n) * 32 + g * W + d] > 0
                part = y[16 * n : 16 * n + 16]
                s[n + 1, d, pl.ds(pl.multiple_of(16 * g, 16), 16)] = jnp.where(
                    keep, part, jnp.zeros_like(part)
                ).astype(BF)
        return carry

    lax.fori_loop(0, NG, regroup, 0)
    for k in range(8):
        t = dest_of(a, k)

        def one(i, carry, k=k, t=t):
            n = 2 * t + i
            for e in range(W):
                ds = [d for d in range(W) if 0 <= e - d + 1 < W]
                lhs = jnp.concatenate([s[n + d, e - d + 1] for d in ds], axis=1)
                rhs = k4_ref[n, ds[0] : ds[-1] + 1].reshape(256 * len(ds), 256)
                outs[k][i * W + e] = jnp.dot(lhs, rhs, preferred_element_type=F32).astype(BF)
            return carry

        lax.fori_loop(0, 2, one, 0)


def second_products(pos, pat, perm, ta, k4):
    return pl.pallas_call(
        second_kernel,
        in_specs=[sspec(), sspec(), vspec(), vspec(), vspec()],
        out_specs=[vspec()] * 8,
        out_shape=[jax.ShapeDtypeStruct((2 * W, 160, 256), BF)] * 8,
        scratch_shapes=[pltpu.VMEM((NOB + 2, W, 160, 256), BF)],
        compiler_params=pltpu.CompilerParams(vmem_limit_bytes=VLIM),
        cost_estimate=pl.CostEstimate(flops=4 * 10**9, bytes_accessed=15 * 10**6, transcendentals=0),
        name="second",
    )(pos, pat, perm, ta, k4)


def first_kernel(pos, pat, perm, w_ref, *rest):
    tb, out, s = rest[:8], rest[8], rest[9]
    a, o = pos[0], pos[1]
    lane = lax.broadcasted_iota(jnp.int32, (96, NPD * 128), 1)
    low = lax.rem(lane, 128) < 64
    for k in range(8):
        src = src_of(a, k)
        base = lax.rem(src, 2) * 40 + (src // 2) * 10

        def one(i, carry, k=k, src=src, base=base):
            n = 2 * a + i
            columns = []
            for p in range(NPD):
                rows = []
                for d in range(W):
                    keep = pat[pat_row(o, k, n) * 32 + lax.div(o * NPD + p, ABS) * W + d] > 0
                    x = tb[k][i, d, p]
                    x = jnp.where(keep, x, jnp.zeros_like(x))
                    rows.append(x)
                    rows.append(jnp.concatenate([x[:, 64:], x[:, :64]], axis=1))
                columns.append(jnp.concatenate(rows, axis=0))
            y = jnp.dot(w_ref[i], jnp.concatenate(columns, axis=1), preferred_element_type=F32)
            y = jnp.where(low, y[:96], y[96:]).astype(BF)
            for p in range(NPD):
                s[i, base + p] = y[:, 128 * p : 128 * p + 128]
            return carry

        lax.fori_loop(0, 2, one, 0)

    def regroup(j, carry):
        i = j // 5
        g = lax.rem(j, 5)
        tiles = s[i, pl.ds(16 * g, 16)]
        for e in range(W):
            x = jnp.concatenate(
                [tiles[:, 32 * e + 16 * h : 32 * e + 16 * h + 16].reshape(256, 128) for h in range(2)], axis=1
            )
            y = jnp.dot(perm[...], x, preferred_element_type=F32).astype(BF)
            for h in range(2):
                for q in range(16):
                    qq = 16 * h + q
                    out[qq // 2, i * W + e, pl.ds(pl.multiple_of(16 * g, 16), 16),
                        128 * (qq % 2) : 128 * (qq % 2) + 128] = y[16 * q : 16 * q + 16, 128 * h : 128 * h + 128]
        return carry

    lax.fori_loop(0, 10, regroup, 0)


def first_products(pos, pat, perm, w, tb):
    return pl.pallas_call(
        first_kernel,
        in_specs=[sspec(), sspec(), vspec(), vspec()] + [vspec()] * 8,
        out_specs=vspec(),
        out_shape=jax.ShapeDtypeStruct((16, 2 * W, 80, 256), BF),
        scratch_shapes=[pltpu.VMEM((2, 80, 96, 128), BF)],
        compiler_params=pltpu.CompilerParams(vmem_limit_bytes=VLIM),
        cost_estimate=pl.CostEstimate(flops=3 * 10**9, bytes_accessed=8 * 10**6, transcendentals=0),
        name="first",
    )(pos, pat, perm, w, *tb)


def chi_kernel(pos, first_ref, *rest):
    us, theirs, mine, rhs = rest[:8], rest[8], rest[9], rest[10]
    a = pos[0]
    core0 = lax.rem(a, 2) == 0
    t = pl.program_id(0)

    @pl.when(t == 0)
    def _():
        for k in range(8):
            row = pl.multiple_of(src_of(a, k) * 160, 16)
            for kk in range(6):
                rhs[pl.ds(row, 160), 256 * kk : 256 * kk + 256] = us[k][kk]


    lhs = jnp.concatenate([first_ref[:, kk].reshape(1280, 256) for kk in range(6)], axis=1)
    r = lax.dot_general(
        lhs,
        rhs[pl.ds(pl.multiple_of(256 * t, 256), 256)],
        (((1,), (1,)), ((), ())),
        preferred_element_type=F32,
    )
    for b in range(16):
        lo, hi = r[80 * b : 80 * b + 40], r[80 * b + 40 : 80 * b + 80]
        mine[b] = jnp.where(core0, lo, hi)
        theirs[b] = jnp.where(core0, hi, lo)


def chi_share(pos, first, us):
    return pl.pallas_call(
        chi_kernel,
        grid=(5,),
        in_specs=[sspec(), vspec()] + [vspec()] * 8,
        out_specs=[pl.BlockSpec((16, 40, 256), lambda t: (0, 0, t))] * 2,
        out_shape=[jax.ShapeDtypeStruct((16, 40, 1280), F32)] * 2,
        scratch_shapes=[pltpu.VMEM((1280, 1536), BF)],
        compiler_params=pltpu.CompilerParams(vmem_limit_bytes=VLIM),
        cost_estimate=pl.CostEstimate(flops=5 * 10**9, bytes_accessed=15 * 10**6, transcendentals=0),
        name="chi",
    )(pos, first, *us)


def deinterleave():
    rows = np.zeros((2, 32, 64), np.float32)
    cols = np.zeros((2, 64, 64), np.float32)
    for g in range(2):
        for q in range(32):
            rows[g, q, 2 * q + g] = 1.0
        for j in range(2):
            for c in range(32):
                cols[g, 2 * c + (g ^ j), 32 * j + c] = 1.0
    return jnp.asarray(rows, BF), jnp.asarray(cols, BF)


def orb_pairs(dy, dz):
    return [(i, ((i // 4 + dy) % 4) * 4 + (i % 4 + dz) % 4) for i in range(16)]


def body(three_center, atom_size, tensor_pattern, green_occ, green_virt, green_pattern):
    a, o = lax.axis_index("aux"), lax.axis_index("orb")
    pos = jnp.stack([a, o]).astype(jnp.int32)
    perm = swap16()
    rows, cols = deinterleave()
    tpat = jnp.pad(tensor_pattern.reshape(1, NG * W), ((0, 0), (0, 128 - NG * W)))
    own = prep(pos, atom_size, green_pattern.reshape(W), green_occ.reshape(W, BS, BS),
               green_virt.reshape(W, BS, BS), rows, cols, tpat)
    own, three_center = lax.optimization_barrier((own, three_center))
    x = three_center.transpose(0, 2, 1, 3)
    ta = lax.all_to_all(row_slabs(x), "orb", split_axis=0, concat_axis=0, tiled=True)
    tb = block_pairs(pos, perm, x)
    tb = [tb[0]] + [lax.ppermute(tb[k], "aux", pairs_of(k)) for k in range(1, 8)]

    line = jnp.stack([own] + [lax.ppermute(own, "orb", orb_pairs(0, dz)) for dz in range(1, 4)])
    plane = [line] + [lax.ppermute(line, "orb", orb_pairs(dy, 0)) for dy in range(1, 4)]
    k4, w = greens(pos, plane)
    pat = jnp.concatenate([g[:, 192] for g in plane], axis=0)
    pat = jnp.stack([pat, lax.ppermute(pat, "aux", pairs_of(1))])
    pat = jnp.stack([pat] + [lax.ppermute(pat, "aux", pairs_of(2 * dx)) for dx in range(1, 4)])
    pat = pat[..., :32].astype(jnp.int32).reshape(-1)

    us = second_products(pos, pat, perm, ta.reshape(160, W, NOB, 256), k4)
    first = first_products(pos, pat, perm, w, tb)
    first = lax.all_to_all(first, "orb", split_axis=0, concat_axis=0, tiled=True)
    us = [us[0]] + [lax.ppermute(us[k], "aux", pairs_of(k)) for k in range(1, 8)]

    theirs, mine = chi_share(pos, first, us)
    part = (mine + lax.ppermute(theirs, "aux", pairs_of(1))).astype(BF)
    part = lax.all_to_all(part, "orb", split_axis=0, concat_axis=0, tiled=True)
    part = jnp.sum(part.astype(F32), axis=0).reshape(4, NPD, 1280)
    x = a // 2
    total = lax.dynamic_index_in_dim(part, x, 0, keepdims=False)
    for dx in range(1, 4):
        piece = lax.dynamic_index_in_dim(part, lax.rem(x + dx, 4), 0, keepdims=False)
        total = total + lax.ppermute(piece, "aux", pairs_of(2 * dx))
    return total


def solution(mesh):
    return jax.shard_map(
        body,
        mesh=mesh,
        in_specs=(
            P(("aux", "orb"), None, None, None),
            P(),
            P("aux", "orb", None),
            P("orb", None, None),
            P("orb", None, None),
            P("orb", None),
        ),
        out_specs=P(("aux", "orb"), None),
        check_vma=False,
    )
```

```python
import functools

import jax
import jax.numpy as jnp
import numpy as np
from jax import lax
from jax.experimental import pallas as pl
from jax.experimental.pallas import tpu as pltpu
from jax.sharding import PartitionSpec as P

BS = 64
R = 1
W = 3
ABS = 16
NOB = 16
NPD = 10
NG = 10
BF = jnp.bfloat16
F32 = jnp.float32
VLIM = 56 * 1024 * 1024

STEPS = [(k // 2, k % 2) for k in range(8)]


def pairs_of(k):
    dx, dc = STEPS[k]
    return [(i, ((i // 2 + dx) % 4) * 2 + ((i % 2) ^ dc)) for i in range(8)]


def dest_of(a, k):
    dx, dc = STEPS[k]
    return lax.rem(a // 2 + dx, 4) * 2 + (lax.rem(a, 2) if dc == 0 else 1 - lax.rem(a, 2))


def meta_row(o, n):
    return lax.rem(o // 4 + 4 - n // 4, 4) * 4 + lax.rem(lax.rem(o, 4) + 4 - lax.rem(n, 4), 4)


def src_of(a, k):
    dx, dc = STEPS[k]
    return lax.rem(a // 2 + 4 - dx, 4) * 2 + (lax.rem(a, 2) if dc == 0 else 1 - lax.rem(a, 2))


def swap16():
    r = np.arange(256)
    m = np.zeros((256, 256), np.float32)
    m[r, (r % 16) * 16 + r // 16] = 1.0
    return jnp.asarray(m, BF)


def vspec():
    return pl.BlockSpec(memory_space=pltpu.VMEM)


def sspec():
    return pl.BlockSpec(memory_space=pltpu.SMEM)


def rows_kernel(x_ref, ta_ref):
    for p in range(2):
        for d in range(W):
            for o in range(16):
                ta_ref[o, p * W + d] = x_ref[p, d, :, 256 * o : 256 * o + 256]


def row_slabs(x):
    return pl.pallas_call(
        rows_kernel,
        grid=(NPD // 2,),
        in_specs=[pl.BlockSpec((2, W, NOB, 4096), lambda i: (i, 0, 0, 0))],
        out_specs=pl.BlockSpec((16, 2 * W, NOB, 256), lambda i: (0, i, 0, 0)),
        out_shape=jax.ShapeDtypeStruct((16, NPD * W, NOB, 256), BF),
        compiler_params=pltpu.CompilerParams(vmem_limit_bytes=VLIM),
        cost_estimate=pl.CostEstimate(flops=0, bytes_accessed=8 * 10**6, transcendentals=0),
        name="row_slabs",
    )(x)


def pairs_kernel(pos, meta, perm, x_ref, *rest):
    tb, s = rest[:8], rest[8]
    a, o = pos[0], pos[1]
    for p in range(2):
        g = lax.div(o * NPD + pl.program_id(0) * 2 + p, ABS)
        for d in range(W):
            x = x_ref[p, d]
            halves = [
                jnp.concatenate([x[:, 128 * (16 * h + c) : 128 * (16 * h + c) + 128] for c in range(16)], axis=0)
                for h in range(2)
            ]
            y = jnp.dot(perm[...], jnp.concatenate(halves, axis=1), preferred_element_type=F32)
            for n in range(NOB):
                part = y[16 * n : 16 * n + 16]
                keep = meta[meta_row(o, n) * 128 + g * W + d] > 0
                part = jnp.where(keep, part, jnp.zeros_like(part)).astype(BF)
                for h in range(2):
                    s[n, d, p, 16 * h : 16 * h + 16] = part[:, 128 * h : 128 * h + 128]
    for k in range(8):
        t = dest_of(a, k)
        for i in range(2):
            tb[k][i] = s[2 * t + i]


def block_pairs(pos, meta, perm, x):
    return pl.pallas_call(
        pairs_kernel,
        grid=(NPD // 2,),
        in_specs=[
            sspec(),
            sspec(),
            pl.BlockSpec((256, 256), lambda i: (0, 0)),
            pl.BlockSpec((2, W, NOB, 4096), lambda i: (i, 0, 0, 0)),
        ],
        out_specs=[pl.BlockSpec((2, W, 2, 32, 128), lambda i: (0, 0, i, 0, 0))] * 8,
        out_shape=[jax.ShapeDtypeStruct((2, W, NPD, 32, 128), BF)] * 8,
        scratch_shapes=[pltpu.VMEM((NOB, W, 2, 32, 128), BF)],
        compiler_params=pltpu.CompilerParams(vmem_limit_bytes=VLIM),
        cost_estimate=pl.CostEstimate(flops=10**9, bytes_accessed=8 * 10**6, transcendentals=0),
        name="block_pairs",
    )(pos, meta, perm, x)


def greens_kernel(pos, size, meta, g_ref, rows_ref, cols_ref, k4_ref, w_ref, o_ref):
    a, o = pos[0], pos[1]
    lane = lax.broadcasted_iota(jnp.int32, (64, 128), 1)
    zero = jnp.zeros((64, 128), BF)
    row = lax.broadcasted_iota(jnp.int32, (BS, BS), 0)
    col = lax.broadcasted_iota(jnp.int32, (BS, BS), 1)

    def one(n, carry):
        r = meta_row(o, n)
        for d in range(W):
            m = n + d - R
            ok = (m >= 0) & (m < NOB)
            if d != R:
                ok = ok & (meta[r * 128 + NG * W + d] > 0)
            rows_in = jnp.where(ok, size[jnp.clip(m, 0, NOB - 1)], 0)
            mask = (row < rows_in) & (col < size[n])
            occ = jnp.where(mask, g_ref[r, d], jnp.zeros((BS, BS), BF))
            v = jnp.where(mask, g_ref[r, W + d], jnp.zeros((BS, BS), BF))
            for g in range(2):
                t = jnp.dot(rows_ref[g], occ, preferred_element_type=F32).astype(BF)
                o_ref[n, d, 32 * g : 32 * g + 32] = jnp.dot(
                    t, cols_ref[g], preferred_element_type=F32
                ).astype(BF)
            vv = jnp.concatenate([v, v], axis=1)
            lo = jnp.where(lane < 64, vv, zero)
            hi = jnp.where(lane < 64, zero, vv)
            for q in range(4):
                for t in range(2):
                    part = zero if q // 2 != t else (lo if q % 2 == 0 else hi)
                    k4_ref[n, d, 64 * q : 64 * q + 64, 128 * t : 128 * t + 128] = part
        return carry

    lax.fori_loop(0, NOB, one, 0)
    z = jnp.zeros((32, 64), BF)
    for i in range(2):
        for g in range(2):
            for e in range(W):
                cols = []
                for d in range(W):
                    f = e - d + 1
                    if f < 0 or f >= W:
                        cols.append(z)
                        continue
                    m = 2 * a + i + d - 1
                    ok = (m >= 0) & (m < NOB)
                    mc = jnp.clip(m, 0, NOB - 1)
                    v = o_ref[mc, f, 32 * g : 32 * g + 32]
                    cols.append(jnp.where(ok, v, z))
                row = (g * W + e) * 32
                w_ref[i, row : row + 32, :] = jnp.concatenate(cols, axis=1)


def greens(pos, size, meta, g, rows, cols):
    return pl.pallas_call(
        greens_kernel,
        in_specs=[sspec()] * 3 + [vspec()] * 3,
        out_specs=[vspec(), vspec()],
        scratch_shapes=[pltpu.VMEM((NOB, W, 64, 64), BF)],
        out_shape=[
            jax.ShapeDtypeStruct((NOB, W, 256, 256), BF),
            jax.ShapeDtypeStruct((2, 192, 192), BF),
        ],
        compiler_params=pltpu.CompilerParams(vmem_limit_bytes=VLIM),
        cost_estimate=pl.CostEstimate(flops=10**6, bytes_accessed=8 * 10**6, transcendentals=0),
        name="greens",
    )(pos, size, meta, g, rows, cols)


def second_kernel(pos, pat, perm, ta_ref, k4_ref, *rest):
    outs, s = rest[:8], rest[8]
    a, o = pos[0], pos[1]
    s[0] = jnp.zeros(s.shape[1:], BF)
    s[NOB + 1] = jnp.zeros(s.shape[1:], BF)

    def regroup(g, carry):
        for d in range(W):
            x = ta_ref[pl.ds(16 * g, 16), d].reshape(256, 256)
            y = jnp.dot(perm[...], x, preferred_element_type=F32)
            for n in range(NOB):
                keep = pat[meta_row(o, n) * 128 + g * W + d] > 0
                part = y[16 * n : 16 * n + 16]
                s[n + 1, d, pl.ds(pl.multiple_of(16 * g, 16), 16)] = jnp.where(
                    keep, part, jnp.zeros_like(part)
                ).astype(BF)
        return carry

    lax.fori_loop(0, NG, regroup, 0)
    for k in range(8):
        t = dest_of(a, k)

        def one(i, carry, k=k, t=t):
            n = 2 * t + i
            for e in range(W):
                ds = [d for d in range(W) if 0 <= e - d + 1 < W]
                lhs = jnp.concatenate([s[n + d, e - d + 1] for d in ds], axis=1)
                rhs = k4_ref[n, ds[0] : ds[-1] + 1].reshape(256 * len(ds), 256)
                outs[k][i * W + e] = jnp.dot(lhs, rhs, preferred_element_type=F32).astype(BF)
            return carry

        lax.fori_loop(0, 2, one, 0)


def second_products(pos, pat, perm, ta, k4):
    return pl.pallas_call(
        second_kernel,
        in_specs=[sspec(), sspec(), vspec(), vspec(), vspec()],
        out_specs=[vspec()] * 8,
        out_shape=[jax.ShapeDtypeStruct((2 * W, 160, 256), BF)] * 8,
        scratch_shapes=[pltpu.VMEM((NOB + 2, W, 160, 256), BF)],
        compiler_params=pltpu.CompilerParams(vmem_limit_bytes=VLIM),
        cost_estimate=pl.CostEstimate(flops=4 * 10**9, bytes_accessed=15 * 10**6, transcendentals=0),
        name="second",
    )(pos, pat, perm, ta, k4)


def first_kernel(pos, perm, w_ref, *rest):
    tb, out, s = rest[:8], rest[8], rest[9]
    a = pos[0]
    lane = lax.broadcasted_iota(jnp.int32, (96, NPD * 128), 1)
    low = lax.rem(lane, 128) < 64
    for k in range(8):
        src = src_of(a, k)
        base = lax.rem(src, 2) * 40 + (src // 2) * 10

        def one(i, carry, k=k, base=base):
            columns = []
            for p in range(NPD):
                rows = []
                for d in range(W):
                    x = tb[k][i, d, p]
                    rows.append(x)
                    rows.append(jnp.concatenate([x[:, 64:], x[:, :64]], axis=1))
                columns.append(jnp.concatenate(rows, axis=0))
            y = jnp.dot(w_ref[i], jnp.concatenate(columns, axis=1), preferred_element_type=F32)
            y = jnp.where(low, y[:96], y[96:]).astype(BF)
            for p in range(NPD):
                s[i, base + p] = y[:, 128 * p : 128 * p + 128]
            return carry

        lax.fori_loop(0, 2, one, 0)

    def regroup(j, carry):
        i = j // 5
        g = lax.rem(j, 5)
        tiles = s[i, pl.ds(16 * g, 16)]
        for e in range(W):
            x = jnp.concatenate(
                [tiles[:, 32 * e + 16 * h : 32 * e + 16 * h + 16].reshape(256, 128) for h in range(2)], axis=1
            )
            y = jnp.dot(perm[...], x, preferred_element_type=F32).astype(BF)
            for h in range(2):
                for q in range(16):
                    qq = 16 * h + q
                    out[qq // 2, i * W + e, pl.ds(pl.multiple_of(16 * g, 16), 16),
                        128 * (qq % 2) : 128 * (qq % 2) + 128] = y[16 * q : 16 * q + 16, 128 * h : 128 * h + 128]
        return carry

    lax.fori_loop(0, 10, regroup, 0)


def first_products(pos, perm, w, tb):
    return pl.pallas_call(
        first_kernel,
        in_specs=[sspec(), vspec(), vspec()] + [vspec()] * 8,
        out_specs=vspec(),
        out_shape=jax.ShapeDtypeStruct((16, 2 * W, 80, 256), BF),
        scratch_shapes=[pltpu.VMEM((2, 80, 96, 128), BF)],
        compiler_params=pltpu.CompilerParams(vmem_limit_bytes=VLIM),
        cost_estimate=pl.CostEstimate(flops=3 * 10**9, bytes_accessed=8 * 10**6, transcendentals=0),
        name="first",
    )(pos, perm, w, *tb)


def chi_kernel(pos, first_ref, *rest):
    us, theirs, mine, rhs = rest[:8], rest[8], rest[9], rest[10]
    a = pos[0]
    core0 = lax.rem(a, 2) == 0
    t = pl.program_id(0)

    @pl.when(t == 0)
    def _():
        for k in range(8):
            row = pl.multiple_of(src_of(a, k) * 160, 16)
            for kk in range(6):
                rhs[pl.ds(row, 160), 256 * kk : 256 * kk + 256] = us[k][kk]


    lhs = jnp.concatenate([first_ref[:, kk].reshape(1280, 256) for kk in range(6)], axis=1)
    r = lax.dot_general(
        lhs,
        rhs[pl.ds(pl.multiple_of(256 * t, 256), 256)],
        (((1,), (1,)), ((), ())),
        preferred_element_type=F32,
    )
    for b in range(16):
        lo, hi = r[80 * b : 80 * b + 40], r[80 * b + 40 : 80 * b + 80]
        mine[b] = jnp.where(core0, lo, hi)
        theirs[b] = jnp.where(core0, hi, lo)


def chi_share(pos, first, us):
    return pl.pallas_call(
        chi_kernel,
        grid=(5,),
        in_specs=[sspec(), vspec()] + [vspec()] * 8,
        out_specs=[pl.BlockSpec((16, 40, 256), lambda t: (0, 0, t))] * 2,
        out_shape=[jax.ShapeDtypeStruct((16, 40, 1280), F32)] * 2,
        scratch_shapes=[pltpu.VMEM((1280, 1536), BF)],
        compiler_params=pltpu.CompilerParams(vmem_limit_bytes=VLIM),
        cost_estimate=pl.CostEstimate(flops=5 * 10**9, bytes_accessed=15 * 10**6, transcendentals=0),
        name="chi",
    )(pos, first, *us)


def deinterleave():
    rows = np.zeros((2, 32, 64), np.float32)
    cols = np.zeros((2, 64, 64), np.float32)
    for g in range(2):
        for q in range(32):
            rows[g, q, 2 * q + g] = 1.0
        for j in range(2):
            for c in range(32):
                cols[g, 2 * c + (g ^ j), 32 * j + c] = 1.0
    return jnp.asarray(rows, BF), jnp.asarray(cols, BF)


def orb_pairs(dy, dz):
    return [(i, ((i // 4 + dy) % 4) * 4 + (i % 4 + dz) % 4) for i in range(16)]


def body(three_center, atom_size, tensor_pattern, green_occ, green_virt, green_pattern):
    a, o = lax.axis_index("aux"), lax.axis_index("orb")
    pos = jnp.stack([a, o]).astype(jnp.int32)
    perm = swap16()
    rows, cols = deinterleave()
    x = three_center.transpose(0, 2, 1, 3)

    marks = jnp.concatenate([tensor_pattern.reshape(1, NG * W), green_pattern], axis=1).astype(BF)
    marks = jnp.pad(marks, ((0, 1), (0, 4096 - NG * W - W)))
    own = jnp.concatenate([green_occ[0], green_virt[0], marks], axis=0)
    line = jnp.stack([own] + [lax.ppermute(own, "orb", orb_pairs(0, dz)) for dz in range(1, 4)])
    plane = [line] + [lax.ppermute(line, "orb", orb_pairs(dy, 0)) for dy in range(1, 4)]
    *plane, ta = lax.optimization_barrier((*plane, row_slabs(x)))
    ta = lax.all_to_all(ta, "orb", split_axis=0, concat_axis=0, tiled=True)
    meta = jnp.concatenate([g[:, 2 * W, :128] for g in plane], axis=0).astype(jnp.int32).reshape(-1)
    tb = block_pairs(pos, meta, perm, x)
    tb = [tb[0]] + [lax.ppermute(tb[k], "aux", pairs_of(k)) for k in range(1, 8)]
    blocks = jnp.concatenate([g[:, : 2 * W] for g in plane], axis=0).reshape(NOB, 2 * W, BS, BS)
    k4, w = greens(pos, atom_size, meta, blocks, rows, cols)

    us = second_products(pos, meta, perm, ta.reshape(160, W, NOB, 256), k4)
    first = first_products(pos, perm, w, tb)
    first = lax.all_to_all(first, "orb", split_axis=0, concat_axis=0, tiled=True)
    us = [us[0]] + [lax.ppermute(us[k], "aux", pairs_of(k)) for k in range(1, 8)]

    theirs, mine = chi_share(pos, first, us)
    part = (mine + lax.ppermute(theirs, "aux", pairs_of(1))).astype(BF)
    part = lax.all_to_all(part, "orb", split_axis=0, concat_axis=0, tiled=True)
    part = jnp.sum(part.astype(F32), axis=0).reshape(4, NPD, 1280)
    x = a // 2
    total = lax.dynamic_index_in_dim(part, x, 0, keepdims=False)
    for dx in range(1, 4):
        piece = lax.dynamic_index_in_dim(part, lax.rem(x + dx, 4), 0, keepdims=False)
        total = total + lax.ppermute(piece, "aux", pairs_of(2 * dx))
    return total


def solution(mesh):
    return jax.shard_map(
        body,
        mesh=mesh,
        in_specs=(
            P(("aux", "orb"), None, None, None),
            P(),
            P("aux", "orb", None),
            P("orb", None, None),
            P("orb", None, None),
            P("orb", None),
        ),
        out_specs=P(("aux", "orb"), None),
        check_vma=False,
    )
```

```python
import functools

import jax
import jax.numpy as jnp
import numpy as np
from jax import lax
from jax.experimental import pallas as pl
from jax.experimental.pallas import tpu as pltpu
from jax.sharding import PartitionSpec as P

BS = 64
R = 1
W = 3
ABS = 16
NOB = 16
NPD = 10
NG = 10
BF = jnp.bfloat16
F32 = jnp.float32
VLIM = 56 * 1024 * 1024

STEPS = [(k // 2, k % 2) for k in range(8)]


def pairs_of(k):
    dx, dc = STEPS[k]
    return [(i, ((i // 2 + dx) % 4) * 2 + ((i % 2) ^ dc)) for i in range(8)]


def dest_of(a, k):
    dx, dc = STEPS[k]
    return lax.rem(a // 2 + dx, 4) * 2 + (lax.rem(a, 2) if dc == 0 else 1 - lax.rem(a, 2))


def src_of(a, k):
    dx, dc = STEPS[k]
    return lax.rem(a // 2 + 4 - dx, 4) * 2 + (lax.rem(a, 2) if dc == 0 else 1 - lax.rem(a, 2))


def swap16():
    r = np.arange(256)
    m = np.zeros((256, 256), np.float32)
    m[r, (r % 16) * 16 + r // 16] = 1.0
    return jnp.asarray(m, BF)


def vspec():
    return pl.BlockSpec(memory_space=pltpu.VMEM)


def sspec():
    return pl.BlockSpec(memory_space=pltpu.SMEM)


def rows_kernel(x_ref, ta_ref):
    for p in range(2):
        for d in range(W):
            for o in range(16):
                ta_ref[o, p * W + d] = x_ref[p, d, :, 256 * o : 256 * o + 256]


def row_slabs(x):
    return pl.pallas_call(
        rows_kernel,
        grid=(NPD // 2,),
        in_specs=[pl.BlockSpec((2, W, NOB, 4096), lambda i: (i, 0, 0, 0))],
        out_specs=pl.BlockSpec((16, 2 * W, NOB, 256), lambda i: (0, i, 0, 0)),
        out_shape=jax.ShapeDtypeStruct((16, NPD * W, NOB, 256), BF),
        compiler_params=pltpu.CompilerParams(vmem_limit_bytes=VLIM),
        cost_estimate=pl.CostEstimate(flops=0, bytes_accessed=8 * 10**6, transcendentals=0),
        name="row_slabs",
    )(x)


def pairs_kernel(pos, perm, x_ref, *rest):
    tb, s = rest[:8], rest[8]
    a = pos[0]
    for p in range(2):
        for d in range(W):
            x = x_ref[p, d]
            halves = [
                jnp.concatenate([x[:, 128 * (16 * h + c) : 128 * (16 * h + c) + 128] for c in range(16)], axis=0)
                for h in range(2)
            ]
            y = jnp.dot(perm[...], jnp.concatenate(halves, axis=1), preferred_element_type=F32).astype(BF)
            for n in range(NOB):
                part = y[16 * n : 16 * n + 16]
                for h in range(2):
                    s[n, d, p, 16 * h : 16 * h + 16] = part[:, 128 * h : 128 * h + 128]
    for k in range(8):
        t = dest_of(a, k)
        for i in range(2):
            tb[k][i] = s[2 * t + i]


def block_pairs(pos, perm, x):
    return pl.pallas_call(
        pairs_kernel,
        grid=(NPD // 2,),
        in_specs=[
            sspec(),
            pl.BlockSpec((256, 256), lambda i: (0, 0)),
            pl.BlockSpec((2, W, NOB, 4096), lambda i: (i, 0, 0, 0)),
        ],
        out_specs=[pl.BlockSpec((2, W, 2, 32, 128), lambda i: (0, 0, i, 0, 0))] * 8,
        out_shape=[jax.ShapeDtypeStruct((2, W, NPD, 32, 128), BF)] * 8,
        scratch_shapes=[pltpu.VMEM((NOB, W, 2, 32, 128), BF)],
        compiler_params=pltpu.CompilerParams(vmem_limit_bytes=VLIM),
        cost_estimate=pl.CostEstimate(flops=10**9, bytes_accessed=8 * 10**6, transcendentals=0),
        name="block_pairs",
    )(pos, perm, x)


def greens_kernel(pos, size, meta, g_ref, rows_ref, cols_ref, v_ref, w_ref, o_ref):
    a = pos[0]
    row = lax.broadcasted_iota(jnp.int32, (BS, BS), 0)
    col = lax.broadcasted_iota(jnp.int32, (BS, BS), 1)

    def one(n, carry):
        for d in range(W):
            m = n + d - R
            ok = (m >= 0) & (m < NOB)
            if d != R:
                ok = ok & (meta[n * 128 + NG * W + d] > 0)
            rows_in = jnp.where(ok, size[jnp.clip(m, 0, NOB - 1)], 0)
            mask = (row < rows_in) & (col < size[n])
            occ = jnp.where(mask, g_ref[n, d], jnp.zeros((BS, BS), BF))
            v = jnp.where(mask, g_ref[n, W + d], jnp.zeros((BS, BS), BF))
            for g in range(2):
                t = jnp.dot(rows_ref[g], occ, preferred_element_type=F32).astype(BF)
                o_ref[n, d, 32 * g : 32 * g + 32] = jnp.dot(
                    t, cols_ref[g], preferred_element_type=F32
                ).astype(BF)
            v_ref[n, d] = jnp.concatenate([v, v], axis=1)
        return carry

    lax.fori_loop(0, NOB, one, 0)
    z = jnp.zeros((32, 64), BF)
    for i in range(2):
        for g in range(2):
            for e in range(W):
                cols = []
                for d in range(W):
                    f = e - d + 1
                    if f < 0 or f >= W:
                        cols.append(z)
                        continue
                    m = 2 * a + i + d - 1
                    ok = (m >= 0) & (m < NOB)
                    mc = jnp.clip(m, 0, NOB - 1)
                    v = o_ref[mc, f, 32 * g : 32 * g + 32]
                    cols.append(jnp.where(ok, v, z))
                row = (g * W + e) * 32
                w_ref[i, row : row + 32, :] = jnp.concatenate(cols, axis=1)


def greens(pos, size, meta, g, rows, cols):
    return pl.pallas_call(
        greens_kernel,
        in_specs=[sspec()] * 3 + [vspec()] * 3,
        out_specs=[vspec(), vspec()],
        scratch_shapes=[pltpu.VMEM((NOB, W, 64, 64), BF)],
        out_shape=[
            jax.ShapeDtypeStruct((NOB, W, BS, 128), BF),
            jax.ShapeDtypeStruct((2, 192, 192), BF),
        ],
        compiler_params=pltpu.CompilerParams(vmem_limit_bytes=VLIM),
        cost_estimate=pl.CostEstimate(flops=10**6, bytes_accessed=8 * 10**6, transcendentals=0),
        name="greens",
    )(pos, size, meta, g, rows, cols)


def second_kernel(pos, pat, perm, ta_ref, v_ref, *rest):
    outs, s, kb = rest[:8], rest[8], rest[9]
    a = pos[0]
    low = lax.broadcasted_iota(jnp.int32, (BS, 128), 1) < 64
    zero = jnp.zeros((BS, 128), BF)
    kb[...] = jnp.zeros(kb.shape, BF)
    s[0] = jnp.zeros(s.shape[1:], BF)
    s[NOB + 1] = jnp.zeros(s.shape[1:], BF)

    def regroup(g, carry):
        for d in range(W):
            x = ta_ref[pl.ds(16 * g, 16), d].reshape(256, 256)
            y = jnp.dot(perm[...], x, preferred_element_type=F32)
            for n in range(NOB):
                keep = pat[n * 128 + g * W + d] > 0
                part = y[16 * n : 16 * n + 16]
                s[n + 1, d, pl.ds(pl.multiple_of(16 * g, 16), 16)] = jnp.where(
                    keep, part, jnp.zeros_like(part)
                ).astype(BF)
        return carry

    lax.fori_loop(0, NG, regroup, 0)
    for k in range(8):
        t = dest_of(a, k)

        def one(i, carry, k=k, t=t):
            n = 2 * t + i
            for d in range(W):
                v = v_ref[n, d]
                lo, hi = jnp.where(low, v, zero), jnp.where(low, zero, v)
                for q in range(4):
                    row, col = 256 * d + 64 * q, 128 * (q // 2)
                    kb[row : row + 64, col : col + 128] = hi if q % 2 else lo
            for e in range(W):
                ds = [d for d in range(W) if 0 <= e - d + 1 < W]
                lhs = jnp.concatenate([s[n + d, e - d + 1] for d in ds], axis=1)
                rhs = kb[256 * ds[0] : 256 * ds[-1] + 256]
                outs[k][i * W + e] = jnp.dot(lhs, rhs, preferred_element_type=F32).astype(BF)
            return carry

        lax.fori_loop(0, 2, one, 0)


def second_products(pos, pat, perm, ta, v):
    return pl.pallas_call(
        second_kernel,
        in_specs=[sspec(), sspec(), vspec(), vspec(), vspec()],
        out_specs=[vspec()] * 8,
        out_shape=[jax.ShapeDtypeStruct((2 * W, 160, 256), BF)] * 8,
        scratch_shapes=[pltpu.VMEM((NOB + 2, W, 160, 256), BF), pltpu.VMEM((256 * W, 256), BF)],
        compiler_params=pltpu.CompilerParams(vmem_limit_bytes=VLIM),
        cost_estimate=pl.CostEstimate(flops=4 * 10**9, bytes_accessed=15 * 10**6, transcendentals=0),
        name="second",
    )(pos, pat, perm, ta, v)


def first_kernel(pos, pat, perm, w_ref, *rest):
    tb, out, s = rest[:8], rest[8], rest[9]
    a, o = pos[0], pos[1]
    lane = lax.broadcasted_iota(jnp.int32, (96, NPD * 128), 1)
    low = lax.rem(lane, 128) < 64
    for k in range(8):
        src = src_of(a, k)
        base = lax.rem(src, 2) * 40 + (src // 2) * 10

        def one(i, carry, k=k, base=base):
            n = 2 * a + i
            columns = []
            for p in range(NPD):
                rows = []
                for d in range(W):
                    keep = pat[(k * NOB + n) * 32 + lax.div(o * NPD + p, ABS) * W + d] > 0
                    x = tb[k][i, d, p]
                    x = jnp.where(keep, x, jnp.zeros_like(x))
                    rows.append(x)
                    rows.append(jnp.concatenate([x[:, 64:], x[:, :64]], axis=1))
                columns.append(jnp.concatenate(rows, axis=0))
            y = jnp.dot(w_ref[i], jnp.concatenate(columns, axis=1), preferred_element_type=F32)
            y = jnp.where(low, y[:96], y[96:]).astype(BF)
            for p in range(NPD):
                s[i, base + p] = y[:, 128 * p : 128 * p + 128]
            return carry

        lax.fori_loop(0, 2, one, 0)

    def regroup(j, carry):
        i = j // 5
        g = lax.rem(j, 5)
        tiles = s[i, pl.ds(16 * g, 16)]
        for e in range(W):
            x = jnp.concatenate(
                [tiles[:, 32 * e + 16 * h : 32 * e + 16 * h + 16].reshape(256, 128) for h in range(2)], axis=1
            )
            y = jnp.dot(perm[...], x, preferred_element_type=F32).astype(BF)
            for h in range(2):
                for q in range(16):
                    qq = 16 * h + q
                    out[qq // 2, i * W + e, pl.ds(pl.multiple_of(16 * g, 16), 16),
                        128 * (qq % 2) : 128 * (qq % 2) + 128] = y[16 * q : 16 * q + 16, 128 * h : 128 * h + 128]
        return carry

    lax.fori_loop(0, 10, regroup, 0)


def first_products(pos, pat, perm, w, tb):
    return pl.pallas_call(
        first_kernel,
        in_specs=[sspec(), sspec(), vspec(), vspec()] + [vspec()] * 8,
        out_specs=vspec(),
        out_shape=jax.ShapeDtypeStruct((16, 2 * W, 80, 256), BF),
        scratch_shapes=[pltpu.VMEM((2, 80, 96, 128), BF)],
        compiler_params=pltpu.CompilerParams(vmem_limit_bytes=VLIM),
        cost_estimate=pl.CostEstimate(flops=3 * 10**9, bytes_accessed=8 * 10**6, transcendentals=0),
        name="first",
    )(pos, pat, perm, w, *tb)


HALVES = [(0, 1, 6, 7), (4, 5, 2, 3)]


def chi_kernel(half, pos, first_ref, *rest):
    us, theirs, mine, rhs = rest[:4], rest[4], rest[5], rest[6]
    core = lax.rem(pos[0], 2)
    for j, k in enumerate(HALVES[half]):
        c = core if k % 2 == 0 else 1 - core
        row = pl.multiple_of((j // 2) * 320 + c * 160, 32)
        for kk in range(6):
            rhs[pl.ds(row, 160), 256 * kk : 256 * kk + 256] = us[j][kk]
    for c0, cw in ((0, 256), (256, 256), (512, 128)):
        lhs = jnp.concatenate([first_ref[:, kk].reshape(1280, 256) for kk in range(6)], axis=1)
        r = lax.dot_general(
            lhs, rhs[c0 : c0 + cw], (((1,), (1,)), ((), ())), preferred_element_type=F32
        )
        for b in range(16):
            lo, hi = r[80 * b : 80 * b + 40], r[80 * b + 40 : 80 * b + 80]
            mine[b, :, c0 : c0 + cw] = jnp.where(core == 0, lo, hi)
            theirs[b, :, c0 : c0 + cw] = jnp.where(core == 0, hi, lo).astype(BF)


def chi_share(half, pos, first, us):
    return pl.pallas_call(
        functools.partial(chi_kernel, half),
        in_specs=[sspec(), vspec()] + [vspec()] * 4,
        out_specs=[vspec()] * 2,
        out_shape=[jax.ShapeDtypeStruct((16, 40, 640), BF), jax.ShapeDtypeStruct((16, 40, 640), F32)],
        scratch_shapes=[pltpu.VMEM((640, 1536), BF)],
        compiler_params=pltpu.CompilerParams(vmem_limit_bytes=VLIM),
        cost_estimate=pl.CostEstimate(flops=25 * 10**8, bytes_accessed=10 * 10**6, transcendentals=0),
        name="chi",
    )(pos, first, *[us[k] for k in HALVES[half]])


def deinterleave():
    rows = np.zeros((2, 32, 64), np.float32)
    cols = np.zeros((2, 64, 64), np.float32)
    for g in range(2):
        for q in range(32):
            rows[g, q, 2 * q + g] = 1.0
        for j in range(2):
            for c in range(32):
                cols[g, 2 * c + (g ^ j), 32 * j + c] = 1.0
    return jnp.asarray(rows, BF), jnp.asarray(cols, BF)


def body(three_center, atom_size, tensor_pattern, green_occ, green_virt, green_pattern):
    a, o = lax.axis_index("aux"), lax.axis_index("orb")
    pos = jnp.stack([a, o]).astype(jnp.int32)
    perm = swap16()
    rows, cols = deinterleave()
    x = three_center.transpose(0, 2, 1, 3)

    marks = jnp.concatenate([tensor_pattern.reshape(1, NG * W), green_pattern], axis=1).astype(BF)
    marks = jnp.pad(marks, ((0, 1), (0, 4096 - NG * W - W)))
    own = jnp.concatenate([green_occ[0], green_virt[0], marks], axis=0)
    every = jnp.broadcast_to(own[None], (NOB,) + own.shape)
    every = lax.all_to_all(every, "orb", split_axis=0, concat_axis=0, tiled=True)

    *tb, x = lax.optimization_barrier((*block_pairs(pos, perm, x), x))
    tb = [tb[0]] + [lax.ppermute(tb[k], "aux", pairs_of(k)) for k in range(1, 8)]
    every, tb[1], tb[2], tb[6], ta = lax.optimization_barrier((every, tb[1], tb[2], tb[6], row_slabs(x)))
    ta = lax.all_to_all(ta, "orb", split_axis=0, concat_axis=0, tiled=True)

    marks = every[:, 2 * W, :128]
    meta = marks.astype(jnp.int32).reshape(-1)
    pat = jnp.stack([marks, lax.ppermute(marks, "aux", pairs_of(1))])
    pat = jnp.stack([pat] + [lax.ppermute(pat, "aux", pairs_of(2 * dx)) for dx in range(1, 4)])
    pat = pat[..., :32].astype(jnp.int32).reshape(-1)
    blocks = every[:, : 2 * W].reshape(NOB, 2 * W, BS, BS)
    v, w = greens(pos, atom_size, meta, blocks, rows, cols)

    first = first_products(pos, pat, perm, w, tb)
    first = lax.all_to_all(first, "orb", split_axis=0, concat_axis=0, tiled=True)
    us = second_products(pos, meta, perm, ta.reshape(160, W, NOB, 256), v)
    us = [us[0]] + [lax.ppermute(us[k], "aux", pairs_of(k)) for k in range(1, 8)]

    parts = []
    for half in range(2):
        theirs, mine = chi_share(half, pos, first, us)
        parts.append(mine + lax.ppermute(theirs, "aux", pairs_of(1)).astype(F32))
    part = jnp.concatenate(parts, axis=2).astype(BF)
    part = lax.all_to_all(part, "orb", split_axis=0, concat_axis=0, tiled=True)
    part = jnp.sum(part.astype(F32), axis=0)
    x = a // 2
    part = lax.dynamic_slice(
        jnp.concatenate([part, part], axis=1), (0, lax.rem(4 - x, 4) * 320), (40, 1280)
    ).reshape(4, NPD, 1280)
    total = lax.dynamic_index_in_dim(part, x, 0, keepdims=False)
    for dx in range(1, 4):
        piece = lax.dynamic_index_in_dim(part, lax.rem(x + dx, 4), 0, keepdims=False)
        total = total + lax.ppermute(piece, "aux", pairs_of(2 * dx))
    return total


def solution(mesh):
    return jax.shard_map(
        body,
        mesh=mesh,
        in_specs=(
            P(("aux", "orb"), None, None, None),
            P(),
            P("aux", "orb", None),
            P("orb", None, None),
            P("orb", None, None),
            P("orb", None),
        ),
        out_specs=P(("aux", "orb"), None),
        check_vma=False,
    )
```

```python
import functools

import jax
import jax.numpy as jnp
import numpy as np
from jax import lax
from jax.experimental import pallas as pl
from jax.experimental.pallas import tpu as pltpu
from jax.sharding import PartitionSpec as P

BS = 64
R = 1
W = 3
ABS = 16
NOB = 16
NPD = 10
NG = 10
BF = jnp.bfloat16
F32 = jnp.float32
VLIM = 56 * 1024 * 1024

STEPS = [(k // 2, k % 2) for k in range(8)]


def pairs_of(k):
    dx, dc = STEPS[k]
    return [(i, ((i // 2 + dx) % 4) * 2 + ((i % 2) ^ dc)) for i in range(8)]


def dest_of(a, k):
    dx, dc = STEPS[k]
    return lax.rem(a // 2 + dx, 4) * 2 + (lax.rem(a, 2) if dc == 0 else 1 - lax.rem(a, 2))


def src_of(a, k):
    dx, dc = STEPS[k]
    return lax.rem(a // 2 + 4 - dx, 4) * 2 + (lax.rem(a, 2) if dc == 0 else 1 - lax.rem(a, 2))


def swap16():
    r = np.arange(256)
    m = np.zeros((256, 256), np.float32)
    m[r, (r % 16) * 16 + r // 16] = 1.0
    return jnp.asarray(m, BF)


def vspec():
    return pl.BlockSpec(memory_space=pltpu.VMEM)


def sspec():
    return pl.BlockSpec(memory_space=pltpu.SMEM)


def rows_kernel(x_ref, ta_ref):
    for p in range(2):
        for d in range(W):
            for o in range(16):
                ta_ref[o, p * W + d] = x_ref[p, d, :, 256 * o : 256 * o + 256]


def row_slabs(x):
    return pl.pallas_call(
        rows_kernel,
        grid=(NPD // 2,),
        in_specs=[pl.BlockSpec((2, W, NOB, 4096), lambda i: (i, 0, 0, 0))],
        out_specs=pl.BlockSpec((16, 2 * W, NOB, 256), lambda i: (0, i, 0, 0)),
        out_shape=jax.ShapeDtypeStruct((16, NPD * W, NOB, 256), BF),
        compiler_params=pltpu.CompilerParams(vmem_limit_bytes=VLIM),
        cost_estimate=pl.CostEstimate(flops=0, bytes_accessed=8 * 10**6, transcendentals=0),
        name="row_slabs",
    )(x)


def pairs_kernel(pos, perm, x_ref, *rest):
    tb, s = rest[:8], rest[8]
    a = pos[0]
    for p in range(2):
        for d in range(W):
            x = x_ref[p, d]
            halves = [
                jnp.concatenate([x[:, 128 * (16 * h + c) : 128 * (16 * h + c) + 128] for c in range(16)], axis=0)
                for h in range(2)
            ]
            y = jnp.dot(perm[...], jnp.concatenate(halves, axis=1), preferred_element_type=F32).astype(BF)
            for n in range(NOB):
                part = y[16 * n : 16 * n + 16]
                for h in range(2):
                    s[n, d, p, 16 * h : 16 * h + 16] = part[:, 128 * h : 128 * h + 128]
    for k in range(8):
        t = dest_of(a, k)
        for i in range(2):
            tb[k][i] = s[2 * t + i]


def block_pairs(pos, perm, x):
    return pl.pallas_call(
        pairs_kernel,
        grid=(NPD // 2,),
        in_specs=[
            sspec(),
            pl.BlockSpec((256, 256), lambda i: (0, 0)),
            pl.BlockSpec((2, W, NOB, 4096), lambda i: (i, 0, 0, 0)),
        ],
        out_specs=[pl.BlockSpec((2, W, 2, 32, 128), lambda i: (0, 0, i, 0, 0))] * 8,
        out_shape=[jax.ShapeDtypeStruct((2, W, NPD, 32, 128), BF)] * 8,
        scratch_shapes=[pltpu.VMEM((NOB, W, 2, 32, 128), BF)],
        compiler_params=pltpu.CompilerParams(vmem_limit_bytes=VLIM),
        cost_estimate=pl.CostEstimate(flops=10**9, bytes_accessed=8 * 10**6, transcendentals=0),
        name="block_pairs",
    )(pos, perm, x)


def greens_kernel(pos, size, meta, g_ref, rows_ref, cols_ref, v_ref, w_ref, o_ref):
    a = pos[0]
    row = lax.broadcasted_iota(jnp.int32, (BS, BS), 0)
    col = lax.broadcasted_iota(jnp.int32, (BS, BS), 1)

    def one(n, carry):
        for d in range(W):
            m = n + d - R
            ok = (m >= 0) & (m < NOB)
            if d != R:
                ok = ok & (meta[n * 128 + NG * W + d] > 0)
            rows_in = jnp.where(ok, size[jnp.clip(m, 0, NOB - 1)], 0)
            mask = (row < rows_in) & (col < size[n])
            occ = jnp.where(mask, g_ref[n, d], jnp.zeros((BS, BS), BF))
            v = jnp.where(mask, g_ref[n, W + d], jnp.zeros((BS, BS), BF))
            for g in range(2):
                t = jnp.dot(rows_ref[g], occ, preferred_element_type=F32).astype(BF)
                o_ref[n, d, 32 * g : 32 * g + 32] = jnp.dot(
                    t, cols_ref[g], preferred_element_type=F32
                ).astype(BF)
            v_ref[n, d] = jnp.concatenate([v, v], axis=1)
        return carry

    lax.fori_loop(0, NOB, one, 0)
    z = jnp.zeros((32, 64), BF)
    for i in range(2):
        for g in range(2):
            for e in range(W):
                cols = []
                for d in range(W):
                    f = e - d + 1
                    if f < 0 or f >= W:
                        cols.append(z)
                        continue
                    m = 2 * a + i + d - 1
                    ok = (m >= 0) & (m < NOB)
                    mc = jnp.clip(m, 0, NOB - 1)
                    v = o_ref[mc, f, 32 * g : 32 * g + 32]
                    cols.append(jnp.where(ok, v, z))
                row = (g * W + e) * 32
                w_ref[i, row : row + 32, :] = jnp.concatenate(cols, axis=1)


def greens(pos, size, meta, g, rows, cols):
    return pl.pallas_call(
        greens_kernel,
        in_specs=[sspec()] * 3 + [vspec()] * 3,
        out_specs=[vspec(), vspec()],
        scratch_shapes=[pltpu.VMEM((NOB, W, 64, 64), BF)],
        out_shape=[
            jax.ShapeDtypeStruct((NOB, W, BS, 128), BF),
            jax.ShapeDtypeStruct((2, 192, 192), BF),
        ],
        compiler_params=pltpu.CompilerParams(vmem_limit_bytes=VLIM),
        cost_estimate=pl.CostEstimate(flops=10**6, bytes_accessed=8 * 10**6, transcendentals=0),
        name="greens",
    )(pos, size, meta, g, rows, cols)


def second_kernel(pos, pat, perm, ta_ref, v_ref, *rest):
    outs, s, kb = rest[:8], rest[8], rest[9]
    a = pos[0]
    low = lax.broadcasted_iota(jnp.int32, (BS, 128), 1) < 64
    zero = jnp.zeros((BS, 128), BF)
    kb[...] = jnp.zeros(kb.shape, BF)
    s[0] = jnp.zeros(s.shape[1:], BF)
    s[NOB + 1] = jnp.zeros(s.shape[1:], BF)

    def regroup(g, carry):
        for d in range(W):
            x = ta_ref[pl.ds(16 * g, 16), d].reshape(256, 256)
            y = jnp.dot(perm[...], x, preferred_element_type=F32).astype(BF)
            for n in range(NOB):
                keep = pat[n * 128 + g * W + d] > 0
                part = y[16 * n : 16 * n + 16]
                s[n + 1, d, pl.ds(pl.multiple_of(16 * g, 16), 16)] = jnp.where(
                    keep, part, jnp.zeros_like(part)
                )
        return carry

    lax.fori_loop(0, NG, regroup, 0)
    for k in range(8):
        t = dest_of(a, k)

        def one(i, carry, k=k, t=t):
            n = 2 * t + i
            for d in range(W):
                v = v_ref[n, d]
                lo, hi = jnp.where(low, v, zero), jnp.where(low, zero, v)
                for q in range(4):
                    row, col = 256 * d + 64 * q, 128 * (q // 2)
                    kb[row : row + 64, col : col + 128] = hi if q % 2 else lo
            for e in range(W):
                ds = [d for d in range(W) if 0 <= e - d + 1 < W]
                lhs = jnp.concatenate([s[n + d, e - d + 1] for d in ds], axis=1)
                rhs = kb[256 * ds[0] : 256 * ds[-1] + 256]
                outs[k][i * W + e] = jnp.dot(lhs, rhs, preferred_element_type=F32).astype(BF)
            return carry

        lax.fori_loop(0, 2, one, 0)


def second_products(pos, pat, perm, ta, v):
    return pl.pallas_call(
        second_kernel,
        in_specs=[sspec(), sspec(), vspec(), vspec(), vspec()],
        out_specs=[vspec()] * 8,
        out_shape=[jax.ShapeDtypeStruct((2 * W, 160, 256), BF)] * 8,
        scratch_shapes=[pltpu.VMEM((NOB + 2, W, 160, 256), BF), pltpu.VMEM((256 * W, 256), BF)],
        compiler_params=pltpu.CompilerParams(vmem_limit_bytes=VLIM),
        cost_estimate=pl.CostEstimate(flops=4 * 10**9, bytes_accessed=15 * 10**6, transcendentals=0),
        name="second",
    )(pos, pat, perm, ta, v)


def first_kernel(pos, pat, perm, w_ref, *rest):
    tb, out, s = rest[:8], rest[8], rest[9]
    a, o = pos[0], pos[1]
    lane = lax.broadcasted_iota(jnp.int32, (96, NPD * 128), 1)
    low = lax.rem(lane, 128) < 64
    for k in range(8):
        src = src_of(a, k)
        base = lax.rem(src, 2) * 40 + (src // 2) * 10

        def one(i, carry, k=k, base=base):
            n = 2 * a + i
            columns = []
            for p in range(NPD):
                rows = []
                for d in range(W):
                    keep = pat[(k * NOB + n) * 32 + lax.div(o * NPD + p, ABS) * W + d] > 0
                    x = tb[k][i, d, p]
                    x = jnp.where(keep, x, jnp.zeros_like(x))
                    rows.append(x)
                    rows.append(jnp.concatenate([x[:, 64:], x[:, :64]], axis=1))
                columns.append(jnp.concatenate(rows, axis=0))
            y = jnp.dot(w_ref[i], jnp.concatenate(columns, axis=1), preferred_element_type=F32)
            y = jnp.where(low, y[:96], y[96:]).astype(BF)
            for p in range(NPD):
                s[i, base + p] = y[:, 128 * p : 128 * p + 128]
            return carry

        lax.fori_loop(0, 2, one, 0)

    def regroup(j, carry):
        i = j // 5
        g = lax.rem(j, 5)
        tiles = s[i, pl.ds(16 * g, 16)]
        for e in range(W):
            x = jnp.concatenate(
                [tiles[:, 32 * e + 16 * h : 32 * e + 16 * h + 16].reshape(256, 128) for h in range(2)], axis=1
            )
            y = jnp.dot(perm[...], x, preferred_element_type=F32).astype(BF)
            for h in range(2):
                for q in range(16):
                    qq = 16 * h + q
                    out[qq // 2, i * W + e, pl.ds(pl.multiple_of(16 * g, 16), 16),
                        128 * (qq % 2) : 128 * (qq % 2) + 128] = y[16 * q : 16 * q + 16, 128 * h : 128 * h + 128]
        return carry

    lax.fori_loop(0, 10, regroup, 0)


def first_products(pos, pat, perm, w, tb):
    return pl.pallas_call(
        first_kernel,
        in_specs=[sspec(), sspec(), vspec(), vspec()] + [vspec()] * 8,
        out_specs=vspec(),
        out_shape=jax.ShapeDtypeStruct((16, 2 * W, 80, 256), BF),
        scratch_shapes=[pltpu.VMEM((2, 80, 96, 128), BF)],
        compiler_params=pltpu.CompilerParams(vmem_limit_bytes=VLIM),
        cost_estimate=pl.CostEstimate(flops=3 * 10**9, bytes_accessed=8 * 10**6, transcendentals=0),
        name="first",
    )(pos, pat, perm, w, *tb)


def chi_kernel(pos, first_ref, *rest):
    us, theirs, mine, rhs = rest[:8], rest[8], rest[9], rest[10]
    a = pos[0]
    core0 = lax.rem(a, 2) == 0
    t = pl.program_id(0)

    @pl.when(t == 0)
    def _():
        for k in range(8):
            row = pl.multiple_of(src_of(a, k) * 160, 32)
            for kk in range(6):
                rhs[pl.ds(row, 160), 256 * kk : 256 * kk + 256] = us[k][kk]

    lhs = jnp.concatenate([first_ref[:, kk].reshape(1280, 256) for kk in range(6)], axis=1)
    r = lax.dot_general(
        lhs,
        rhs[pl.ds(pl.multiple_of(256 * t, 256), 256)],
        (((1,), (1,)), ((), ())),
        preferred_element_type=F32,
    )
    for b in range(16):
        lo, hi = r[80 * b : 80 * b + 40], r[80 * b + 40 : 80 * b + 80]
        mine[b] = jnp.where(core0, lo, hi)
        theirs[b] = jnp.where(core0, hi, lo).astype(BF)


def chi_share(pos, first, us):
    return pl.pallas_call(
        chi_kernel,
        grid=(5,),
        in_specs=[sspec(), vspec()] + [vspec()] * 8,
        out_specs=[pl.BlockSpec((16, 40, 256), lambda t: (0, 0, t))] * 2,
        out_shape=[jax.ShapeDtypeStruct((16, 40, 1280), BF), jax.ShapeDtypeStruct((16, 40, 1280), F32)],
        scratch_shapes=[pltpu.VMEM((1280, 1536), BF)],
        compiler_params=pltpu.CompilerParams(vmem_limit_bytes=VLIM),
        cost_estimate=pl.CostEstimate(flops=5 * 10**9, bytes_accessed=13 * 10**6, transcendentals=0),
        name="chi",
    )(pos, first, *us)


def deinterleave():
    rows = np.zeros((2, 32, 64), np.float32)
    cols = np.zeros((2, 64, 64), np.float32)
    for g in range(2):
        for q in range(32):
            rows[g, q, 2 * q + g] = 1.0
        for j in range(2):
            for c in range(32):
                cols[g, 2 * c + (g ^ j), 32 * j + c] = 1.0
    return jnp.asarray(rows, BF), jnp.asarray(cols, BF)


def body(three_center, atom_size, tensor_pattern, green_occ, green_virt, green_pattern):
    a, o = lax.axis_index("aux"), lax.axis_index("orb")
    pos = jnp.stack([a, o]).astype(jnp.int32)
    perm = swap16()
    rows, cols = deinterleave()
    x = three_center.transpose(0, 2, 1, 3)

    marks = jnp.concatenate([tensor_pattern.reshape(1, NG * W), green_pattern], axis=1).astype(BF)
    marks = jnp.pad(marks, ((0, 1), (0, 4096 - NG * W - W)))
    own = jnp.concatenate([green_occ[0], green_virt[0], marks], axis=0)
    every = jnp.broadcast_to(own[None], (NOB,) + own.shape)
    every = lax.all_to_all(every, "orb", split_axis=0, concat_axis=0, tiled=True)

    *tb, x = lax.optimization_barrier((*block_pairs(pos, perm, x), x))
    tb = [tb[0]] + [lax.ppermute(tb[k], "aux", pairs_of(k)) for k in range(1, 8)]
    every, tb[1], tb[2], tb[6], ta = lax.optimization_barrier((every, tb[1], tb[2], tb[6], row_slabs(x)))
    ta = lax.all_to_all(ta, "orb", split_axis=0, concat_axis=0, tiled=True)

    marks = every[:, 2 * W, :128]
    meta = marks.astype(jnp.int32).reshape(-1)
    blocks = every[:, : 2 * W].reshape(NOB, 2 * W, BS, BS)
    v, w, marks = lax.optimization_barrier((*greens(pos, atom_size, meta, blocks, rows, cols), marks))
    pat = jnp.stack([marks, lax.ppermute(marks, "aux", pairs_of(1))])
    pat = jnp.stack([pat] + [lax.ppermute(pat, "aux", pairs_of(2 * dx)) for dx in range(1, 4)])
    pat = pat[..., :32].astype(jnp.int32).reshape(-1)

    first = first_products(pos, pat, perm, w, tb)
    first = lax.all_to_all(first, "orb", split_axis=0, concat_axis=0, tiled=True)
    us = second_products(pos, meta, perm, ta.reshape(160, W, NOB, 256), v)
    us = [us[0]] + [lax.ppermute(us[k], "aux", pairs_of(k)) for k in range(1, 8)]

    theirs, mine = chi_share(pos, first, us)
    part = (mine + lax.ppermute(theirs, "aux", pairs_of(1)).astype(F32)).astype(BF)
    part = lax.all_to_all(part, "orb", split_axis=0, concat_axis=0, tiled=True)
    part = jnp.sum(part.astype(F32), axis=0).reshape(4, NPD, 1280)
    x = a // 2
    total = lax.dynamic_index_in_dim(part, x, 0, keepdims=False)
    for dx in range(1, 4):
        piece = lax.dynamic_index_in_dim(part, lax.rem(x + dx, 4), 0, keepdims=False)
        total = total + lax.ppermute(piece, "aux", pairs_of(2 * dx))
    return total


def solution(mesh):
    return jax.shard_map(
        body,
        mesh=mesh,
        in_specs=(
            P(("aux", "orb"), None, None, None),
            P(),
            P("aux", "orb", None),
            P("orb", None, None),
            P("orb", None, None),
            P("orb", None),
        ),
        out_specs=P(("aux", "orb"), None),
        check_vma=False,
    )
```

```python
import functools

import jax
import jax.numpy as jnp
import numpy as np
from jax import lax
from jax.experimental import pallas as pl
from jax.experimental.pallas import tpu as pltpu
from jax.sharding import PartitionSpec as P

BS = 64
R = 1
W = 3
ABS = 16
NOB = 16
NPD = 10
NG = 10
BF = jnp.bfloat16
F32 = jnp.float32
VLIM = 24 * 1024 * 1024

STEPS = [(k // 2, k % 2) for k in range(8)]


def pairs_of(k):
    dx, dc = STEPS[k]
    return [(i, ((i // 2 + dx) % 4) * 2 + ((i % 2) ^ dc)) for i in range(8)]


def dest_of(a, k):
    dx, dc = STEPS[k]
    return lax.rem(a // 2 + dx, 4) * 2 + (lax.rem(a, 2) if dc == 0 else 1 - lax.rem(a, 2))


def src_of(a, k):
    dx, dc = STEPS[k]
    return lax.rem(a // 2 + 4 - dx, 4) * 2 + (lax.rem(a, 2) if dc == 0 else 1 - lax.rem(a, 2))


def swap16():
    r = np.arange(256)
    m = np.zeros((256, 256), np.float32)
    m[r, (r % 16) * 16 + r // 16] = 1.0
    return jnp.asarray(m, BF)


def vspec():
    return pl.BlockSpec(memory_space=pltpu.VMEM)


def sspec():
    return pl.BlockSpec(memory_space=pltpu.SMEM)


def rows_kernel(x_ref, ta_ref):
    for p in range(2):
        for d in range(W):
            for o in range(16):
                ta_ref[o, p * W + d] = x_ref[p, d, :, 256 * o : 256 * o + 256]


def row_slabs(x):
    return pl.pallas_call(
        rows_kernel,
        grid=(NPD // 2,),
        in_specs=[pl.BlockSpec((2, W, NOB, 4096), lambda i: (i, 0, 0, 0))],
        out_specs=pl.BlockSpec((16, 2 * W, NOB, 256), lambda i: (0, i, 0, 0)),
        out_shape=jax.ShapeDtypeStruct((16, NPD * W, NOB, 256), BF),
        compiler_params=pltpu.CompilerParams(vmem_limit_bytes=VLIM),
        cost_estimate=pl.CostEstimate(flops=0, bytes_accessed=8 * 10**6, transcendentals=0),
        name="row_slabs",
    )(x)


def pairs_kernel(pos, perm, x_ref, *rest):
    tb, s = rest[:8], rest[8]
    a = pos[0]
    for p in range(2):
        for d in range(W):
            x = x_ref[p, d]
            halves = [
                jnp.concatenate([x[:, 128 * (16 * h + c) : 128 * (16 * h + c) + 128] for c in range(16)], axis=0)
                for h in range(2)
            ]
            y = jnp.dot(perm[...], jnp.concatenate(halves, axis=1), preferred_element_type=F32).astype(BF)
            for n in range(NOB):
                part = y[16 * n : 16 * n + 16]
                for h in range(2):
                    s[n, d, p, 16 * h : 16 * h + 16] = part[:, 128 * h : 128 * h + 128]
    for k in range(8):
        t = dest_of(a, k)
        for i in range(2):
            tb[k][i] = s[2 * t + i]


def block_pairs(pos, perm, x):
    return pl.pallas_call(
        pairs_kernel,
        grid=(NPD // 2,),
        in_specs=[
            sspec(),
            pl.BlockSpec((256, 256), lambda i: (0, 0)),
            pl.BlockSpec((2, W, NOB, 4096), lambda i: (i, 0, 0, 0)),
        ],
        out_specs=[pl.BlockSpec((2, W, 2, 32, 128), lambda i: (0, 0, i, 0, 0))] * 8,
        out_shape=[jax.ShapeDtypeStruct((2, W, NPD, 32, 128), BF)] * 8,
        scratch_shapes=[pltpu.VMEM((NOB, W, 2, 32, 128), BF)],
        compiler_params=pltpu.CompilerParams(vmem_limit_bytes=VLIM),
        cost_estimate=pl.CostEstimate(flops=10**9, bytes_accessed=8 * 10**6, transcendentals=0),
        name="block_pairs",
    )(pos, perm, x)


def greens_kernel(pos, size, meta, g_ref, rows_ref, cols_ref, v_ref, w_ref, o_ref):
    a = pos[0]
    row = lax.broadcasted_iota(jnp.int32, (BS, BS), 0)
    col = lax.broadcasted_iota(jnp.int32, (BS, BS), 1)

    def one(n, carry):
        for d in range(W):
            m = n + d - R
            ok = (m >= 0) & (m < NOB)
            if d != R:
                ok = ok & (meta[n * 128 + NG * W + d] > 0)
            rows_in = jnp.where(ok, size[jnp.clip(m, 0, NOB - 1)], 0)
            mask = (row < rows_in) & (col < size[n])
            occ = jnp.where(mask, g_ref[n, d], jnp.zeros((BS, BS), BF))
            v = jnp.where(mask, g_ref[n, W + d], jnp.zeros((BS, BS), BF))
            for g in range(2):
                t = jnp.dot(rows_ref[g], occ, preferred_element_type=F32).astype(BF)
                o_ref[n, d, 32 * g : 32 * g + 32] = jnp.dot(
                    t, cols_ref[g], preferred_element_type=F32
                ).astype(BF)
            v_ref[n, d] = jnp.concatenate([v, v], axis=1)
        return carry

    lax.fori_loop(0, NOB, one, 0)
    z = jnp.zeros((32, 64), BF)
    for i in range(2):
        for g in range(2):
            for e in range(W):
                cols = []
                for d in range(W):
                    f = e - d + 1
                    if f < 0 or f >= W:
                        cols.append(z)
                        continue
                    m = 2 * a + i + d - 1
                    ok = (m >= 0) & (m < NOB)
                    mc = jnp.clip(m, 0, NOB - 1)
                    v = o_ref[mc, f, 32 * g : 32 * g + 32]
                    cols.append(jnp.where(ok, v, z))
                row = (g * W + e) * 32
                w_ref[i, row : row + 32, :] = jnp.concatenate(cols, axis=1)


def greens(pos, size, meta, g, rows, cols):
    return pl.pallas_call(
        greens_kernel,
        in_specs=[sspec()] * 3 + [vspec()] * 3,
        out_specs=[vspec(), vspec()],
        scratch_shapes=[pltpu.VMEM((NOB, W, 64, 64), BF)],
        out_shape=[
            jax.ShapeDtypeStruct((NOB, W, BS, 128), BF),
            jax.ShapeDtypeStruct((2, 192, 192), BF),
        ],
        compiler_params=pltpu.CompilerParams(vmem_limit_bytes=VLIM),
        cost_estimate=pl.CostEstimate(flops=10**6, bytes_accessed=8 * 10**6, transcendentals=0),
        name="greens",
    )(pos, size, meta, g, rows, cols)


def second_kernel(pos, pat, perm, ta_ref, v_ref, *rest):
    outs, s, kb = rest[:8], rest[8], rest[9]
    a = pos[0]
    low = lax.broadcasted_iota(jnp.int32, (BS, 128), 1) < 64
    zero = jnp.zeros((BS, 128), BF)
    kb[...] = jnp.zeros(kb.shape, BF)
    s[0] = jnp.zeros(s.shape[1:], BF)
    s[NOB + 1] = jnp.zeros(s.shape[1:], BF)

    def regroup(g, carry):
        for d in range(W):
            x = ta_ref[pl.ds(16 * g, 16), d].reshape(256, 256)
            y = jnp.dot(perm[...], x, preferred_element_type=F32).astype(BF)
            for n in range(NOB):
                keep = pat[n * 128 + g * W + d] > 0
                part = y[16 * n : 16 * n + 16]
                s[n + 1, d, pl.ds(pl.multiple_of(16 * g, 16), 16)] = jnp.where(
                    keep, part, jnp.zeros_like(part)
                )
        return carry

    lax.fori_loop(0, NG, regroup, 0)
    for k in range(8):
        t = dest_of(a, k)

        def one(i, carry, k=k, t=t):
            n = 2 * t + i
            for d in range(W):
                v = v_ref[n, d]
                lo, hi = jnp.where(low, v, zero), jnp.where(low, zero, v)
                for q in range(4):
                    row, col = 256 * d + 64 * q, 128 * (q // 2)
                    kb[row : row + 64, col : col + 128] = hi if q % 2 else lo
            for e in range(W):
                ds = [d for d in range(W) if 0 <= e - d + 1 < W]
                lhs = jnp.concatenate([s[n + d, e - d + 1] for d in ds], axis=1)
                rhs = kb[256 * ds[0] : 256 * ds[-1] + 256]
                outs[k][i * W + e] = jnp.dot(lhs, rhs, preferred_element_type=F32).astype(BF)
            return carry

        lax.fori_loop(0, 2, one, 0)


def second_products(pos, pat, perm, ta, v):
    return pl.pallas_call(
        second_kernel,
        in_specs=[sspec(), sspec(), vspec(), vspec(), vspec()],
        out_specs=[vspec()] * 8,
        out_shape=[jax.ShapeDtypeStruct((2 * W, 160, 256), BF)] * 8,
        scratch_shapes=[pltpu.VMEM((NOB + 2, W, 160, 256), BF), pltpu.VMEM((256 * W, 256), BF)],
        compiler_params=pltpu.CompilerParams(vmem_limit_bytes=VLIM),
        cost_estimate=pl.CostEstimate(flops=4 * 10**9, bytes_accessed=15 * 10**6, transcendentals=0),
        name="second",
    )(pos, pat, perm, ta, v)


def first_kernel(pos, pat, perm, w_ref, *rest):
    tb, out, s = rest[:8], rest[8], rest[9]
    a, o = pos[0], pos[1]
    lane = lax.broadcasted_iota(jnp.int32, (96, NPD * 128), 1)
    low = lax.rem(lane, 128) < 64
    for k in range(8):
        src = src_of(a, k)
        base = lax.rem(src, 2) * 40 + (src // 2) * 10

        def one(i, carry, k=k, base=base):
            n = 2 * a + i
            columns = []
            for p in range(NPD):
                rows = []
                for d in range(W):
                    keep = pat[(k * NOB + n) * 32 + lax.div(o * NPD + p, ABS) * W + d] > 0
                    x = tb[k][i, d, p]
                    x = jnp.where(keep, x, jnp.zeros_like(x))
                    rows.append(x)
                    rows.append(jnp.concatenate([x[:, 64:], x[:, :64]], axis=1))
                columns.append(jnp.concatenate(rows, axis=0))
            y = jnp.dot(w_ref[i], jnp.concatenate(columns, axis=1), preferred_element_type=F32)
            y = jnp.where(low, y[:96], y[96:]).astype(BF)
            for p in range(NPD):
                s[i, base + p] = y[:, 128 * p : 128 * p + 128]
            return carry

        lax.fori_loop(0, 2, one, 0)

    def regroup(j, carry):
        i = j // 5
        g = lax.rem(j, 5)
        tiles = s[i, pl.ds(16 * g, 16)]
        for e in range(W):
            x = jnp.concatenate(
                [tiles[:, 32 * e + 16 * h : 32 * e + 16 * h + 16].reshape(256, 128) for h in range(2)], axis=1
            )
            y = jnp.dot(perm[...], x, preferred_element_type=F32).astype(BF)
            for h in range(2):
                for q in range(16):
                    qq = 16 * h + q
                    out[qq // 2, i * W + e, pl.ds(pl.multiple_of(16 * g, 16), 16),
                        128 * (qq % 2) : 128 * (qq % 2) + 128] = y[16 * q : 16 * q + 16, 128 * h : 128 * h + 128]
        return carry

    lax.fori_loop(0, 10, regroup, 0)


def first_products(pos, pat, perm, w, tb):
    return pl.pallas_call(
        first_kernel,
        in_specs=[sspec(), sspec(), vspec(), vspec()] + [vspec()] * 8,
        out_specs=vspec(),
        out_shape=jax.ShapeDtypeStruct((16, 2 * W, 80, 256), BF),
        scratch_shapes=[pltpu.VMEM((2, 80, 96, 128), BF)],
        compiler_params=pltpu.CompilerParams(vmem_limit_bytes=VLIM),
        cost_estimate=pl.CostEstimate(flops=3 * 10**9, bytes_accessed=8 * 10**6, transcendentals=0),
        name="first",
    )(pos, pat, perm, w, *tb)


def chi_kernel(pos, first_ref, *rest):
    us, theirs, mine, rhs = rest[:8], rest[8], rest[9], rest[10]
    a = pos[0]
    core0 = lax.rem(a, 2) == 0
    t = pl.program_id(0)

    @pl.when(t == 0)
    def _():
        for k in range(8):
            row = pl.multiple_of(src_of(a, k) * 160, 32)
            for kk in range(6):
                rhs[pl.ds(row, 160), 256 * kk : 256 * kk + 256] = us[k][kk]

    lhs = jnp.concatenate([first_ref[:, kk].reshape(1280, 256) for kk in range(6)], axis=1)
    r = lax.dot_general(
        lhs,
        rhs[pl.ds(pl.multiple_of(256 * t, 256), 256)],
        (((1,), (1,)), ((), ())),
        preferred_element_type=F32,
    )
    for b in range(16):
        lo, hi = r[80 * b : 80 * b + 40], r[80 * b + 40 : 80 * b + 80]
        mine[b] = jnp.where(core0, lo, hi)
        theirs[b] = jnp.where(core0, hi, lo).astype(BF)


def chi_share(pos, first, us):
    return pl.pallas_call(
        chi_kernel,
        grid=(5,),
        in_specs=[sspec(), vspec()] + [vspec()] * 8,
        out_specs=[pl.BlockSpec((16, 40, 256), lambda t: (0, 0, t))] * 2,
        out_shape=[jax.ShapeDtypeStruct((16, 40, 1280), BF), jax.ShapeDtypeStruct((16, 40, 1280), F32)],
        scratch_shapes=[pltpu.VMEM((1280, 1536), BF)],
        compiler_params=pltpu.CompilerParams(vmem_limit_bytes=VLIM),
        cost_estimate=pl.CostEstimate(flops=5 * 10**9, bytes_accessed=13 * 10**6, transcendentals=0),
        name="chi",
    )(pos, first, *us)


def deinterleave():
    rows = np.zeros((2, 32, 64), np.float32)
    cols = np.zeros((2, 64, 64), np.float32)
    for g in range(2):
        for q in range(32):
            rows[g, q, 2 * q + g] = 1.0
        for j in range(2):
            for c in range(32):
                cols[g, 2 * c + (g ^ j), 32 * j + c] = 1.0
    return jnp.asarray(rows, BF), jnp.asarray(cols, BF)


def body(three_center, atom_size, tensor_pattern, green_occ, green_virt, green_pattern):
    a, o = lax.axis_index("aux"), lax.axis_index("orb")
    pos = jnp.stack([a, o]).astype(jnp.int32)
    perm = swap16()
    rows, cols = deinterleave()
    x = three_center.transpose(0, 2, 1, 3)

    marks = jnp.concatenate([tensor_pattern.reshape(1, NG * W), green_pattern], axis=1).astype(BF)
    marks = jnp.pad(marks, ((0, 1), (0, 4096 - NG * W - W)))
    own = jnp.concatenate([green_occ[0], green_virt[0], marks], axis=0)
    every = jnp.broadcast_to(own[None], (NOB,) + own.shape)
    every = lax.all_to_all(every, "orb", split_axis=0, concat_axis=0, tiled=True)

    *tb, x = lax.optimization_barrier((*block_pairs(pos, perm, x), x))
    tb = [tb[0]] + [lax.ppermute(tb[k], "aux", pairs_of(k)) for k in range(1, 8)]
    every, ta = lax.optimization_barrier((every, row_slabs(x)))
    marks = every[:, 2 * W, :128]
    pat = jnp.stack([marks, lax.ppermute(marks, "aux", pairs_of(1))])
    pat = jnp.stack([pat] + [lax.ppermute(pat, "aux", pairs_of(2 * dx)) for dx in range(1, 4)])
    every, pat, tb[1], tb[2], tb[6], ta = lax.optimization_barrier(
        (every, pat, tb[1], tb[2], tb[6], ta)
    )
    ta = lax.all_to_all(ta, "orb", split_axis=0, concat_axis=0, tiled=True)
    pat = pat[..., :32].astype(jnp.int32).reshape(-1)
    meta = every[:, 2 * W, :128].astype(jnp.int32).reshape(-1)
    blocks = every[:, : 2 * W].reshape(NOB, 2 * W, BS, BS)
    v, w = greens(pos, atom_size, meta, blocks, rows, cols)

    first = first_products(pos, pat, perm, w, tb)
    first = lax.all_to_all(first, "orb", split_axis=0, concat_axis=0, tiled=True)
    us = second_products(pos, meta, perm, ta.reshape(160, W, NOB, 256), v)
    us = [us[0]] + [lax.ppermute(us[k], "aux", pairs_of(k)) for k in range(1, 8)]

    theirs, mine = chi_share(pos, first, us)
    part = (mine + lax.ppermute(theirs, "aux", pairs_of(1)).astype(F32)).astype(BF)
    part = lax.all_to_all(part, "orb", split_axis=0, concat_axis=0, tiled=True)
    part = jnp.sum(part.astype(F32), axis=0).reshape(4, NPD, 1280)
    x = a // 2
    total = lax.dynamic_index_in_dim(part, x, 0, keepdims=False)
    for dx in range(1, 4):
        piece = lax.dynamic_index_in_dim(part, lax.rem(x + dx, 4), 0, keepdims=False)
        total = total + lax.ppermute(piece, "aux", pairs_of(2 * dx))
    return total


def solution(mesh):
    return jax.shard_map(
        body,
        mesh=mesh,
        in_specs=(
            P(("aux", "orb"), None, None, None),
            P(),
            P("aux", "orb", None),
            P("orb", None, None),
            P("orb", None, None),
            P("orb", None),
        ),
        out_specs=P(("aux", "orb"), None),
        check_vma=False,
    )
```

```python
import functools

import jax
import jax.numpy as jnp
import numpy as np
from jax import lax
from jax.experimental import pallas as pl
from jax.experimental.pallas import tpu as pltpu
from jax.sharding import PartitionSpec as P

BS = 64
R = 1
W = 3
ABS = 16
NOB = 16
NPD = 10
NG = 10
BF = jnp.bfloat16
F32 = jnp.float32
VLIM = 24 * 1024 * 1024

STEPS = [(k // 2, k % 2) for k in range(8)]


TROWS = 2 * W * NPD * 32
CARRIERS = (3, 4, 7)


def pairs_of(k):
    dx, dc = STEPS[k]
    return [(i, ((i // 2 + dx) % 4) * 2 + ((i % 2) ^ dc)) for i in range(8)]


def dest_of(a, k):
    dx, dc = STEPS[k]
    return lax.rem(a // 2 + dx, 4) * 2 + (lax.rem(a, 2) if dc == 0 else 1 - lax.rem(a, 2))


def src_of(a, k):
    dx, dc = STEPS[k]
    return lax.rem(a // 2 + 4 - dx, 4) * 2 + (lax.rem(a, 2) if dc == 0 else 1 - lax.rem(a, 2))


def swap16():
    r = np.arange(256)
    m = np.zeros((256, 256), np.float32)
    m[r, (r % 16) * 16 + r // 16] = 1.0
    return jnp.asarray(m, BF)


def vspec():
    return pl.BlockSpec(memory_space=pltpu.VMEM)


def sspec():
    return pl.BlockSpec(memory_space=pltpu.SMEM)


def rows_kernel(x_ref, ta_ref):
    for p in range(2):
        for d in range(W):
            for o in range(16):
                ta_ref[o, p * W + d] = x_ref[p, d, :, 256 * o : 256 * o + 256]


def row_slabs(x):
    return pl.pallas_call(
        rows_kernel,
        grid=(NPD // 2,),
        in_specs=[pl.BlockSpec((2, W, NOB, 4096), lambda i: (i, 0, 0, 0))],
        out_specs=pl.BlockSpec((16, 2 * W, NOB, 256), lambda i: (0, i, 0, 0)),
        out_shape=jax.ShapeDtypeStruct((16, NPD * W, NOB, 256), BF),
        compiler_params=pltpu.CompilerParams(vmem_limit_bytes=VLIM),
        cost_estimate=pl.CostEstimate(flops=0, bytes_accessed=8 * 10**6, transcendentals=0),
        name="row_slabs",
    )(x)


def pairs_kernel(pos, perm, x_ref, *rest):
    tb, s = rest[:8], rest[8]
    a = pos[0]
    for p in range(2):
        for d in range(W):
            x = x_ref[p, d]
            halves = [
                jnp.concatenate([x[:, 128 * (16 * h + c) : 128 * (16 * h + c) + 128] for c in range(16)], axis=0)
                for h in range(2)
            ]
            y = jnp.dot(perm[...], jnp.concatenate(halves, axis=1), preferred_element_type=F32).astype(BF)
            for n in range(NOB):
                part = y[16 * n : 16 * n + 16]
                for h in range(2):
                    s[n, d, p, 16 * h : 16 * h + 16] = part[:, 128 * h : 128 * h + 128]
    for k in range(8):
        t = dest_of(a, k)
        for i in range(2):
            tb[k][i] = s[2 * t + i]


def block_pairs(pos, perm, x):
    return pl.pallas_call(
        pairs_kernel,
        grid=(NPD // 2,),
        in_specs=[
            sspec(),
            pl.BlockSpec((256, 256), lambda i: (0, 0)),
            pl.BlockSpec((2, W, NOB, 4096), lambda i: (i, 0, 0, 0)),
        ],
        out_specs=[pl.BlockSpec((2, W, 2, 32, 128), lambda i: (0, 0, i, 0, 0))] * 8,
        out_shape=[jax.ShapeDtypeStruct((2, W, NPD, 32, 128), BF)] * 8,
        scratch_shapes=[pltpu.VMEM((NOB, W, 2, 32, 128), BF)],
        compiler_params=pltpu.CompilerParams(vmem_limit_bytes=VLIM),
        cost_estimate=pl.CostEstimate(flops=10**9, bytes_accessed=8 * 10**6, transcendentals=0),
        name="block_pairs",
    )(pos, perm, x)


def greens_kernel(pos, size, meta, g_ref, rows_ref, cols_ref, v_ref, w_ref, o_ref):
    a = pos[0]
    row = lax.broadcasted_iota(jnp.int32, (BS, BS), 0)
    col = lax.broadcasted_iota(jnp.int32, (BS, BS), 1)

    def one(n, carry):
        for d in range(W):
            m = n + d - R
            ok = (m >= 0) & (m < NOB)
            if d != R:
                ok = ok & (meta[n * 128 + NG * W + d] > 0)
            rows_in = jnp.where(ok, size[jnp.clip(m, 0, NOB - 1)], 0)
            mask = (row < rows_in) & (col < size[n])
            occ = jnp.where(mask, g_ref[n, d], jnp.zeros((BS, BS), BF))
            v = jnp.where(mask, g_ref[n, W + d], jnp.zeros((BS, BS), BF))
            for g in range(2):
                t = jnp.dot(rows_ref[g], occ, preferred_element_type=F32).astype(BF)
                o_ref[n, d, 32 * g : 32 * g + 32] = jnp.dot(
                    t, cols_ref[g], preferred_element_type=F32
                ).astype(BF)
            v_ref[n, d] = jnp.concatenate([v, v], axis=1)
        return carry

    lax.fori_loop(0, NOB, one, 0)
    z = jnp.zeros((32, 64), BF)
    for i in range(2):
        for g in range(2):
            for e in range(W):
                cols = []
                for d in range(W):
                    f = e - d + 1
                    if f < 0 or f >= W:
                        cols.append(z)
                        continue
                    m = 2 * a + i + d - 1
                    ok = (m >= 0) & (m < NOB)
                    mc = jnp.clip(m, 0, NOB - 1)
                    v = o_ref[mc, f, 32 * g : 32 * g + 32]
                    cols.append(jnp.where(ok, v, z))
                row = (g * W + e) * 32
                w_ref[i, row : row + 32, :] = jnp.concatenate(cols, axis=1)


def greens(pos, size, meta, g, rows, cols):
    return pl.pallas_call(
        greens_kernel,
        in_specs=[sspec()] * 3 + [vspec()] * 3,
        out_specs=[vspec(), vspec()],
        scratch_shapes=[pltpu.VMEM((NOB, W, 64, 64), BF)],
        out_shape=[
            jax.ShapeDtypeStruct((NOB, W, BS, 128), BF),
            jax.ShapeDtypeStruct((2, 192, 192), BF),
        ],
        compiler_params=pltpu.CompilerParams(vmem_limit_bytes=VLIM),
        cost_estimate=pl.CostEstimate(flops=10**6, bytes_accessed=8 * 10**6, transcendentals=0),
        name="greens",
    )(pos, size, meta, g, rows, cols)


def second_kernel(pos, pat, perm, ta_ref, v_ref, *rest):
    outs, s, kb = rest[:8], rest[8], rest[9]
    a = pos[0]
    low = lax.broadcasted_iota(jnp.int32, (BS, 128), 1) < 64
    zero = jnp.zeros((BS, 128), BF)
    kb[...] = jnp.zeros(kb.shape, BF)
    s[0] = jnp.zeros(s.shape[1:], BF)
    s[NOB + 1] = jnp.zeros(s.shape[1:], BF)

    def regroup(g, carry):
        for d in range(W):
            x = ta_ref[pl.ds(16 * g, 16), d].reshape(256, 256)
            y = jnp.dot(perm[...], x, preferred_element_type=F32).astype(BF)
            for n in range(NOB):
                keep = pat[n * 128 + g * W + d] > 0
                part = y[16 * n : 16 * n + 16]
                s[n + 1, d, pl.ds(pl.multiple_of(16 * g, 16), 16)] = jnp.where(
                    keep, part, jnp.zeros_like(part)
                )
        return carry

    lax.fori_loop(0, NG, regroup, 0)
    for k in range(8):
        t = dest_of(a, k)

        def one(i, carry, k=k, t=t):
            n = 2 * t + i
            for d in range(W):
                v = v_ref[n, d]
                lo, hi = jnp.where(low, v, zero), jnp.where(low, zero, v)
                for q in range(4):
                    row, col = 256 * d + 64 * q, 128 * (q // 2)
                    kb[row : row + 64, col : col + 128] = hi if q % 2 else lo
            for e in range(W):
                ds = [d for d in range(W) if 0 <= e - d + 1 < W]
                lhs = jnp.concatenate([s[n + d, e - d + 1] for d in ds], axis=1)
                rhs = kb[256 * ds[0] : 256 * ds[-1] + 256]
                outs[k][i * W + e] = jnp.dot(lhs, rhs, preferred_element_type=F32).astype(BF)
            return carry

        lax.fori_loop(0, 2, one, 0)


def second_products(pos, pat, perm, ta, v):
    return pl.pallas_call(
        second_kernel,
        in_specs=[sspec(), sspec(), vspec(), vspec(), vspec()],
        out_specs=[vspec()] * 8,
        out_shape=[jax.ShapeDtypeStruct((2 * W, 160, 256), BF)] * 8,
        scratch_shapes=[pltpu.VMEM((NOB + 2, W, 160, 256), BF), pltpu.VMEM((256 * W, 256), BF)],
        compiler_params=pltpu.CompilerParams(vmem_limit_bytes=VLIM),
        cost_estimate=pl.CostEstimate(flops=4 * 10**9, bytes_accessed=15 * 10**6, transcendentals=0),
        name="second",
    )(pos, pat, perm, ta, v)


def first_kernel(pos, pat, perm, w_ref, *rest):
    tb, out, s = rest[:8], rest[8], rest[9]
    a, o = pos[0], pos[1]
    lane = lax.broadcasted_iota(jnp.int32, (96, NPD * 128), 1)
    low = lax.rem(lane, 128) < 64
    for k in range(8):
        src = src_of(a, k)
        base = lax.rem(src, 2) * 40 + (src // 2) * 10

        def one(i, carry, k=k, base=base):
            n = 2 * a + i
            columns = []
            for p in range(NPD):
                rows = []
                for d in range(W):
                    keep = pat[(k * NOB + n) * 32 + lax.div(o * NPD + p, ABS) * W + d] > 0
                    row = pl.multiple_of(((i * W + d) * NPD + p) * 32, 32)
                    x = tb[k][pl.ds(row, 32)]
                    x = jnp.where(keep, x, jnp.zeros_like(x))
                    rows.append(x)
                    rows.append(jnp.concatenate([x[:, 64:], x[:, :64]], axis=1))
                columns.append(jnp.concatenate(rows, axis=0))
            y = jnp.dot(w_ref[i], jnp.concatenate(columns, axis=1), preferred_element_type=F32)
            y = jnp.where(low, y[:96], y[96:]).astype(BF)
            for p in range(NPD):
                s[i, base + p] = y[:, 128 * p : 128 * p + 128]
            return carry

        lax.fori_loop(0, 2, one, 0)

    def regroup(j, carry):
        i = j // 5
        g = lax.rem(j, 5)
        tiles = s[i, pl.ds(16 * g, 16)]
        for e in range(W):
            x = jnp.concatenate(
                [tiles[:, 32 * e + 16 * h : 32 * e + 16 * h + 16].reshape(256, 128) for h in range(2)], axis=1
            )
            y = jnp.dot(perm[...], x, preferred_element_type=F32).astype(BF)
            for h in range(2):
                for q in range(16):
                    qq = 16 * h + q
                    out[qq // 2, i * W + e, pl.ds(pl.multiple_of(16 * g, 16), 16),
                        128 * (qq % 2) : 128 * (qq % 2) + 128] = y[16 * q : 16 * q + 16, 128 * h : 128 * h + 128]
        return carry

    lax.fori_loop(0, 10, regroup, 0)


def first_products(pos, pat, perm, w, tb):
    return pl.pallas_call(
        first_kernel,
        in_specs=[sspec(), sspec(), vspec(), vspec()] + [vspec()] * 8,
        out_specs=vspec(),
        out_shape=jax.ShapeDtypeStruct((16, 2 * W, 80, 256), BF),
        scratch_shapes=[pltpu.VMEM((2, 80, 96, 128), BF)],
        compiler_params=pltpu.CompilerParams(vmem_limit_bytes=VLIM),
        cost_estimate=pl.CostEstimate(flops=3 * 10**9, bytes_accessed=8 * 10**6, transcendentals=0),
        name="first",
    )(pos, pat, perm, w, *tb)


def chi_kernel(pos, first_ref, *rest):
    us, theirs, mine, rhs = rest[:8], rest[8], rest[9], rest[10]
    a = pos[0]
    core0 = lax.rem(a, 2) == 0
    t = pl.program_id(0)

    @pl.when(t == 0)
    def _():
        for k in range(8):
            row = pl.multiple_of(src_of(a, k) * 160, 32)
            for kk in range(6):
                rhs[pl.ds(row, 160), 256 * kk : 256 * kk + 256] = us[k][kk]

    lhs = jnp.concatenate([first_ref[:, kk].reshape(1280, 256) for kk in range(6)], axis=1)
    r = lax.dot_general(
        lhs,
        rhs[pl.ds(pl.multiple_of(256 * t, 256), 256)],
        (((1,), (1,)), ((), ())),
        preferred_element_type=F32,
    )
    for b in range(16):
        lo, hi = r[80 * b : 80 * b + 40], r[80 * b + 40 : 80 * b + 80]
        mine[b] = jnp.where(core0, lo, hi)
        theirs[b] = jnp.where(core0, hi, lo).astype(BF)


def chi_share(pos, first, us):
    return pl.pallas_call(
        chi_kernel,
        grid=(5,),
        in_specs=[sspec(), vspec()] + [vspec()] * 8,
        out_specs=[pl.BlockSpec((16, 40, 256), lambda t: (0, 0, t))] * 2,
        out_shape=[jax.ShapeDtypeStruct((16, 40, 1280), BF), jax.ShapeDtypeStruct((16, 40, 1280), F32)],
        scratch_shapes=[pltpu.VMEM((1280, 1536), BF)],
        compiler_params=pltpu.CompilerParams(vmem_limit_bytes=VLIM),
        cost_estimate=pl.CostEstimate(flops=5 * 10**9, bytes_accessed=13 * 10**6, transcendentals=0),
        name="chi",
    )(pos, first, *us)


def deinterleave():
    rows = np.zeros((2, 32, 64), np.float32)
    cols = np.zeros((2, 64, 64), np.float32)
    for g in range(2):
        for q in range(32):
            rows[g, q, 2 * q + g] = 1.0
        for j in range(2):
            for c in range(32):
                cols[g, 2 * c + (g ^ j), 32 * j + c] = 1.0
    return jnp.asarray(rows, BF), jnp.asarray(cols, BF)


def body(three_center, atom_size, tensor_pattern, green_occ, green_virt, green_pattern):
    a, o = lax.axis_index("aux"), lax.axis_index("orb")
    pos = jnp.stack([a, o]).astype(jnp.int32)
    perm = swap16()
    rows, cols = deinterleave()
    x = three_center.transpose(0, 2, 1, 3)

    marks = jnp.concatenate([tensor_pattern.reshape(1, NG * W), green_pattern], axis=1).astype(BF)
    marks = jnp.pad(marks, ((0, 1), (0, 4096 - NG * W - W)))
    own = jnp.concatenate([green_occ[0], green_virt[0], marks], axis=0)
    every = jnp.broadcast_to(own[None], (NOB,) + own.shape)
    every = lax.all_to_all(every, "orb", split_axis=0, concat_axis=0, tiled=True)

    *tb, x = lax.optimization_barrier((*block_pairs(pos, perm, x), x))
    tb = [t.reshape(TROWS, 128) for t in tb]
    for k in (1, 2, 6):
        tb[k] = lax.ppermute(tb[k], "aux", pairs_of(k))
    marks, ta = lax.optimization_barrier((every[:, 2 * W, :128], row_slabs(x)))
    both = jnp.concatenate([marks, lax.ppermute(marks, "aux", pairs_of(1))], axis=0)
    both, tb[1], tb[2], tb[6], ta = lax.optimization_barrier((both, tb[1], tb[2], tb[6], ta))
    ta = lax.all_to_all(ta, "orb", split_axis=0, concat_axis=0, tiled=True)
    for k in CARRIERS:
        tb[k] = jnp.concatenate([tb[k], both], axis=0)
    for k in (3, 4, 5, 7):
        tb[k] = lax.ppermute(tb[k], "aux", pairs_of(k))
    back, far, ahead = [tb[k][TROWS:, :32] for k in CARRIERS]
    pat = jnp.concatenate([both[:, :32], back[16:], back[:16], far, ahead[16:], ahead[:16]], axis=0)
    pat = pat.astype(jnp.int32).reshape(-1)
    meta = marks.astype(jnp.int32).reshape(-1)
    blocks = every[:, : 2 * W].reshape(NOB, 2 * W, BS, BS)
    v, w = greens(pos, atom_size, meta, blocks, rows, cols)

    first = first_products(pos, pat, perm, w, tb)
    first = lax.all_to_all(first, "orb", split_axis=0, concat_axis=0, tiled=True)
    us = second_products(pos, meta, perm, ta.reshape(160, W, NOB, 256), v)
    us = [us[0]] + [lax.ppermute(us[k], "aux", pairs_of(k)) for k in range(1, 8)]

    theirs, mine = chi_share(pos, first, us)
    part = (mine + lax.ppermute(theirs, "aux", pairs_of(1)).astype(F32)).astype(BF)
    part = lax.all_to_all(part, "orb", split_axis=0, concat_axis=0, tiled=True)
    part = jnp.sum(part.astype(F32), axis=0).reshape(4, NPD, 1280)
    x = a // 2
    total = lax.dynamic_index_in_dim(part, x, 0, keepdims=False)
    for dx in range(1, 4):
        piece = lax.dynamic_index_in_dim(part, lax.rem(x + dx, 4), 0, keepdims=False)
        total = total + lax.ppermute(piece, "aux", pairs_of(2 * dx))
    return total


def solution(mesh):
    return jax.shard_map(
        body,
        mesh=mesh,
        in_specs=(
            P(("aux", "orb"), None, None, None),
            P(),
            P("aux", "orb", None),
            P("orb", None, None),
            P("orb", None, None),
            P("orb", None),
        ),
        out_specs=P(("aux", "orb"), None),
        check_vma=False,
    )
```

```python
import functools

import jax
import jax.numpy as jnp
import numpy as np
from jax import lax
from jax.experimental import pallas as pl
from jax.experimental.pallas import tpu as pltpu
from jax.sharding import PartitionSpec as P

BS = 64
R = 1
W = 3
ABS = 16
NOB = 16
NPD = 10
NG = 10
BF = jnp.bfloat16
F32 = jnp.float32
VLIM = 56 * 1024 * 1024
VSMALL = 24 * 1024 * 1024

STEPS = [(k // 2, k % 2) for k in range(8)]


TROWS = 2 * W * NPD * 32
CARRIERS = (3, 4, 7)


def pairs_of(k):
    dx, dc = STEPS[k]
    return [(i, ((i // 2 + dx) % 4) * 2 + ((i % 2) ^ dc)) for i in range(8)]


def dest_of(a, k):
    dx, dc = STEPS[k]
    return lax.rem(a // 2 + dx, 4) * 2 + (lax.rem(a, 2) if dc == 0 else 1 - lax.rem(a, 2))


def src_of(a, k):
    dx, dc = STEPS[k]
    return lax.rem(a // 2 + 4 - dx, 4) * 2 + (lax.rem(a, 2) if dc == 0 else 1 - lax.rem(a, 2))


def swap16():
    r = np.arange(256)
    m = np.zeros((256, 256), np.float32)
    m[r, (r % 16) * 16 + r // 16] = 1.0
    return jnp.asarray(m, BF)


def vspec():
    return pl.BlockSpec(memory_space=pltpu.VMEM)


def sspec():
    return pl.BlockSpec(memory_space=pltpu.SMEM)


def rows_kernel(x_ref, ta_ref):
    for p in range(2):
        for d in range(W):
            for o in range(16):
                ta_ref[o, p * W + d] = x_ref[p, d, :, 256 * o : 256 * o + 256]


def row_slabs(x):
    return pl.pallas_call(
        rows_kernel,
        grid=(NPD // 2,),
        in_specs=[pl.BlockSpec((2, W, NOB, 4096), lambda i: (i, 0, 0, 0))],
        out_specs=pl.BlockSpec((16, 2 * W, NOB, 256), lambda i: (0, i, 0, 0)),
        out_shape=jax.ShapeDtypeStruct((16, NPD * W, NOB, 256), BF),
        compiler_params=pltpu.CompilerParams(vmem_limit_bytes=VSMALL),
        cost_estimate=pl.CostEstimate(flops=0, bytes_accessed=8 * 10**6, transcendentals=0),
        name="row_slabs",
    )(x)


def pairs_kernel(pos, perm, x_ref, *rest):
    tb, s = rest[:8], rest[8]
    a = pos[0]
    for p in range(2):
        for d in range(W):
            x = x_ref[p, d]
            halves = [
                jnp.concatenate([x[:, 128 * (16 * h + c) : 128 * (16 * h + c) + 128] for c in range(16)], axis=0)
                for h in range(2)
            ]
            y = jnp.dot(perm[...], jnp.concatenate(halves, axis=1), preferred_element_type=F32).astype(BF)
            for n in range(NOB):
                part = y[16 * n : 16 * n + 16]
                for h in range(2):
                    s[n, d, p, 16 * h : 16 * h + 16] = part[:, 128 * h : 128 * h + 128]
    for k in range(8):
        t = dest_of(a, k)
        for i in range(2):
            tb[k][i] = s[2 * t + i]


def block_pairs(pos, perm, x):
    return pl.pallas_call(
        pairs_kernel,
        grid=(NPD // 2,),
        in_specs=[
            sspec(),
            pl.BlockSpec((256, 256), lambda i: (0, 0)),
            pl.BlockSpec((2, W, NOB, 4096), lambda i: (i, 0, 0, 0)),
        ],
        out_specs=[pl.BlockSpec((2, W, 2, 32, 128), lambda i: (0, 0, i, 0, 0))] * 8,
        out_shape=[jax.ShapeDtypeStruct((2, W, NPD, 32, 128), BF)] * 8,
        scratch_shapes=[pltpu.VMEM((NOB, W, 2, 32, 128), BF)],
        compiler_params=pltpu.CompilerParams(vmem_limit_bytes=VSMALL),
        cost_estimate=pl.CostEstimate(flops=10**9, bytes_accessed=8 * 10**6, transcendentals=0),
        name="block_pairs",
    )(pos, perm, x)


def greens_kernel(pos, size, meta, g_ref, rows_ref, cols_ref, v_ref, w_ref, o_ref):
    a = pos[0]
    row = lax.broadcasted_iota(jnp.int32, (BS, BS), 0)
    col = lax.broadcasted_iota(jnp.int32, (BS, BS), 1)

    def one(n, carry):
        for d in range(W):
            m = n + d - R
            ok = (m >= 0) & (m < NOB)
            if d != R:
                ok = ok & (meta[n * 128 + NG * W + d] > 0)
            rows_in = jnp.where(ok, size[jnp.clip(m, 0, NOB - 1)], 0)
            mask = (row < rows_in) & (col < size[n])
            occ = jnp.where(mask, g_ref[n, d], jnp.zeros((BS, BS), BF))
            v = jnp.where(mask, g_ref[n, W + d], jnp.zeros((BS, BS), BF))
            for g in range(2):
                t = jnp.dot(rows_ref[g], occ, preferred_element_type=F32).astype(BF)
                o_ref[n, d, 32 * g : 32 * g + 32] = jnp.dot(
                    t, cols_ref[g], preferred_element_type=F32
                ).astype(BF)
            v_ref[n, d] = jnp.concatenate([v, v], axis=1)
        return carry

    lax.fori_loop(0, NOB, one, 0)
    z = jnp.zeros((32, 64), BF)
    for i in range(2):
        for g in range(2):
            for e in range(W):
                cols = []
                for d in range(W):
                    f = e - d + 1
                    if f < 0 or f >= W:
                        cols.append(z)
                        continue
                    m = 2 * a + i + d - 1
                    ok = (m >= 0) & (m < NOB)
                    mc = jnp.clip(m, 0, NOB - 1)
                    v = o_ref[mc, f, 32 * g : 32 * g + 32]
                    cols.append(jnp.where(ok, v, z))
                row = (g * W + e) * 32
                w_ref[i, row : row + 32, :] = jnp.concatenate(cols, axis=1)


def greens(pos, size, meta, g, rows, cols):
    return pl.pallas_call(
        greens_kernel,
        in_specs=[sspec()] * 3 + [vspec()] * 3,
        out_specs=[vspec(), vspec()],
        scratch_shapes=[pltpu.VMEM((NOB, W, 64, 64), BF)],
        out_shape=[
            jax.ShapeDtypeStruct((NOB, W, BS, 128), BF),
            jax.ShapeDtypeStruct((2, 192, 192), BF),
        ],
        compiler_params=pltpu.CompilerParams(vmem_limit_bytes=VLIM),
        cost_estimate=pl.CostEstimate(flops=10**6, bytes_accessed=8 * 10**6, transcendentals=0),
        name="greens",
    )(pos, size, meta, g, rows, cols)


def second_kernel(steps, pos, pat, perm, ta_ref, v_ref, *rest):
    outs, s, kb = rest[:4], rest[4], rest[5]
    a = pos[0]
    low = lax.broadcasted_iota(jnp.int32, (BS, 128), 1) < 64
    zero = jnp.zeros((BS, 128), BF)
    kb[...] = jnp.zeros(kb.shape, BF)
    s[0] = jnp.zeros(s.shape[1:], BF)
    s[NOB + 1] = jnp.zeros(s.shape[1:], BF)

    def regroup(g, carry):
        for d in range(W):
            x = ta_ref[pl.ds(16 * g, 16), d].reshape(256, 256)
            y = jnp.dot(perm[...], x, preferred_element_type=F32).astype(BF)
            for n in range(NOB):
                keep = pat[n * 128 + g * W + d] > 0
                part = y[16 * n : 16 * n + 16]
                s[n + 1, d, pl.ds(pl.multiple_of(16 * g, 16), 16)] = jnp.where(
                    keep, part, jnp.zeros_like(part)
                )
        return carry

    lax.fori_loop(0, NG, regroup, 0)
    for j, k in enumerate(steps):
        t = dest_of(a, k)

        def one(i, carry, j=j, t=t):
            n = 2 * t + i
            for d in range(W):
                v = v_ref[n, d]
                lo, hi = jnp.where(low, v, zero), jnp.where(low, zero, v)
                for q in range(4):
                    row, col = 256 * d + 64 * q, 128 * (q // 2)
                    kb[row : row + 64, col : col + 128] = hi if q % 2 else lo
            for e in range(W):
                ds = [d for d in range(W) if 0 <= e - d + 1 < W]
                lhs = jnp.concatenate([s[n + d, e - d + 1] for d in ds], axis=1)
                rhs = kb[256 * ds[0] : 256 * ds[-1] + 256]
                outs[j][i * W + e] = jnp.dot(lhs, rhs, preferred_element_type=F32).astype(BF)
            return carry

        lax.fori_loop(0, 2, one, 0)


def second_products(steps, pos, pat, perm, ta, v):
    return pl.pallas_call(
        functools.partial(second_kernel, steps),
        in_specs=[sspec(), sspec(), vspec(), vspec(), vspec()],
        out_specs=[vspec()] * 4,
        out_shape=[jax.ShapeDtypeStruct((2 * W, 160, 256), BF)] * 4,
        scratch_shapes=[pltpu.VMEM((NOB + 2, W, 160, 256), BF), pltpu.VMEM((256 * W, 256), BF)],
        compiler_params=pltpu.CompilerParams(vmem_limit_bytes=VLIM),
        cost_estimate=pl.CostEstimate(flops=2 * 10**9, bytes_accessed=15 * 10**6, transcendentals=0),
        name="second",
    )(pos, pat, perm, ta, v)


def first_kernel(pos, pat, perm, w_ref, *rest):
    tb, out, s = rest[:8], rest[8], rest[9]
    a, o = pos[0], pos[1]
    lane = lax.broadcasted_iota(jnp.int32, (96, NPD * 128), 1)
    low = lax.rem(lane, 128) < 64
    for k in range(8):
        src = src_of(a, k)
        base = lax.rem(src, 2) * 40 + (src // 2) * 10

        def one(i, carry, k=k, base=base):
            n = 2 * a + i
            columns = []
            for p in range(NPD):
                rows = []
                for d in range(W):
                    keep = pat[(k * NOB + n) * 32 + lax.div(o * NPD + p, ABS) * W + d] > 0
                    row = pl.multiple_of(((i * W + d) * NPD + p) * 32, 32)
                    x = tb[k][pl.ds(row, 32)]
                    x = jnp.where(keep, x, jnp.zeros_like(x))
                    rows.append(x)
                    rows.append(jnp.concatenate([x[:, 64:], x[:, :64]], axis=1))
                columns.append(jnp.concatenate(rows, axis=0))
            y = jnp.dot(w_ref[i], jnp.concatenate(columns, axis=1), preferred_element_type=F32)
            y = jnp.where(low, y[:96], y[96:]).astype(BF)
            for p in range(NPD):
                s[i, base + p] = y[:, 128 * p : 128 * p + 128]
            return carry

        lax.fori_loop(0, 2, one, 0)

    def regroup(j, carry):
        i = j // 5
        g = lax.rem(j, 5)
        tiles = s[i, pl.ds(16 * g, 16)]
        for e in range(W):
            x = jnp.concatenate(
                [tiles[:, 32 * e + 16 * h : 32 * e + 16 * h + 16].reshape(256, 128) for h in range(2)], axis=1
            )
            y = jnp.dot(perm[...], x, preferred_element_type=F32).astype(BF)
            for h in range(2):
                for q in range(16):
                    qq = 16 * h + q
                    out[qq // 2, i * W + e, pl.ds(pl.multiple_of(16 * g, 16), 16),
                        128 * (qq % 2) : 128 * (qq % 2) + 128] = y[16 * q : 16 * q + 16, 128 * h : 128 * h + 128]
        return carry

    lax.fori_loop(0, 10, regroup, 0)


def first_products(pos, pat, perm, w, tb):
    return pl.pallas_call(
        first_kernel,
        in_specs=[sspec(), sspec(), vspec(), vspec()] + [vspec()] * 8,
        out_specs=vspec(),
        out_shape=jax.ShapeDtypeStruct((16, 2 * W, 80, 256), BF),
        scratch_shapes=[pltpu.VMEM((2, 80, 96, 128), BF)],
        compiler_params=pltpu.CompilerParams(vmem_limit_bytes=VLIM),
        cost_estimate=pl.CostEstimate(flops=3 * 10**9, bytes_accessed=8 * 10**6, transcendentals=0),
        name="first",
    )(pos, pat, perm, w, *tb)


def chi_kernel(pos, first_ref, *rest):
    us, theirs, mine, rhs = rest[:8], rest[8], rest[9], rest[10]
    a = pos[0]
    core0 = lax.rem(a, 2) == 0
    t = pl.program_id(0)

    @pl.when(t == 0)
    def _():
        for k in range(8):
            row = pl.multiple_of(src_of(a, k) * 160, 32)
            for kk in range(6):
                rhs[pl.ds(row, 160), 256 * kk : 256 * kk + 256] = us[k][kk]

    lhs = jnp.concatenate([first_ref[:, kk].reshape(1280, 256) for kk in range(6)], axis=1)
    r = lax.dot_general(
        lhs,
        rhs[pl.ds(pl.multiple_of(256 * t, 256), 256)],
        (((1,), (1,)), ((), ())),
        preferred_element_type=F32,
    )
    for b in range(16):
        lo, hi = r[80 * b : 80 * b + 40], r[80 * b + 40 : 80 * b + 80]
        mine[b] = jnp.where(core0, lo, hi)
        theirs[b] = jnp.where(core0, hi, lo).astype(BF)


def chi_share(pos, first, us):
    return pl.pallas_call(
        chi_kernel,
        grid=(5,),
        in_specs=[sspec(), vspec()] + [vspec()] * 8,
        out_specs=[pl.BlockSpec((16, 40, 256), lambda t: (0, 0, t))] * 2,
        out_shape=[jax.ShapeDtypeStruct((16, 40, 1280), BF), jax.ShapeDtypeStruct((16, 40, 1280), F32)],
        scratch_shapes=[pltpu.VMEM((1280, 1536), BF)],
        compiler_params=pltpu.CompilerParams(vmem_limit_bytes=VLIM),
        cost_estimate=pl.CostEstimate(flops=5 * 10**9, bytes_accessed=13 * 10**6, transcendentals=0),
        name="chi",
    )(pos, first, *us)


def deinterleave():
    rows = np.zeros((2, 32, 64), np.float32)
    cols = np.zeros((2, 64, 64), np.float32)
    for g in range(2):
        for q in range(32):
            rows[g, q, 2 * q + g] = 1.0
        for j in range(2):
            for c in range(32):
                cols[g, 2 * c + (g ^ j), 32 * j + c] = 1.0
    return jnp.asarray(rows, BF), jnp.asarray(cols, BF)


def body(three_center, atom_size, tensor_pattern, green_occ, green_virt, green_pattern):
    a, o = lax.axis_index("aux"), lax.axis_index("orb")
    pos = jnp.stack([a, o]).astype(jnp.int32)
    perm = swap16()
    rows, cols = deinterleave()
    x = three_center.transpose(0, 2, 1, 3)

    marks = jnp.concatenate([tensor_pattern.reshape(1, NG * W), green_pattern], axis=1).astype(BF)
    marks = jnp.pad(marks, ((0, 1), (0, 4096 - NG * W - W)))
    own = jnp.concatenate([green_occ[0], green_virt[0], marks], axis=0)
    every = jnp.broadcast_to(own[None], (NOB,) + own.shape)
    every = lax.all_to_all(every, "orb", split_axis=0, concat_axis=0, tiled=True)

    *tb, x = lax.optimization_barrier((*block_pairs(pos, perm, x), x))
    tb = [t.reshape(TROWS, 128) for t in tb]
    for k in (1, 2, 6):
        tb[k] = lax.ppermute(tb[k], "aux", pairs_of(k))
    marks, ta = lax.optimization_barrier((every[:, 2 * W, :128], row_slabs(x)))
    both = jnp.concatenate([marks, lax.ppermute(marks, "aux", pairs_of(1))], axis=0)
    both, tb[1], tb[2], tb[6], ta = lax.optimization_barrier((both, tb[1], tb[2], tb[6], ta))
    ta = lax.all_to_all(ta, "orb", split_axis=0, concat_axis=0, tiled=True)
    for k in CARRIERS:
        tb[k] = jnp.concatenate([tb[k], both], axis=0)
    for k in (3, 4, 5, 7):
        tb[k] = lax.ppermute(tb[k], "aux", pairs_of(k))
    back, far, ahead = [tb[k][TROWS:, :32] for k in CARRIERS]
    pat = jnp.concatenate([both[:, :32], back[16:], back[:16], far, ahead[16:], ahead[:16]], axis=0)
    pat = pat.astype(jnp.int32).reshape(-1)
    meta = marks.astype(jnp.int32).reshape(-1)
    blocks = every[:, : 2 * W].reshape(NOB, 2 * W, BS, BS)
    v, w = greens(pos, atom_size, meta, blocks, rows, cols)

    first = first_products(pos, pat, perm, w, tb)
    first = lax.all_to_all(first, "orb", split_axis=0, concat_axis=0, tiled=True)
    us = [None] * 8
    ta = ta.reshape(160, W, NOB, 256)
    late = (4, 5, 1)
    for k, u in zip((2, 6, 3, 7), second_products((2, 6, 3, 7), pos, meta, perm, ta, v)):
        us[k] = lax.ppermute(u, "aux", pairs_of(k))
    *parts, us[0] = second_products(late + (0,), pos, meta, perm, ta, v)
    *parts, us[2], us[6] = lax.optimization_barrier((*parts, us[2], us[6]))
    for k, u in zip(late, parts):
        us[k] = lax.ppermute(u, "aux", pairs_of(k))

    theirs, mine = chi_share(pos, first, us)
    part = (mine + lax.ppermute(theirs, "aux", pairs_of(1)).astype(F32)).astype(BF)
    part = lax.all_to_all(part, "orb", split_axis=0, concat_axis=0, tiled=True)
    part = jnp.sum(part.astype(F32), axis=0).reshape(4, NPD, 1280)
    x = a // 2
    total = lax.dynamic_index_in_dim(part, x, 0, keepdims=False)
    for dx in range(1, 4):
        piece = lax.dynamic_index_in_dim(part, lax.rem(x + dx, 4), 0, keepdims=False)
        total = total + lax.ppermute(piece, "aux", pairs_of(2 * dx))
    return total


def solution(mesh):
    return jax.shard_map(
        body,
        mesh=mesh,
        in_specs=(
            P(("aux", "orb"), None, None, None),
            P(),
            P("aux", "orb", None),
            P("orb", None, None),
            P("orb", None, None),
            P("orb", None),
        ),
        out_specs=P(("aux", "orb"), None),
        check_vma=False,
    )
```

```python
import functools

import jax
import jax.numpy as jnp
import numpy as np
from jax import lax
from jax.experimental import pallas as pl
from jax.experimental.pallas import tpu as pltpu
from jax.sharding import PartitionSpec as P

BS = 64
R = 1
W = 3
ABS = 16
NOB = 16
NPD = 10
NG = 10
BF = jnp.bfloat16
F32 = jnp.float32
VLIM = 56 * 1024 * 1024
VSMALL = 24 * 1024 * 1024

STEPS = [(k // 2, k % 2) for k in range(8)]


TROWS = 2 * W * NPD * 32
CARRIERS = (3, 4, 7)


def pairs_of(k):
    dx, dc = STEPS[k]
    return [(i, ((i // 2 + dx) % 4) * 2 + ((i % 2) ^ dc)) for i in range(8)]


def dest_of(a, k):
    dx, dc = STEPS[k]
    return lax.rem(a // 2 + dx, 4) * 2 + (lax.rem(a, 2) if dc == 0 else 1 - lax.rem(a, 2))


def src_of(a, k):
    dx, dc = STEPS[k]
    return lax.rem(a // 2 + 4 - dx, 4) * 2 + (lax.rem(a, 2) if dc == 0 else 1 - lax.rem(a, 2))


def swap16():
    r = np.arange(256)
    m = np.zeros((256, 256), np.float32)
    m[r, (r % 16) * 16 + r // 16] = 1.0
    return jnp.asarray(m, BF)


def vspec():
    return pl.BlockSpec(memory_space=pltpu.VMEM)


def sspec():
    return pl.BlockSpec(memory_space=pltpu.SMEM)


def rows_kernel(x_ref, ta_ref):
    for p in range(2):
        for d in range(W):
            for o in range(16):
                ta_ref[o, p * W + d] = x_ref[p, d, :, 256 * o : 256 * o + 256]


def row_slabs(x):
    return pl.pallas_call(
        rows_kernel,
        grid=(NPD // 2,),
        in_specs=[pl.BlockSpec((2, W, NOB, 4096), lambda i: (i, 0, 0, 0))],
        out_specs=pl.BlockSpec((16, 2 * W, NOB, 256), lambda i: (0, i, 0, 0)),
        out_shape=jax.ShapeDtypeStruct((16, NPD * W, NOB, 256), BF),
        compiler_params=pltpu.CompilerParams(vmem_limit_bytes=VSMALL),
        cost_estimate=pl.CostEstimate(flops=0, bytes_accessed=8 * 10**6, transcendentals=0),
        name="row_slabs",
    )(x)


def pairs_kernel(pos, perm, x_ref, *rest):
    tb, s = rest[:8], rest[8]
    a = pos[0]
    for p in range(2):
        for d in range(W):
            x = x_ref[p, d]
            halves = [
                jnp.concatenate([x[:, 128 * (16 * h + c) : 128 * (16 * h + c) + 128] for c in range(16)], axis=0)
                for h in range(2)
            ]
            y = jnp.dot(perm[...], jnp.concatenate(halves, axis=1), preferred_element_type=F32).astype(BF)
            for n in range(NOB):
                part = y[16 * n : 16 * n + 16]
                for h in range(2):
                    s[n, d, p, 16 * h : 16 * h + 16] = part[:, 128 * h : 128 * h + 128]
    for k in range(8):
        t = dest_of(a, k)
        for i in range(2):
            tb[k][i] = s[2 * t + i]


def block_pairs(pos, perm, x):
    return pl.pallas_call(
        pairs_kernel,
        grid=(NPD // 2,),
        in_specs=[
            sspec(),
            pl.BlockSpec((256, 256), lambda i: (0, 0)),
            pl.BlockSpec((2, W, NOB, 4096), lambda i: (i, 0, 0, 0)),
        ],
        out_specs=[pl.BlockSpec((2, W, 2, 32, 128), lambda i: (0, 0, i, 0, 0))] * 8,
        out_shape=[jax.ShapeDtypeStruct((2, W, NPD, 32, 128), BF)] * 8,
        scratch_shapes=[pltpu.VMEM((NOB, W, 2, 32, 128), BF)],
        compiler_params=pltpu.CompilerParams(vmem_limit_bytes=VSMALL),
        cost_estimate=pl.CostEstimate(flops=10**9, bytes_accessed=8 * 10**6, transcendentals=0),
        name="block_pairs",
    )(pos, perm, x)


def pack_kernel(tpat, gpat, occ_ref, virt_ref, out):
    lane = lax.broadcasted_iota(jnp.int32, (1, 128), 1)
    row = jnp.zeros((1, 128), jnp.int32)
    for d in range(W):
        for g in range(NG):
            row = jnp.where(lane == g * W + d, tpat[d, 0, g], row)
        row = jnp.where(lane == NG * W + d, gpat[0, d], row)
    tail = jnp.concatenate([row, jnp.zeros((1, 128), jnp.int32)], axis=0).astype(F32).astype(BF)
    rest = jnp.zeros((2, 4096 - 128), BF)
    own = jnp.concatenate([occ_ref[0], virt_ref[0], jnp.concatenate([tail, rest], axis=1)], axis=0)
    for o in range(NOB):
        out[o] = own


def pack(tpat, gpat, occ, virt):
    return pl.pallas_call(
        pack_kernel,
        in_specs=[sspec(), sspec(), vspec(), vspec()],
        out_specs=vspec(),
        out_shape=jax.ShapeDtypeStruct((NOB, 8, 4096), BF),
        compiler_params=pltpu.CompilerParams(vmem_limit_bytes=VSMALL),
        cost_estimate=pl.CostEstimate(flops=0, bytes_accessed=11 * 10**5, transcendentals=0),
        name="pack",
    )(tpat, gpat, occ, virt)


def greens_kernel(pos, size, meta, g_ref, rows_ref, cols_ref, v_ref, w_ref, o_ref):
    a = pos[0]
    row = lax.broadcasted_iota(jnp.int32, (BS, BS), 0)
    col = lax.broadcasted_iota(jnp.int32, (BS, BS), 1)

    def one(n, carry):
        for d in range(W):
            m = n + d - R
            ok = (m >= 0) & (m < NOB)
            if d != R:
                ok = ok & (meta[n * 128 + NG * W + d] > 0)
            rows_in = jnp.where(ok, size[jnp.clip(m, 0, NOB - 1)], 0)
            mask = (row < rows_in) & (col < size[n])
            occ = jnp.where(mask, g_ref[n, d], jnp.zeros((BS, BS), BF))
            v = jnp.where(mask, g_ref[n, W + d], jnp.zeros((BS, BS), BF))
            for g in range(2):
                t = jnp.dot(rows_ref[g], occ, preferred_element_type=F32).astype(BF)
                o_ref[n, d, 32 * g : 32 * g + 32] = jnp.dot(
                    t, cols_ref[g], preferred_element_type=F32
                ).astype(BF)
            v_ref[n, d] = jnp.concatenate([v, v], axis=1)
        return carry

    lax.fori_loop(0, NOB, one, 0)
    z = jnp.zeros((32, 64), BF)
    for i in range(2):
        for g in range(2):
            for e in range(W):
                cols = []
                for d in range(W):
                    f = e - d + 1
                    if f < 0 or f >= W:
                        cols.append(z)
                        continue
                    m = 2 * a + i + d - 1
                    ok = (m >= 0) & (m < NOB)
                    mc = jnp.clip(m, 0, NOB - 1)
                    v = o_ref[mc, f, 32 * g : 32 * g + 32]
                    cols.append(jnp.where(ok, v, z))
                row = (g * W + e) * 32
                w_ref[i, row : row + 32, :] = jnp.concatenate(cols, axis=1)


def greens(pos, size, meta, g, rows, cols):
    return pl.pallas_call(
        greens_kernel,
        in_specs=[sspec()] * 3 + [vspec()] * 3,
        out_specs=[vspec(), vspec()],
        scratch_shapes=[pltpu.VMEM((NOB, W, 64, 64), BF)],
        out_shape=[
            jax.ShapeDtypeStruct((NOB, W, BS, 128), BF),
            jax.ShapeDtypeStruct((2, 192, 192), BF),
        ],
        compiler_params=pltpu.CompilerParams(vmem_limit_bytes=VLIM),
        cost_estimate=pl.CostEstimate(flops=10**6, bytes_accessed=8 * 10**6, transcendentals=0),
        name="greens",
    )(pos, size, meta, g, rows, cols)


def second_kernel(steps, pos, pat, perm, ta_ref, v_ref, *rest):
    outs, s, kb = rest[:4], rest[4], rest[5]
    a = pos[0]
    low = lax.broadcasted_iota(jnp.int32, (BS, 128), 1) < 64
    zero = jnp.zeros((BS, 128), BF)
    kb[...] = jnp.zeros(kb.shape, BF)
    s[0] = jnp.zeros(s.shape[1:], BF)
    s[NOB + 1] = jnp.zeros(s.shape[1:], BF)

    def regroup(g, carry):
        for d in range(W):
            x = ta_ref[pl.ds(16 * g, 16), d].reshape(256, 256)
            y = jnp.dot(perm[...], x, preferred_element_type=F32).astype(BF)
            for n in range(NOB):
                keep = pat[n * 128 + g * W + d] > 0
                part = y[16 * n : 16 * n + 16]
                s[n + 1, d, pl.ds(pl.multiple_of(16 * g, 16), 16)] = jnp.where(
                    keep, part, jnp.zeros_like(part)
                )
        return carry

    lax.fori_loop(0, NG, regroup, 0)
    for j, k in enumerate(steps):
        t = dest_of(a, k)

        def one(i, carry, j=j, t=t):
            n = 2 * t + i
            for d in range(W):
                v = v_ref[n, d]
                lo, hi = jnp.where(low, v, zero), jnp.where(low, zero, v)
                for q in range(4):
                    row, col = 256 * d + 64 * q, 128 * (q // 2)
                    kb[row : row + 64, col : col + 128] = hi if q % 2 else lo
            for e in range(W):
                ds = [d for d in range(W) if 0 <= e - d + 1 < W]
                lhs = jnp.concatenate([s[n + d, e - d + 1] for d in ds], axis=1)
                rhs = kb[256 * ds[0] : 256 * ds[-1] + 256]
                outs[j][i * W + e] = jnp.dot(lhs, rhs, preferred_element_type=F32).astype(BF)
            return carry

        lax.fori_loop(0, 2, one, 0)


def second_products(steps, pos, pat, perm, ta, v):
    return pl.pallas_call(
        functools.partial(second_kernel, steps),
        in_specs=[sspec(), sspec(), vspec(), vspec(), vspec()],
        out_specs=[vspec()] * 4,
        out_shape=[jax.ShapeDtypeStruct((2 * W, 160, 256), BF)] * 4,
        scratch_shapes=[pltpu.VMEM((NOB + 2, W, 160, 256), BF), pltpu.VMEM((256 * W, 256), BF)],
        compiler_params=pltpu.CompilerParams(vmem_limit_bytes=VLIM),
        cost_estimate=pl.CostEstimate(flops=2 * 10**9, bytes_accessed=15 * 10**6, transcendentals=0),
        name="second",
    )(pos, pat, perm, ta, v)


def first_kernel(pos, pat, perm, w_ref, *rest):
    tb, out, s = rest[:8], rest[8], rest[9]
    a, o = pos[0], pos[1]
    lane = lax.broadcasted_iota(jnp.int32, (96, NPD * 128), 1)
    low = lax.rem(lane, 128) < 64
    for k in range(8):
        src = src_of(a, k)
        base = lax.rem(src, 2) * 40 + (src // 2) * 10

        def one(i, carry, k=k, base=base):
            n = 2 * a + i
            columns = []
            for p in range(NPD):
                rows = []
                for d in range(W):
                    keep = pat[(k * NOB + n) * 32 + lax.div(o * NPD + p, ABS) * W + d] > 0
                    row = pl.multiple_of(((i * W + d) * NPD + p) * 32, 32)
                    x = tb[k][pl.ds(row, 32)]
                    x = jnp.where(keep, x, jnp.zeros_like(x))
                    rows.append(x)
                    rows.append(jnp.concatenate([x[:, 64:], x[:, :64]], axis=1))
                columns.append(jnp.concatenate(rows, axis=0))
            y = jnp.dot(w_ref[i], jnp.concatenate(columns, axis=1), preferred_element_type=F32)
            y = jnp.where(low, y[:96], y[96:]).astype(BF)
            for p in range(NPD):
                s[i, base + p] = y[:, 128 * p : 128 * p + 128]
            return carry

        lax.fori_loop(0, 2, one, 0)

    def regroup(j, carry):
        i = j // 5
        g = lax.rem(j, 5)
        tiles = s[i, pl.ds(16 * g, 16)]
        for e in range(W):
            x = jnp.concatenate(
                [tiles[:, 32 * e + 16 * h : 32 * e + 16 * h + 16].reshape(256, 128) for h in range(2)], axis=1
            )
            y = jnp.dot(perm[...], x, preferred_element_type=F32).astype(BF)
            for h in range(2):
                for q in range(16):
                    qq = 16 * h + q
                    out[qq // 2, i * W + e, pl.ds(pl.multiple_of(16 * g, 16), 16),
                        128 * (qq % 2) : 128 * (qq % 2) + 128] = y[16 * q : 16 * q + 16, 128 * h : 128 * h + 128]
        return carry

    lax.fori_loop(0, 10, regroup, 0)


def first_products(pos, pat, perm, w, tb):
    return pl.pallas_call(
        first_kernel,
        in_specs=[sspec(), sspec(), vspec(), vspec()] + [vspec()] * 8,
        out_specs=vspec(),
        out_shape=jax.ShapeDtypeStruct((16, 2 * W, 80, 256), BF),
        scratch_shapes=[pltpu.VMEM((2, 80, 96, 128), BF)],
        compiler_params=pltpu.CompilerParams(vmem_limit_bytes=VLIM),
        cost_estimate=pl.CostEstimate(flops=3 * 10**9, bytes_accessed=8 * 10**6, transcendentals=0),
        name="first",
    )(pos, pat, perm, w, *tb)


def chi_kernel(pos, first_ref, *rest):
    us, theirs, mine, rhs = rest[:8], rest[8], rest[9], rest[10]
    a = pos[0]
    core0 = lax.rem(a, 2) == 0
    t = pl.program_id(0)

    @pl.when(t == 0)
    def _():
        for k in range(8):
            row = pl.multiple_of(src_of(a, k) * 160, 32)
            for kk in range(6):
                rhs[pl.ds(row, 160), 256 * kk : 256 * kk + 256] = us[k][kk]

    lhs = jnp.concatenate([first_ref[:, kk].reshape(1280, 256) for kk in range(6)], axis=1)
    r = lax.dot_general(
        lhs,
        rhs[pl.ds(pl.multiple_of(256 * t, 256), 256)],
        (((1,), (1,)), ((), ())),
        preferred_element_type=F32,
    )
    for b in range(16):
        lo, hi = r[80 * b : 80 * b + 40], r[80 * b + 40 : 80 * b + 80]
        mine[b] = jnp.where(core0, lo, hi)
        theirs[b] = jnp.where(core0, hi, lo).astype(BF)


def chi_share(pos, first, us):
    return pl.pallas_call(
        chi_kernel,
        grid=(5,),
        in_specs=[sspec(), vspec()] + [vspec()] * 8,
        out_specs=[pl.BlockSpec((16, 40, 256), lambda t: (0, 0, t))] * 2,
        out_shape=[jax.ShapeDtypeStruct((16, 40, 1280), BF), jax.ShapeDtypeStruct((16, 40, 1280), F32)],
        scratch_shapes=[pltpu.VMEM((1280, 1536), BF)],
        compiler_params=pltpu.CompilerParams(vmem_limit_bytes=VLIM),
        cost_estimate=pl.CostEstimate(flops=5 * 10**9, bytes_accessed=13 * 10**6, transcendentals=0),
        name="chi",
    )(pos, first, *us)


def deinterleave():
    rows = np.zeros((2, 32, 64), np.float32)
    cols = np.zeros((2, 64, 64), np.float32)
    for g in range(2):
        for q in range(32):
            rows[g, q, 2 * q + g] = 1.0
        for j in range(2):
            for c in range(32):
                cols[g, 2 * c + (g ^ j), 32 * j + c] = 1.0
    return jnp.asarray(rows, BF), jnp.asarray(cols, BF)


def body(three_center, atom_size, tensor_pattern, green_occ, green_virt, green_pattern):
    a, o = lax.axis_index("aux"), lax.axis_index("orb")
    pos = jnp.stack([a, o]).astype(jnp.int32)
    perm = swap16()
    rows, cols = deinterleave()
    x = three_center.transpose(0, 2, 1, 3)

    every = pack(tensor_pattern.transpose(2, 1, 0), green_pattern, green_occ, green_virt)
    every = lax.all_to_all(every, "orb", split_axis=0, concat_axis=0, tiled=True)

    *tb, x = lax.optimization_barrier((*block_pairs(pos, perm, x), x))
    tb = [t.reshape(TROWS, 128) for t in tb]
    for k in (1, 2, 6):
        tb[k] = lax.ppermute(tb[k], "aux", pairs_of(k))
    marks, ta = lax.optimization_barrier((every[:, 2 * W, :128], row_slabs(x)))
    both = jnp.concatenate([marks, lax.ppermute(marks, "aux", pairs_of(1))], axis=0)
    both, tb[1], tb[2], tb[6], ta = lax.optimization_barrier((both, tb[1], tb[2], tb[6], ta))
    ta = lax.all_to_all(ta, "orb", split_axis=0, concat_axis=0, tiled=True)
    for k in CARRIERS:
        tb[k] = jnp.concatenate([tb[k], both], axis=0)
    for k in (3, 4, 5, 7):
        tb[k] = lax.ppermute(tb[k], "aux", pairs_of(k))
    back, far, ahead = [tb[k][TROWS:, :32] for k in CARRIERS]
    pat = jnp.concatenate([both[:, :32], back[16:], back[:16], far, ahead[16:], ahead[:16]], axis=0)
    pat = pat.astype(jnp.int32).reshape(-1)
    meta = marks.astype(jnp.int32).reshape(-1)
    blocks = every[:, : 2 * W].reshape(NOB, 2 * W, BS, BS)
    v, w = greens(pos, atom_size, meta, blocks, rows, cols)

    first = first_products(pos, pat, perm, w, tb)
    first = lax.all_to_all(first, "orb", split_axis=0, concat_axis=0, tiled=True)
    us = [None] * 8
    ta = ta.reshape(160, W, NOB, 256)
    late = (4, 5, 1)
    for k, u in zip((2, 6, 3, 7), second_products((2, 6, 3, 7), pos, meta, perm, ta, v)):
        us[k] = lax.ppermute(u, "aux", pairs_of(k))
    *parts, us[0] = second_products(late + (0,), pos, meta, perm, ta, v)
    *parts, us[2], us[6] = lax.optimization_barrier((*parts, us[2], us[6]))
    for k, u in zip(late, parts):
        us[k] = lax.ppermute(u, "aux", pairs_of(k))

    theirs, mine = chi_share(pos, first, us)
    part = (mine + lax.ppermute(theirs, "aux", pairs_of(1)).astype(F32)).astype(BF)
    part = lax.all_to_all(part, "orb", split_axis=0, concat_axis=0, tiled=True)
    part = jnp.sum(part.astype(F32), axis=0).reshape(4, NPD, 1280)
    x = a // 2
    high, low = (x // 2) * 2, lax.rem(x, 2)
    kept = lax.dynamic_slice_in_dim(part, high, 2, axis=0)
    sent = lax.dynamic_slice_in_dim(part, 2 - high, 2, axis=0)
    kept = kept + lax.ppermute(sent, "aux", pairs_of(4))
    sent = lax.dynamic_index_in_dim(kept, 1 - low, 0, keepdims=False)
    kept = lax.dynamic_index_in_dim(kept, low, 0, keepdims=False)
    return kept + lax.ppermute(sent, "aux", [(i, i ^ 2) for i in range(8)])


def solution(mesh):
    return jax.shard_map(
        body,
        mesh=mesh,
        in_specs=(
            P(("aux", "orb"), None, None, None),
            P(),
            P("aux", "orb", None),
            P("orb", None, None),
            P("orb", None, None),
            P("orb", None),
        ),
        out_specs=P(("aux", "orb"), None),
        check_vma=False,
    )
```

```python
import functools

import jax
import jax.numpy as jnp
import numpy as np
from jax import lax
from jax.experimental import pallas as pl
from jax.experimental.pallas import tpu as pltpu
from jax.sharding import PartitionSpec as P

BS = 64
R = 1
W = 3
ABS = 16
NOB = 16
NPD = 10
NG = 10
BF = jnp.bfloat16
F32 = jnp.float32
VLIM = 56 * 1024 * 1024
VSMALL = 24 * 1024 * 1024

STEPS = [(k // 2, k % 2) for k in range(8)]


TROWS = 2 * W * NPD * 32
CARRIERS = (3, 4, 7)


def pairs_of(k):
    dx, dc = STEPS[k]
    return [(i, ((i // 2 + dx) % 4) * 2 + ((i % 2) ^ dc)) for i in range(8)]


def dest_of(a, k):
    dx, dc = STEPS[k]
    return lax.rem(a // 2 + dx, 4) * 2 + (lax.rem(a, 2) if dc == 0 else 1 - lax.rem(a, 2))


def src_of(a, k):
    dx, dc = STEPS[k]
    return lax.rem(a // 2 + 4 - dx, 4) * 2 + (lax.rem(a, 2) if dc == 0 else 1 - lax.rem(a, 2))


def swap16():
    r = np.arange(256)
    m = np.zeros((256, 256), np.float32)
    m[r, (r % 16) * 16 + r // 16] = 1.0
    return jnp.asarray(m, BF)


def vspec():
    return pl.BlockSpec(memory_space=pltpu.VMEM)


def sspec():
    return pl.BlockSpec(memory_space=pltpu.SMEM)


def rows_kernel(x_ref, ta_ref):
    for p in range(2):
        for d in range(W):
            for o in range(16):
                ta_ref[o, p * W + d] = x_ref[p, d, :, 256 * o : 256 * o + 256]


def row_slabs(x):
    return pl.pallas_call(
        rows_kernel,
        grid=(NPD // 2,),
        in_specs=[pl.BlockSpec((2, W, NOB, 4096), lambda i: (i, 0, 0, 0))],
        out_specs=pl.BlockSpec((16, 2 * W, NOB, 256), lambda i: (0, i, 0, 0)),
        out_shape=jax.ShapeDtypeStruct((16, NPD * W, NOB, 256), BF),
        compiler_params=pltpu.CompilerParams(vmem_limit_bytes=VSMALL),
        cost_estimate=pl.CostEstimate(flops=0, bytes_accessed=8 * 10**6, transcendentals=0),
        name="row_slabs",
    )(x)


def pairs_kernel(pos, perm, x_ref, *rest):
    tb, s = rest[:8], rest[8]
    a = pos[0]
    for p in range(2):
        for d in range(W):
            x = x_ref[p, d]
            halves = [
                jnp.concatenate([x[:, 128 * (16 * h + c) : 128 * (16 * h + c) + 128] for c in range(16)], axis=0)
                for h in range(2)
            ]
            y = jnp.dot(perm[...], jnp.concatenate(halves, axis=1), preferred_element_type=F32).astype(BF)
            for n in range(NOB):
                part = y[16 * n : 16 * n + 16]
                for h in range(2):
                    s[n, d, p, 16 * h : 16 * h + 16] = part[:, 128 * h : 128 * h + 128]
    for k in range(8):
        t = dest_of(a, k)
        for i in range(2):
            tb[k][i] = s[2 * t + i]


def block_pairs(pos, perm, x):
    return pl.pallas_call(
        pairs_kernel,
        grid=(NPD // 2,),
        in_specs=[
            sspec(),
            pl.BlockSpec((256, 256), lambda i: (0, 0)),
            pl.BlockSpec((2, W, NOB, 4096), lambda i: (i, 0, 0, 0)),
        ],
        out_specs=[pl.BlockSpec((2, W, 2, 32, 128), lambda i: (0, 0, i, 0, 0))] * 8,
        out_shape=[jax.ShapeDtypeStruct((2, W, NPD, 32, 128), BF)] * 8,
        scratch_shapes=[pltpu.VMEM((NOB, W, 2, 32, 128), BF)],
        compiler_params=pltpu.CompilerParams(vmem_limit_bytes=VSMALL),
        cost_estimate=pl.CostEstimate(flops=10**9, bytes_accessed=8 * 10**6, transcendentals=0),
        name="block_pairs",
    )(pos, perm, x)


def greens_kernel(pos, size, meta, g_ref, rows_ref, cols_ref, v_ref, w_ref, o_ref):
    a = pos[0]
    row = lax.broadcasted_iota(jnp.int32, (BS, BS), 0)
    col = lax.broadcasted_iota(jnp.int32, (BS, BS), 1)

    def one(n, carry):
        for d in range(W):
            m = n + d - R
            ok = (m >= 0) & (m < NOB)
            if d != R:
                ok = ok & (meta[n * 128 + NG * W + d] > 0)
            rows_in = jnp.where(ok, size[jnp.clip(m, 0, NOB - 1)], 0)
            mask = (row < rows_in) & (col < size[n])
            occ = jnp.where(mask, g_ref[n, d], jnp.zeros((BS, BS), BF))
            v = jnp.where(mask, g_ref[n, W + d], jnp.zeros((BS, BS), BF))
            for g in range(2):
                t = jnp.dot(rows_ref[g], occ, preferred_element_type=F32).astype(BF)
                o_ref[n, d, 32 * g : 32 * g + 32] = jnp.dot(
                    t, cols_ref[g], preferred_element_type=F32
                ).astype(BF)
            v_ref[n, d] = jnp.concatenate([v, v], axis=1)
        return carry

    lax.fori_loop(0, NOB, one, 0)
    z = jnp.zeros((32, 64), BF)
    for i in range(2):
        for g in range(2):
            for e in range(W):
                cols = []
                for d in range(W):
                    f = e - d + 1
                    if f < 0 or f >= W:
                        cols.append(z)
                        continue
                    m = 2 * a + i + d - 1
                    ok = (m >= 0) & (m < NOB)
                    mc = jnp.clip(m, 0, NOB - 1)
                    v = o_ref[mc, f, 32 * g : 32 * g + 32]
                    cols.append(jnp.where(ok, v, z))
                row = (g * W + e) * 32
                w_ref[i, row : row + 32, :] = jnp.concatenate(cols, axis=1)


def greens(pos, size, meta, g, rows, cols):
    return pl.pallas_call(
        greens_kernel,
        in_specs=[sspec()] * 3 + [vspec()] * 3,
        out_specs=[vspec(), vspec()],
        scratch_shapes=[pltpu.VMEM((NOB, W, 64, 64), BF)],
        out_shape=[
            jax.ShapeDtypeStruct((NOB, W, BS, 128), BF),
            jax.ShapeDtypeStruct((2, 192, 192), BF),
        ],
        compiler_params=pltpu.CompilerParams(vmem_limit_bytes=VLIM),
        cost_estimate=pl.CostEstimate(flops=10**6, bytes_accessed=8 * 10**6, transcendentals=0),
        name="greens",
    )(pos, size, meta, g, rows, cols)


def second_kernel(steps, pos, pat, perm, ta_ref, v_ref, *rest):
    outs, s, kb = rest[:4], rest[4], rest[5]
    a = pos[0]
    low = lax.broadcasted_iota(jnp.int32, (BS, 128), 1) < 64
    zero = jnp.zeros((BS, 128), BF)
    kb[...] = jnp.zeros(kb.shape, BF)
    s[0] = jnp.zeros(s.shape[1:], BF)
    s[NOB + 1] = jnp.zeros(s.shape[1:], BF)

    def regroup(g, carry):
        for d in range(W):
            x = ta_ref[pl.ds(16 * g, 16), d].reshape(256, 256)
            y = jnp.dot(perm[...], x, preferred_element_type=F32).astype(BF)
            for n in range(NOB):
                keep = pat[n * 128 + g * W + d] > 0
                part = y[16 * n : 16 * n + 16]
                s[n + 1, d, pl.ds(pl.multiple_of(16 * g, 16), 16)] = jnp.where(
                    keep, part, jnp.zeros_like(part)
                )
        return carry

    lax.fori_loop(0, NG, regroup, 0)
    for j, k in enumerate(steps):
        t = dest_of(a, k)

        def one(i, carry, j=j, t=t):
            n = 2 * t + i
            for d in range(W):
                v = v_ref[n, d]
                lo, hi = jnp.where(low, v, zero), jnp.where(low, zero, v)
                for q in range(4):
                    row, col = 256 * d + 64 * q, 128 * (q // 2)
                    kb[row : row + 64, col : col + 128] = hi if q % 2 else lo
            for e in range(W):
                ds = [d for d in range(W) if 0 <= e - d + 1 < W]
                lhs = jnp.concatenate([s[n + d, e - d + 1] for d in ds], axis=1)
                rhs = kb[256 * ds[0] : 256 * ds[-1] + 256]
                outs[j][i * W + e] = jnp.dot(lhs, rhs, preferred_element_type=F32).astype(BF)
            return carry

        lax.fori_loop(0, 2, one, 0)


def second_products(steps, pos, pat, perm, ta, v):
    return pl.pallas_call(
        functools.partial(second_kernel, steps),
        in_specs=[sspec(), sspec(), vspec(), vspec(), vspec()],
        out_specs=[vspec()] * 4,
        out_shape=[jax.ShapeDtypeStruct((2 * W, 160, 256), BF)] * 4,
        scratch_shapes=[pltpu.VMEM((NOB + 2, W, 160, 256), BF), pltpu.VMEM((256 * W, 256), BF)],
        compiler_params=pltpu.CompilerParams(vmem_limit_bytes=VSMALL),
        cost_estimate=pl.CostEstimate(flops=2 * 10**9, bytes_accessed=15 * 10**6, transcendentals=0),
        name="second",
    )(pos, pat, perm, ta, v)


def first_kernel(pos, pat, perm, w_ref, *rest):
    tb, out, s = rest[:8], rest[8], rest[9]
    a, o = pos[0], pos[1]
    lane = lax.broadcasted_iota(jnp.int32, (96, NPD * 128), 1)
    low = lax.rem(lane, 128) < 64
    for k in range(8):
        src = src_of(a, k)
        base = lax.rem(src, 2) * 40 + (src // 2) * 10

        def one(i, carry, k=k, base=base):
            n = 2 * a + i
            columns = []
            for p in range(NPD):
                rows = []
                for d in range(W):
                    keep = pat[(k * NOB + n) * 32 + lax.div(o * NPD + p, ABS) * W + d] > 0
                    row = pl.multiple_of(((i * W + d) * NPD + p) * 32, 32)
                    x = tb[k][pl.ds(row, 32)]
                    x = jnp.where(keep, x, jnp.zeros_like(x))
                    rows.append(x)
                    rows.append(jnp.concatenate([x[:, 64:], x[:, :64]], axis=1))
                columns.append(jnp.concatenate(rows, axis=0))
            y = jnp.dot(w_ref[i], jnp.concatenate(columns, axis=1), preferred_element_type=F32)
            y = jnp.where(low, y[:96], y[96:]).astype(BF)
            for p in range(NPD):
                s[i, base + p] = y[:, 128 * p : 128 * p + 128]
            return carry

        lax.fori_loop(0, 2, one, 0)

    def regroup(j, carry):
        i = j // 5
        g = lax.rem(j, 5)
        tiles = s[i, pl.ds(16 * g, 16)]
        for e in range(W):
            x = jnp.concatenate(
                [tiles[:, 32 * e + 16 * h : 32 * e + 16 * h + 16].reshape(256, 128) for h in range(2)], axis=1
            )
            y = jnp.dot(perm[...], x, preferred_element_type=F32).astype(BF)
            for h in range(2):
                for q in range(16):
                    qq = 16 * h + q
                    out[qq // 2, i * W + e, pl.ds(pl.multiple_of(16 * g, 16), 16),
                        128 * (qq % 2) : 128 * (qq % 2) + 128] = y[16 * q : 16 * q + 16, 128 * h : 128 * h + 128]
        return carry

    lax.fori_loop(0, 10, regroup, 0)


def first_products(pos, pat, perm, w, tb):
    return pl.pallas_call(
        first_kernel,
        in_specs=[sspec(), sspec(), vspec(), vspec()] + [vspec()] * 8,
        out_specs=vspec(),
        out_shape=jax.ShapeDtypeStruct((16, 2 * W, 80, 256), BF),
        scratch_shapes=[pltpu.VMEM((2, 80, 96, 128), BF)],
        compiler_params=pltpu.CompilerParams(vmem_limit_bytes=VLIM),
        cost_estimate=pl.CostEstimate(flops=3 * 10**9, bytes_accessed=8 * 10**6, transcendentals=0),
        name="first",
    )(pos, pat, perm, w, *tb)


def chi_kernel(pos, first_ref, *rest):
    us, theirs, mine, rhs = rest[:8], rest[8], rest[9], rest[10]
    a = pos[0]
    core0 = lax.rem(a, 2) == 0
    t = pl.program_id(0)

    @pl.when(t == 0)
    def _():
        for k in range(8):
            row = pl.multiple_of(src_of(a, k) * 160, 32)
            for kk in range(6):
                rhs[pl.ds(row, 160), 256 * kk : 256 * kk + 256] = us[k][kk]

    lhs = jnp.concatenate([first_ref[:, kk].reshape(1280, 256) for kk in range(6)], axis=1)
    r = lax.dot_general(
        lhs,
        rhs[pl.ds(pl.multiple_of(256 * t, 256), 256)],
        (((1,), (1,)), ((), ())),
        preferred_element_type=F32,
    )
    for b in range(16):
        lo, hi = r[80 * b : 80 * b + 40], r[80 * b + 40 : 80 * b + 80]
        mine[b] = jnp.where(core0, lo, hi)
        theirs[b] = jnp.where(core0, hi, lo).astype(BF)


def chi_share(pos, first, us):
    return pl.pallas_call(
        chi_kernel,
        grid=(5,),
        in_specs=[sspec(), vspec()] + [vspec()] * 8,
        out_specs=[pl.BlockSpec((16, 40, 256), lambda t: (0, 0, t))] * 2,
        out_shape=[jax.ShapeDtypeStruct((16, 40, 1280), BF), jax.ShapeDtypeStruct((16, 40, 1280), F32)],
        scratch_shapes=[pltpu.VMEM((1280, 1536), BF)],
        compiler_params=pltpu.CompilerParams(vmem_limit_bytes=VSMALL),
        cost_estimate=pl.CostEstimate(flops=5 * 10**9, bytes_accessed=13 * 10**6, transcendentals=0),
        name="chi",
    )(pos, first, *us)


def deinterleave():
    rows = np.zeros((2, 32, 64), np.float32)
    cols = np.zeros((2, 64, 64), np.float32)
    for g in range(2):
        for q in range(32):
            rows[g, q, 2 * q + g] = 1.0
        for j in range(2):
            for c in range(32):
                cols[g, 2 * c + (g ^ j), 32 * j + c] = 1.0
    return jnp.asarray(rows, BF), jnp.asarray(cols, BF)


def body(three_center, atom_size, tensor_pattern, green_occ, green_virt, green_pattern):
    a, o = lax.axis_index("aux"), lax.axis_index("orb")
    pos = jnp.stack([a, o]).astype(jnp.int32)
    perm = swap16()
    rows, cols = deinterleave()
    x = three_center.transpose(0, 2, 1, 3)

    marks = jnp.concatenate([tensor_pattern.reshape(1, NG * W), green_pattern], axis=1).astype(BF)
    marks = jnp.pad(marks, ((0, 1), (0, 4096 - NG * W - W)))
    own = jnp.concatenate([green_occ[0], green_virt[0], marks], axis=0)
    every = jnp.broadcast_to(own[None], (NOB,) + own.shape)
    every = lax.all_to_all(every, "orb", split_axis=0, concat_axis=0, tiled=True)

    *tb, x = lax.optimization_barrier((*block_pairs(pos, perm, x), x))
    tb = [t.reshape(TROWS, 128) for t in tb]
    for k in (1, 2, 6):
        tb[k] = lax.ppermute(tb[k], "aux", pairs_of(k))
    marks, ta = lax.optimization_barrier((every[:, 2 * W, :128], row_slabs(x)))
    both = jnp.concatenate([marks, lax.ppermute(marks, "aux", pairs_of(1))], axis=0)
    both, tb[1], tb[2], tb[6], ta = lax.optimization_barrier((both, tb[1], tb[2], tb[6], ta))
    ta = lax.all_to_all(ta, "orb", split_axis=0, concat_axis=0, tiled=True)
    for k in CARRIERS:
        tb[k] = jnp.concatenate([tb[k], both], axis=0)
    for k in (3, 4, 5, 7):
        tb[k] = lax.ppermute(tb[k], "aux", pairs_of(k))
    back, far, ahead = [tb[k][TROWS:, :32] for k in CARRIERS]
    pat = jnp.concatenate([both[:, :32], back[16:], back[:16], far, ahead[16:], ahead[:16]], axis=0)
    pat = pat.astype(jnp.int32).reshape(-1)
    meta = marks.astype(jnp.int32).reshape(-1)
    blocks = every[:, : 2 * W].reshape(NOB, 2 * W, BS, BS)
    v, w = greens(pos, atom_size, meta, blocks, rows, cols)

    first = first_products(pos, pat, perm, w, tb)
    first = lax.all_to_all(first, "orb", split_axis=0, concat_axis=0, tiled=True)
    us = [None] * 8
    ta = ta.reshape(160, W, NOB, 256)
    late = (4, 5, 1)
    for k, u in zip((2, 6, 3, 7), second_products((2, 6, 3, 7), pos, meta, perm, ta, v)):
        us[k] = lax.ppermute(u, "aux", pairs_of(k))
    *parts, us[0] = second_products(late + (0,), pos, meta, perm, ta, v)
    *parts, us[2], us[6] = lax.optimization_barrier((*parts, us[2], us[6]))
    for k, u in zip(late, parts):
        us[k] = lax.ppermute(u, "aux", pairs_of(k))

    theirs, mine = chi_share(pos, first, us)
    part = (mine + lax.ppermute(theirs, "aux", pairs_of(1)).astype(F32)).astype(BF)
    part = lax.all_to_all(part, "orb", split_axis=0, concat_axis=0, tiled=True)
    part = jnp.sum(part.astype(F32), axis=0).reshape(4, NPD, 1280)
    x = a // 2
    total = lax.dynamic_index_in_dim(part, x, 0, keepdims=False)
    for dx in range(1, 4):
        piece = lax.dynamic_index_in_dim(part, lax.rem(x + dx, 4), 0, keepdims=False)
        total = total + lax.ppermute(piece, "aux", pairs_of(2 * dx))
    return total


def solution(mesh):
    return jax.shard_map(
        body,
        mesh=mesh,
        in_specs=(
            P(("aux", "orb"), None, None, None),
            P(),
            P("aux", "orb", None),
            P("orb", None, None),
            P("orb", None, None),
            P("orb", None),
        ),
        out_specs=P(("aux", "orb"), None),
        check_vma=False,
    )
```

```python
import functools

import jax
import jax.numpy as jnp
import numpy as np
from jax import lax
from jax.experimental import pallas as pl
from jax.experimental.pallas import tpu as pltpu
from jax.sharding import PartitionSpec as P

BS = 64
R = 1
W = 3
ABS = 16
NOB = 16
NPD = 10
NG = 10
BF = jnp.bfloat16
F32 = jnp.float32
VLIM = 56 * 1024 * 1024
VSMALL = 24 * 1024 * 1024

STEPS = [(k // 2, k % 2) for k in range(8)]


TROWS = 2 * W * NPD * 32
CARRIERS = (3, 4, 7)


def pairs_of(k):
    dx, dc = STEPS[k]
    return [(i, ((i // 2 + dx) % 4) * 2 + ((i % 2) ^ dc)) for i in range(8)]


def dest_of(a, k):
    dx, dc = STEPS[k]
    return lax.rem(a // 2 + dx, 4) * 2 + (lax.rem(a, 2) if dc == 0 else 1 - lax.rem(a, 2))


def src_of(a, k):
    dx, dc = STEPS[k]
    return lax.rem(a // 2 + 4 - dx, 4) * 2 + (lax.rem(a, 2) if dc == 0 else 1 - lax.rem(a, 2))


def swap16():
    r = np.arange(256)
    m = np.zeros((256, 256), np.float32)
    m[r, (r % 16) * 16 + r // 16] = 1.0
    return jnp.asarray(m, BF)


def vspec():
    return pl.BlockSpec(memory_space=pltpu.VMEM)


def sspec():
    return pl.BlockSpec(memory_space=pltpu.SMEM)


def rows_kernel(x_ref, ta_ref):
    for p in range(2):
        for d in range(W):
            for o in range(16):
                ta_ref[o, p * W + d] = x_ref[p, d, :, 256 * o : 256 * o + 256]


def row_slabs(x):
    return pl.pallas_call(
        rows_kernel,
        grid=(NPD // 2,),
        in_specs=[pl.BlockSpec((2, W, NOB, 4096), lambda i: (i, 0, 0, 0))],
        out_specs=pl.BlockSpec((16, 2 * W, NOB, 256), lambda i: (0, i, 0, 0)),
        out_shape=jax.ShapeDtypeStruct((16, NPD * W, NOB, 256), BF),
        compiler_params=pltpu.CompilerParams(vmem_limit_bytes=VSMALL),
        cost_estimate=pl.CostEstimate(flops=0, bytes_accessed=8 * 10**6, transcendentals=0),
        name="row_slabs",
    )(x)


def pairs_kernel(pos, perm, x_ref, *rest):
    tb, s = rest[:8], rest[8]
    a = pos[0]
    for p in range(2):
        for d in range(W):
            x = x_ref[p, d]
            halves = [
                jnp.concatenate([x[:, 128 * (16 * h + c) : 128 * (16 * h + c) + 128] for c in range(16)], axis=0)
                for h in range(2)
            ]
            y = jnp.dot(perm[...], jnp.concatenate(halves, axis=1), preferred_element_type=F32).astype(BF)
            for n in range(NOB):
                part = y[16 * n : 16 * n + 16]
                for h in range(2):
                    s[n, d, p, 16 * h : 16 * h + 16] = part[:, 128 * h : 128 * h + 128]
    for k in range(8):
        t = dest_of(a, k)
        for i in range(2):
            tb[k][i] = s[2 * t + i]


def block_pairs(pos, perm, x):
    return pl.pallas_call(
        pairs_kernel,
        grid=(NPD // 2,),
        in_specs=[
            sspec(),
            pl.BlockSpec((256, 256), lambda i: (0, 0)),
            pl.BlockSpec((2, W, NOB, 4096), lambda i: (i, 0, 0, 0)),
        ],
        out_specs=[pl.BlockSpec((2, W, 2, 32, 128), lambda i: (0, 0, i, 0, 0))] * 8,
        out_shape=[jax.ShapeDtypeStruct((2, W, NPD, 32, 128), BF)] * 8,
        scratch_shapes=[pltpu.VMEM((NOB, W, 2, 32, 128), BF)],
        compiler_params=pltpu.CompilerParams(vmem_limit_bytes=VSMALL),
        cost_estimate=pl.CostEstimate(flops=10**9, bytes_accessed=8 * 10**6, transcendentals=0),
        name="block_pairs",
    )(pos, perm, x)


def pack_kernel(tpat, gpat, occ_ref, virt_ref, out):
    lane = lax.broadcasted_iota(jnp.int32, (1, 128), 1)
    row = jnp.zeros((1, 128), jnp.int32)
    for d in range(W):
        for g in range(NG):
            row = jnp.where(lane == g * W + d, tpat[d, 0, g], row)
        row = jnp.where(lane == NG * W + d, gpat[0, d], row)
    tail = jnp.concatenate([row, jnp.zeros((1, 128), jnp.int32)], axis=0).astype(F32).astype(BF)
    rest = jnp.zeros((2, 4096 - 128), BF)
    own = jnp.concatenate([occ_ref[0], virt_ref[0], jnp.concatenate([tail, rest], axis=1)], axis=0)
    for o in range(NOB):
        out[o] = own


def pack(tpat, gpat, occ, virt):
    return pl.pallas_call(
        pack_kernel,
        in_specs=[sspec(), sspec(), vspec(), vspec()],
        out_specs=vspec(),
        out_shape=jax.ShapeDtypeStruct((NOB, 8, 4096), BF),
        compiler_params=pltpu.CompilerParams(vmem_limit_bytes=VLIM),
        cost_estimate=pl.CostEstimate(flops=0, bytes_accessed=11 * 10**5, transcendentals=0),
        name="pack",
    )(tpat, gpat, occ, virt)


def greens_kernel(pos, size, meta, g_ref, rows_ref, cols_ref, v_ref, w_ref, o_ref):
    a = pos[0]
    row = lax.broadcasted_iota(jnp.int32, (BS, BS), 0)
    col = lax.broadcasted_iota(jnp.int32, (BS, BS), 1)

    def one(n, carry):
        for d in range(W):
            m = n + d - R
            ok = (m >= 0) & (m < NOB)
            if d != R:
                ok = ok & (meta[n * 128 + NG * W + d] > 0)
            rows_in = jnp.where(ok, size[jnp.clip(m, 0, NOB - 1)], 0)
            mask = (row < rows_in) & (col < size[n])
            occ = jnp.where(mask, g_ref[n, d], jnp.zeros((BS, BS), BF))
            v = jnp.where(mask, g_ref[n, W + d], jnp.zeros((BS, BS), BF))
            for g in range(2):
                t = jnp.dot(rows_ref[g], occ, preferred_element_type=F32).astype(BF)
                o_ref[n, d, 32 * g : 32 * g + 32] = jnp.dot(
                    t, cols_ref[g], preferred_element_type=F32
                ).astype(BF)
            v_ref[n, d] = jnp.concatenate([v, v], axis=1)
        return carry

    lax.fori_loop(0, NOB, one, 0)
    z = jnp.zeros((32, 64), BF)
    for i in range(2):
        for g in range(2):
            for e in range(W):
                cols = []
                for d in range(W):
                    f = e - d + 1
                    if f < 0 or f >= W:
                        cols.append(z)
                        continue
                    m = 2 * a + i + d - 1
                    ok = (m >= 0) & (m < NOB)
                    mc = jnp.clip(m, 0, NOB - 1)
                    v = o_ref[mc, f, 32 * g : 32 * g + 32]
                    cols.append(jnp.where(ok, v, z))
                row = (g * W + e) * 32
                w_ref[i, row : row + 32, :] = jnp.concatenate(cols, axis=1)


def greens(pos, size, meta, g, rows, cols):
    return pl.pallas_call(
        greens_kernel,
        in_specs=[sspec()] * 3 + [vspec()] * 3,
        out_specs=[vspec(), vspec()],
        scratch_shapes=[pltpu.VMEM((NOB, W, 64, 64), BF)],
        out_shape=[
            jax.ShapeDtypeStruct((NOB, W, BS, 128), BF),
            jax.ShapeDtypeStruct((2, 192, 192), BF),
        ],
        compiler_params=pltpu.CompilerParams(vmem_limit_bytes=VLIM),
        cost_estimate=pl.CostEstimate(flops=10**6, bytes_accessed=8 * 10**6, transcendentals=0),
        name="greens",
    )(pos, size, meta, g, rows, cols)


def second_kernel(steps, pos, pat, perm, ta_ref, v_ref, *rest):
    outs, s, kb = rest[:4], rest[4], rest[5]
    a = pos[0]
    low = lax.broadcasted_iota(jnp.int32, (BS, 128), 1) < 64
    zero = jnp.zeros((BS, 128), BF)
    kb[...] = jnp.zeros(kb.shape, BF)
    s[0] = jnp.zeros(s.shape[1:], BF)
    s[NOB + 1] = jnp.zeros(s.shape[1:], BF)

    def regroup(g, carry):
        for d in range(W):
            x = ta_ref[pl.ds(16 * g, 16), d].reshape(256, 256)
            y = jnp.dot(perm[...], x, preferred_element_type=F32).astype(BF)
            for n in range(NOB):
                keep = pat[n * 128 + g * W + d] > 0
                part = y[16 * n : 16 * n + 16]
                s[n + 1, d, pl.ds(pl.multiple_of(16 * g, 16), 16)] = jnp.where(
                    keep, part, jnp.zeros_like(part)
                )
        return carry

    lax.fori_loop(0, NG, regroup, 0)
    for j, k in enumerate(steps):
        t = dest_of(a, k)

        def one(i, carry, j=j, t=t):
            n = 2 * t + i
            for d in range(W):
                v = v_ref[n, d]
                lo, hi = jnp.where(low, v, zero), jnp.where(low, zero, v)
                for q in range(4):
                    row, col = 256 * d + 64 * q, 128 * (q // 2)
                    kb[row : row + 64, col : col + 128] = hi if q % 2 else lo
            for e in range(W):
                ds = [d for d in range(W) if 0 <= e - d + 1 < W]
                lhs = jnp.concatenate([s[n + d, e - d + 1] for d in ds], axis=1)
                rhs = kb[256 * ds[0] : 256 * ds[-1] + 256]
                outs[j][i * W + e] = jnp.dot(lhs, rhs, preferred_element_type=F32).astype(BF)
            return carry

        lax.fori_loop(0, 2, one, 0)


def second_products(steps, pos, pat, perm, ta, v):
    return pl.pallas_call(
        functools.partial(second_kernel, steps),
        in_specs=[sspec(), sspec(), vspec(), vspec(), vspec()],
        out_specs=[vspec()] * 4,
        out_shape=[jax.ShapeDtypeStruct((2 * W, 160, 256), BF)] * 4,
        scratch_shapes=[pltpu.VMEM((NOB + 2, W, 160, 256), BF), pltpu.VMEM((256 * W, 256), BF)],
        compiler_params=pltpu.CompilerParams(vmem_limit_bytes=VSMALL),
        cost_estimate=pl.CostEstimate(flops=2 * 10**9, bytes_accessed=15 * 10**6, transcendentals=0),
        name="second",
    )(pos, pat, perm, ta, v)


def first_kernel(pos, pat, perm, w_ref, *rest):
    tb, out, s = rest[:8], rest[8], rest[9]
    a, o = pos[0], pos[1]
    lane = lax.broadcasted_iota(jnp.int32, (96, NPD * 128), 1)
    low = lax.rem(lane, 128) < 64
    for k in range(8):
        src = src_of(a, k)
        base = lax.rem(src, 2) * 40 + (src // 2) * 10

        def one(i, carry, k=k, base=base):
            n = 2 * a + i
            columns = []
            for p in range(NPD):
                rows = []
                for d in range(W):
                    keep = pat[(k * NOB + n) * 32 + lax.div(o * NPD + p, ABS) * W + d] > 0
                    row = pl.multiple_of(((i * W + d) * NPD + p) * 32, 32)
                    x = tb[k][pl.ds(row, 32)]
                    x = jnp.where(keep, x, jnp.zeros_like(x))
                    rows.append(x)
                    rows.append(jnp.concatenate([x[:, 64:], x[:, :64]], axis=1))
                columns.append(jnp.concatenate(rows, axis=0))
            y = jnp.dot(w_ref[i], jnp.concatenate(columns, axis=1), preferred_element_type=F32)
            y = jnp.where(low, y[:96], y[96:]).astype(BF)
            for p in range(NPD):
                s[i, base + p] = y[:, 128 * p : 128 * p + 128]
            return carry

        lax.fori_loop(0, 2, one, 0)

    def regroup(j, carry):
        i = j // 5
        g = lax.rem(j, 5)
        tiles = s[i, pl.ds(16 * g, 16)]
        for e in range(W):
            x = jnp.concatenate(
                [tiles[:, 32 * e + 16 * h : 32 * e + 16 * h + 16].reshape(256, 128) for h in range(2)], axis=1
            )
            y = jnp.dot(perm[...], x, preferred_element_type=F32).astype(BF)
            for h in range(2):
                for q in range(16):
                    qq = 16 * h + q
                    out[qq // 2, i * W + e, pl.ds(pl.multiple_of(16 * g, 16), 16),
                        128 * (qq % 2) : 128 * (qq % 2) + 128] = y[16 * q : 16 * q + 16, 128 * h : 128 * h + 128]
        return carry

    lax.fori_loop(0, 10, regroup, 0)


def first_products(pos, pat, perm, w, tb):
    return pl.pallas_call(
        first_kernel,
        in_specs=[sspec(), sspec(), vspec(), vspec()] + [vspec()] * 8,
        out_specs=vspec(),
        out_shape=jax.ShapeDtypeStruct((16, 2 * W, 80, 256), BF),
        scratch_shapes=[pltpu.VMEM((2, 80, 96, 128), BF)],
        compiler_params=pltpu.CompilerParams(vmem_limit_bytes=VLIM),
        cost_estimate=pl.CostEstimate(flops=3 * 10**9, bytes_accessed=8 * 10**6, transcendentals=0),
        name="first",
    )(pos, pat, perm, w, *tb)


def chi_kernel(pos, first_ref, *rest):
    us, theirs, mine, rhs = rest[:8], rest[8], rest[9], rest[10]
    a = pos[0]
    core0 = lax.rem(a, 2) == 0
    t = pl.program_id(0)

    @pl.when(t == 0)
    def _():
        for k in range(8):
            row = pl.multiple_of(src_of(a, k) * 160, 32)
            for kk in range(6):
                rhs[pl.ds(row, 160), 256 * kk : 256 * kk + 256] = us[k][kk]

    lhs = jnp.concatenate([first_ref[:, kk].reshape(1280, 256) for kk in range(6)], axis=1)
    r = lax.dot_general(
        lhs,
        rhs[pl.ds(pl.multiple_of(256 * t, 256), 256)],
        (((1,), (1,)), ((), ())),
        preferred_element_type=F32,
    )
    for b in range(16):
        lo, hi = r[80 * b : 80 * b + 40], r[80 * b + 40 : 80 * b + 80]
        mine[b] = jnp.where(core0, lo, hi)
        theirs[b] = jnp.where(core0, hi, lo).astype(BF)


def chi_share(pos, first, us):
    return pl.pallas_call(
        chi_kernel,
        grid=(5,),
        in_specs=[sspec(), vspec()] + [vspec()] * 8,
        out_specs=[pl.BlockSpec((16, 40, 256), lambda t: (0, 0, t))] * 2,
        out_shape=[jax.ShapeDtypeStruct((16, 40, 1280), BF), jax.ShapeDtypeStruct((16, 40, 1280), F32)],
        scratch_shapes=[pltpu.VMEM((1280, 1536), BF)],
        compiler_params=pltpu.CompilerParams(vmem_limit_bytes=VSMALL),
        cost_estimate=pl.CostEstimate(flops=5 * 10**9, bytes_accessed=13 * 10**6, transcendentals=0),
        name="chi",
    )(pos, first, *us)


def deinterleave():
    rows = np.zeros((2, 32, 64), np.float32)
    cols = np.zeros((2, 64, 64), np.float32)
    for g in range(2):
        for q in range(32):
            rows[g, q, 2 * q + g] = 1.0
        for j in range(2):
            for c in range(32):
                cols[g, 2 * c + (g ^ j), 32 * j + c] = 1.0
    return jnp.asarray(rows, BF), jnp.asarray(cols, BF)


def body(three_center, atom_size, tensor_pattern, green_occ, green_virt, green_pattern):
    a, o = lax.axis_index("aux"), lax.axis_index("orb")
    pos = jnp.stack([a, o]).astype(jnp.int32)
    perm = swap16()
    rows, cols = deinterleave()
    x = three_center.transpose(0, 2, 1, 3)

    every = pack(tensor_pattern.transpose(2, 1, 0), green_pattern, green_occ, green_virt)
    every = lax.all_to_all(every, "orb", split_axis=0, concat_axis=0, tiled=True)

    *tb, x = lax.optimization_barrier((*block_pairs(pos, perm, x), x))
    tb = [t.reshape(TROWS, 128) for t in tb]
    for k in (1, 2, 6):
        tb[k] = lax.ppermute(tb[k], "aux", pairs_of(k))
    marks, ta = lax.optimization_barrier((every[:, 2 * W, :128], row_slabs(x)))
    both = jnp.concatenate([marks, lax.ppermute(marks, "aux", pairs_of(1))], axis=0)
    both, tb[1], tb[2], tb[6], ta = lax.optimization_barrier((both, tb[1], tb[2], tb[6], ta))
    ta = lax.all_to_all(ta, "orb", split_axis=0, concat_axis=0, tiled=True)
    for k in CARRIERS:
        tb[k] = jnp.concatenate([tb[k], both], axis=0)
    for k in (3, 4, 5, 7):
        tb[k] = lax.ppermute(tb[k], "aux", pairs_of(k))
    back, far, ahead = [tb[k][TROWS:, :32] for k in CARRIERS]
    pat = jnp.concatenate([both[:, :32], back[16:], back[:16], far, ahead[16:], ahead[:16]], axis=0)
    pat = pat.astype(jnp.int32).reshape(-1)
    meta = marks.astype(jnp.int32).reshape(-1)
    blocks = every[:, : 2 * W].reshape(NOB, 2 * W, BS, BS)
    v, w = greens(pos, atom_size, meta, blocks, rows, cols)

    first = first_products(pos, pat, perm, w, tb)
    first = lax.all_to_all(first, "orb", split_axis=0, concat_axis=0, tiled=True)
    us = [None] * 8
    ta = ta.reshape(160, W, NOB, 256)
    late = (4, 5, 1)
    for k, u in zip((2, 6, 3, 7), second_products((2, 6, 3, 7), pos, meta, perm, ta, v)):
        us[k] = lax.ppermute(u, "aux", pairs_of(k))
    *parts, us[0] = second_products(late + (0,), pos, meta, perm, ta, v)
    *parts, us[2], us[6] = lax.optimization_barrier((*parts, us[2], us[6]))
    for k, u in zip(late, parts):
        us[k] = lax.ppermute(u, "aux", pairs_of(k))

    theirs, mine = chi_share(pos, first, us)
    part = (mine + lax.ppermute(theirs, "aux", pairs_of(1)).astype(F32)).astype(BF)
    part = lax.all_to_all(part, "orb", split_axis=0, concat_axis=0, tiled=True)
    part = jnp.sum(part.astype(F32), axis=0).reshape(4, NPD, 1280)
    x = a // 2
    total = lax.dynamic_index_in_dim(part, x, 0, keepdims=False)
    for dx in range(1, 4):
        piece = lax.dynamic_index_in_dim(part, lax.rem(x + dx, 4), 0, keepdims=False)
        total = total + lax.ppermute(piece, "aux", pairs_of(2 * dx))
    return total


def solution(mesh):
    return jax.shard_map(
        body,
        mesh=mesh,
        in_specs=(
            P(("aux", "orb"), None, None, None),
            P(),
            P("aux", "orb", None),
            P("orb", None, None),
            P("orb", None, None),
            P("orb", None),
        ),
        out_specs=P(("aux", "orb"), None),
        check_vma=False,
    )
```
